32 devices in a mesh: ctx: 16 (over z, y, core), fsdp: 2 (over x).
Axes of the slice: x: 2, y: 2, z: 4, core: 2. Of those that a mesh axis runs over, the one named last changes fastest.
Arguments:
- tokens: bfloat16 [2, 2048, 2048], P('fsdp', 'ctx'), may hold values from -6 to 6
- cotangent: float32 [2, 2048, 2048], P('fsdp', 'ctx'), may hold values from -6 to 6
- lengths: int32 [2, 4], P('fsdp'), may hold values from 1 to 1024, 2048 in all within a row
- token_order: int32 [2, 2048], P('fsdp'), may hold values from 0 to 2047, as said below
- routes: int32 [2, 2048, 6], P('fsdp', 'ctx'), may hold values from 0 to 15, all different within a row; in each aligned block of 128 rows (0 to 127, 128 to 255, ..., all dimensions but the last counted through in order) at most 64 rows name the same one
- first_gain: float32 [2048], P(('ctx', 'fsdp')), may hold values from 0.1 to 1.9
- latent_gain: float32 [512], P(('ctx', 'fsdp')), may hold values from 0.1 to 1.9
- query_weight: float32 [2048, 3072], P(('ctx', 'fsdp')), may hold values from -0.125 to 0.125
- compress_weight: float32 [2048, 576], P(('ctx', 'fsdp')), may hold values from -0.125 to 0.125
- expand_weight: float32 [512, 4096], P(('ctx', 'fsdp')), may hold values from -0.25 to 0.25
- output_weight: float32 [2048, 2048], P(('ctx', 'fsdp')), may hold values from -0.75 to 0.75
- second_gain: float32 [2048], P(('ctx', 'fsdp')), may hold values from 0.1 to 1.9
- router_weight: float32 [2048, 16], P(('ctx', 'fsdp')), may hold values from -0.0625 to 0.0625
- shared_gate: float32 [2048, 2816], P(('ctx', 'fsdp')), may hold values from -0.125 to 0.125
- shared_up: float32 [2048, 2816], P(('ctx', 'fsdp')), may hold values from -0.125 to 0.125
- shared_down: float32 [2048, 2816], P(('ctx', 'fsdp')), may hold values from -0.109375 to 0.109375
- expert_gate: float32 [16, 2048, 1408], P('ctx', 'fsdp'), may hold values from -0.125 to 0.125
- expert_up: float32 [16, 2048, 1408], P('ctx', 'fsdp'), may hold values from -0.125 to 0.125
- expert_down: float32 [16, 2048, 1408], P('ctx', 'fsdp'), may hold values from -1.25 to 1.25
Outputs:
- output: float32 [2, 2048, 2048], P('fsdp', 'ctx')
- grad_tokens: float32 [2, 2048, 2048], P('fsdp', 'ctx')
- grad_first_gain: float32 [2048], P(('ctx', 'fsdp'))
- grad_latent_gain: float32 [512], P(('ctx', 'fsdp'))
- grad_query_weight: float32 [2048, 3072], P(('ctx', 'fsdp'))
- grad_compress_weight: float32 [2048, 576], P(('ctx', 'fsdp'))
- grad_expand_weight: float32 [512, 4096], P(('ctx', 'fsdp'))
- grad_output_weight: float32 [2048, 2048], P(('ctx', 'fsdp'))
- grad_second_gain: float32 [2048], P(('ctx', 'fsdp'))
- grad_router_weight: float32 [2048, 16], P(('ctx', 'fsdp'))
- grad_shared_gate: float32 [2048, 2816], P(('ctx', 'fsdp'))
- grad_shared_up: float32 [2048, 2816], P(('ctx', 'fsdp'))
- grad_shared_down: float32 [2048, 2816], P(('ctx', 'fsdp'))
- grad_expert_gate: float32 [16, 2048, 1408], P('ctx', 'fsdp')
- grad_expert_up: float32 [16, 2048, 1408], P('ctx', 'fsdp')
- grad_expert_down: float32 [16, 2048, 1408], P('ctx', 'fsdp')
The draws below stay inside these ranges and needn't reach their ends.
Inputs may be any that keep to these rules, and one draw needn't show every extreme that they name: `token_order`: each row holds every number below 2048 exactly once. The lengths of a row add up to 2048; the largest is exactly 1024. `routes`: each token names 6 different experts; among the 128 tokens of one device no expert is named more than 64 times, and in every draw some device names some expert exactly 64 times.
All inputs are finite; a program needn't handle non-finite values.
Results may differ from the reference program's by a relative error of at most 0.035.
Values may be sent and summed in bfloat16 or wider, within the bound.
A program may use at most 448 MiB of HBM per device.

```python
import math
import jax
import jax.numpy as jnp
import numpy as np
from jax import lax

D = 2048
HEADS = 16
NOPE = 128
ROPE = 64
VDIM = 128
LATENT = 512
FF = 1408
TOP = 6
TOK_DEV = 128
SFF = 2816
EXPERTS = 16
GROUP = 2048
LONGEST = 1024
SEQS = 4
CAP = 64
N_CTX = 16
N_FSDP = 2


def shuffled(key, count):
    return jax.random.permutation(key, count).astype(jnp.int32)


def deal_group(group_key):
    round_key, slot_key = jax.random.split(group_key)
    rounds = jax.vmap(shuffled, in_axes=(0, None))(jax.random.split(round_key, TOK_DEV), N_CTX)
    slots = jax.vmap(shuffled, in_axes=(0, None))(jax.random.split(slot_key, N_CTX), TOK_DEV)
    device = jnp.arange(N_CTX, dtype=jnp.int32)[:, None]
    return (slots * N_CTX + rounds[slots, device]).reshape(-1).astype(jnp.int32)


def draw_token_order(key, part):
    key = jax.random.fold_in(key, 11)
    return jax.vmap(deal_group)(jax.random.split(key, N_FSDP))


def levels(key, dims, cuts, least, largest):
    loudness, own = 1.0, jax.random.fold_in(key, 6)
    for dim, parts in cuts:
        draws = jnp.exp(jax.random.uniform(jax.random.fold_in(own, dim), (parts,), jnp.float32, least / len(cuts), largest / len(cuts)))
        loudness = loudness * jnp.repeat(draws, dims[dim] // parts).reshape([-1 if axis == dim else 1 for axis in range(len(dims))])
    return loudness


def split_up(count, total, bound, skew):
    portions = [(1 << 20) // math.isqrt(standing ** skew) + 1 for standing in range(2, count + 1)]
    surplus, given = total - bound - (count - 1), [1] * (count - 1)
    while surplus > 0:
        free = [i for i in range(count - 1) if given[i] < bound]
        whole, left = sum([portions[i] for i in free]), surplus
        for i in free:
            addition = min(bound - given[i], max(1, left * portions[i] // whole), surplus)
            given[i] = given[i] + addition
            surplus = surplus - addition
    return np.array([bound] + given)


def ragged_sizes(own_key, count, total, reach, slope):
    if count == 2:
        one = jax.random.randint(own_key, (), max(1, total - reach), min(reach, total - 1) + 1)
        return jnp.stack([one, total - one])
    sizes = jnp.asarray(split_up(count, total, reach, slope), jnp.int32)
    couples = (count - 1) // 2
    giver, receiver = sizes[1:1 + 2 * couples:2], sizes[2:2 + 2 * couples:2]
    margin = jnp.minimum(giver - 1, reach - receiver)
    passed = jax.random.randint(jax.random.fold_in(own_key, 1), (couples,), 0, 1 << 20) % (margin + 1)
    sizes = sizes.at[1:1 + 2 * couples:2].set(giver - passed).at[2:2 + 2 * couples:2].set(receiver + passed)
    return sizes[jax.random.permutation(jax.random.fold_in(own_key, 2), count)]


def deal_out(key, own, number, rows, number_of, top, reach, lean):
    order = jax.random.permutation(key, number_of)
    heavy_load, common = load_shares(number_of, rows * top, reach, lean, True), load_shares(number_of, rows * top, reach, lean, False)
    places = jnp.arange(number_of)

    def named(tallies, turn):
        used = int((tallies > 0).sum())
        fixed = max(1, used // 4)
        moved = fixed + (places - fixed + turn * (used - fixed)) % max(1, number_of - fixed)
        return jnp.zeros((number_of,), jnp.int32).at[order[jnp.where(places < fixed, places, moved)]].set(jnp.asarray(tallies, jnp.int32))

    tallies = jnp.where(number % 4 == 0, named(heavy_load, number // 4), named(common, number - number // 4 - 1))
    mixed = jax.random.permutation(jax.random.fold_in(own, 3), number_of)
    giver, taker = mixed[0:number_of // 2 * 2:2], mixed[1:number_of // 2 * 2:2]
    slack = jnp.minimum(tallies[giver] - 1, reach - tallies[taker]) // 2
    slack = jnp.where((giver == order[0]) | (taker == order[0]) | (tallies[taker] == 0), 0, jnp.maximum(slack, 0))
    moved = jax.random.randint(jax.random.fold_in(own, 4), (number_of // 2,), 0, 1 << 20) % (slack + 1)
    tallies = tallies.at[giver].add(-moved).at[taker].add(moved)
    labels = jnp.searchsorted(jnp.cumsum(tallies), jnp.arange(rows * top), side="right").astype(jnp.int32)
    table = labels.reshape(top, rows).T
    table = table[jax.random.permutation(jax.random.fold_in(own, 1), rows)]
    turn = jax.random.randint(jax.random.fold_in(own, 2), (rows, 1), 0, top)
    return jnp.take_along_axis(table, (jnp.arange(top)[None, :] + turn) % top, axis=1)


def load_shares(amount, total, limit, slope, full):
    portions = [(1 << 20) // math.isqrt(rank ** slope) + 1 for rank in range(1, amount + 1)]
    largest = limit if full else min(limit, max(-(-total // amount), total * portions[0] // sum(portions)))
    least = 1 if total - largest >= amount - 1 else 0
    given, surplus = [largest] + [least] * (amount - 1), total - largest - least * (amount - 1)
    while surplus > 0:
        free = [i for i in range(1, amount) if given[i] < largest] or [i for i in range(1, amount) if given[i] < limit]
        mass, budget = sum([portions[i] for i in free]), surplus
        for i in free:
            addition = min(limit - given[i], max(1, budget * portions[i] // mass), surplus)
            given[i] = given[i] + addition
            surplus = surplus - addition
    return np.array(given)


def gaussian(own_key, dims, spread, bound, cuts=(), kind=jnp.bfloat16):
    loudness = levels(own_key, dims, cuts, -0.22, 0.18) if cuts else 1.0
    result = jax.random.normal(own_key, dims, jnp.float32) * spread * loudness
    return jnp.minimum(jnp.maximum(result, -bound), bound).astype(kind)


def setup_inputs(seed: int = 0) -> dict:
    seeds = jax.random.split(jax.random.key(seed), 20)
    tokens = gaussian(seeds[0], (N_FSDP, GROUP, D), 1.0, 6.0, ((0, 2), (1, 16)))
    cotangent = gaussian(seeds[1], (N_FSDP, GROUP, D), 1.0, 6.0, ((0, 2), (1, 16)), jnp.float32)
    lengths = jax.vmap(lambda own: ragged_sizes(own, SEQS, GROUP, LONGEST, 2))(jax.random.split(seeds[2], N_FSDP)).reshape((N_FSDP, SEQS)).astype(jnp.int32)
    token_order = draw_token_order(jax.random.fold_in(seeds[19], 71), 0)
    routes_keys = jax.random.split(jax.random.fold_in(seeds[4], 1), N_FSDP * GROUP // TOK_DEV)
    routes_turns = jax.random.permutation(jax.random.fold_in(seeds[4], 3), N_FSDP * GROUP // TOK_DEV)
    routes = jax.vmap(lambda own, number: deal_out(jax.random.fold_in(seeds[4], 2), own, number, TOK_DEV, EXPERTS, TOP, CAP, 1))(routes_keys, routes_turns).reshape((N_FSDP, GROUP, TOP))
    first_gain = jnp.clip(1.0 + 0.18 * jax.random.normal(seeds[5], (D,), jnp.float32), 0.1, 1.9)
    latent_gain = jnp.clip(1.0 + 0.18 * jax.random.normal(seeds[6], (LATENT,), jnp.float32), 0.1, 1.9)
    query_weight = gaussian(seeds[7], (D, HEADS * (NOPE + ROPE)), D ** -0.5, 0.125, ((0, 32),), jnp.float32)
    compress_weight = gaussian(seeds[8], (D, LATENT + ROPE), D ** -0.5, 0.125, ((0, 32),), jnp.float32)
    expand_weight = gaussian(seeds[9], (LATENT, HEADS * (NOPE + VDIM)), LATENT ** -0.5, 0.25, ((0, 32),), jnp.float32)
    output_weight = gaussian(seeds[10], (D, HEADS * VDIM), (HEADS * VDIM // 32) ** -0.5, 0.75, ((0, 32),), jnp.float32)
    second_gain = jnp.clip(1.0 + 0.18 * jax.random.normal(seeds[11], (D,), jnp.float32), 0.1, 1.9)
    router_weight = gaussian(seeds[12], (D, EXPERTS), (4 * D) ** -0.5, 0.0625, ((0, 32),), jnp.float32)
    shared_gate = gaussian(seeds[13], (D, SFF), D ** -0.5, 0.125, ((0, 32),), jnp.float32)
    shared_up = gaussian(seeds[14], (D, SFF), D ** -0.5, 0.125, ((0, 32),), jnp.float32)
    shared_down = gaussian(seeds[15], (D, SFF), SFF ** -0.5, 0.109375, ((0, 32),), jnp.float32)
    expert_gate = gaussian(seeds[16], (EXPERTS, D, FF), D ** -0.5, 0.125, ((0, 16), (1, 2)), jnp.float32)
    expert_up = gaussian(seeds[17], (EXPERTS, D, FF), D ** -0.5, 0.125, ((0, 16), (1, 2)), jnp.float32)
    expert_down = gaussian(seeds[18], (EXPERTS, D, FF), (max(1, 4 * FF // (EXPERTS * EXPERTS))) ** -0.5, 1.25, ((0, 16), (1, 2)), jnp.float32)
    return dict(tokens=tokens, cotangent=cotangent, lengths=lengths, token_order=token_order, routes=routes, first_gain=first_gain, latent_gain=latent_gain, query_weight=query_weight, compress_weight=compress_weight, expand_weight=expand_weight, output_weight=output_weight, second_gain=second_gain, router_weight=router_weight, shared_gate=shared_gate, shared_up=shared_up, shared_down=shared_down, expert_gate=expert_gate, expert_up=expert_up, expert_down=expert_down)


EPS = 1e-06
HIGH = lax.Precision.HIGHEST
NEGATIVE = -1e+30

@jax.custom_vjp
def low(v):
    return lax.optimization_barrier(v.astype(jnp.bfloat16)).astype(jnp.float32)

@jax.custom_vjp
def low_back(v):
    return v

def low_keep(v):
    return (low(v), None)

def low_pass(kept, grad):
    return (grad,)

def back_keep(v):
    return (v, None)

def back_low(kept, grad):
    return (low(grad),)
low.defvjp(low_keep, low_pass)
low_back.defvjp(back_keep, back_low)

def matmul(left, right):
    return jnp.dot(left, right, precision=HIGH, preferred_element_type=jnp.float32)

def matmul_t(left, right):
    return lax.dot_general(left, right, (((1,), (1,)), ((), ())), precision=HIGH, preferred_element_type=jnp.float32)

def rms_norm(value, gain):
    return value * lax.rsqrt(lax.optimization_barrier(jnp.mean(value * value, -1, keepdims=True)) + EPS) * gain

def rotate(value, position):
    half = value.shape[-1] // 2
    freq = 10000.0 ** (-jnp.arange(half, dtype=jnp.float32) / half)
    angle = position.astype(jnp.float32)[:, None] * freq[None, :]
    cosine = jnp.cos(angle)[:, None, :]
    sine = jnp.sin(angle)[:, None, :]
    first = value[..., :half]
    second = value[..., half:]
    return jnp.concatenate([first * cosine - second * sine, first * sine + second * cosine], -1)

def placement(lengths_row, order_row):
    ends = jnp.cumsum(lengths_row).astype(jnp.int32)
    starts = ends - lengths_row
    sequence = lax.optimization_barrier(jnp.sum((order_row[:, None] >= ends[None, :]).astype(jnp.int32), 1)).astype(jnp.int32)
    chosen = sequence[:, None] == jnp.arange(lengths_row.shape[0], dtype=jnp.int32)[None, :]
    offset = lax.optimization_barrier(jnp.sum(jnp.where(chosen, starts[None, :], 0), 1)).astype(jnp.int32)
    return (sequence, (order_row - offset).astype(jnp.int32))

def expert_slots(route_rows, experts):
    flat = route_rows.reshape(-1)
    onehot = (flat[:, None] == jnp.arange(experts, dtype=jnp.int32)[None, :]).astype(jnp.int32)
    before = jnp.cumsum(onehot, 0) - onehot
    return (flat, lax.optimization_barrier(jnp.sum(before * onehot, 1)).astype(jnp.int32))

def group_forward(hidden_in, sequence, position, route_rows, params):
    first_gain, latent_gain, query_weight, compress_weight, expand_weight, output_weight, second_gain, router_weight, shared_gate, shared_up, shared_down, expert_gate, expert_up, expert_down = params
    group = hidden_in.shape[0]
    normed = low(rms_norm(hidden_in, first_gain))
    query = low_back(matmul(normed, query_weight)).reshape(group, HEADS, NOPE + ROPE)
    query = low(jnp.concatenate([query[..., :NOPE], rotate(query[..., NOPE:], position)], -1))
    compressed = low_back(matmul(normed, compress_weight))
    latent = low(rms_norm(compressed[:, :LATENT], latent_gain))
    expanded = low_back(matmul(latent, expand_weight)).reshape(group, HEADS, NOPE + VDIM)
    shared_rope = rotate(compressed[:, None, LATENT:], position)
    keys = low(jnp.concatenate([expanded[..., :NOPE], jnp.broadcast_to(shared_rope, (group, HEADS, ROPE))], -1))
    values = low(expanded[..., NOPE:])
    scale = (NOPE + ROPE) ** (-0.5)
    block = min(512, group)

    def attend(pieces):
        query_block, seq_block, pos_block = pieces
        scores = low_back(jnp.einsum('qhd,khd->hqk', query_block, keys, precision=HIGH) * scale)
        visible = (seq_block[:, None] == sequence[None, :]) & (position[None, :] <= pos_block[:, None])
        scores = jnp.where(visible[None], scores, NEGATIVE)
        top_score = lax.optimization_barrier(jnp.max(scores, -1, keepdims=True))
        weights = jnp.where(visible[None], jnp.exp(scores - top_score), 0.0)
        weights = weights / lax.optimization_barrier(jnp.sum(weights, -1, keepdims=True))
        return jnp.einsum('hqk,khd->qhd', low(weights), values, precision=HIGH)
    mixed = lax.map(jax.checkpoint(attend), (query.reshape(group // block, block, HEADS, NOPE + ROPE), sequence.reshape(group // block, block), position.reshape(group // block, block)))
    mixed = low(low_back(mixed.reshape(group, HEADS * VDIM)))
    residual = hidden_in + low_back(matmul_t(mixed, output_weight))
    normed_two = low(rms_norm(residual, second_gain))
    logits = low_back(matmul(normed_two, router_weight))
    experts = router_weight.shape[1]
    pick = (route_rows[:, :, None] == jnp.arange(experts, dtype=jnp.int32)[None, None, :]).astype(jnp.float32)
    router_probs = jax.nn.softmax(logits, -1)
    gates = lax.optimization_barrier(jnp.sum(pick * router_probs[:, None, :], -1))
    shared_hidden = low(jax.nn.silu(low_back(matmul(normed_two, shared_gate))) * low_back(matmul(normed_two, shared_up)))
    shared_out = low_back(matmul_t(shared_hidden, shared_down))
    devices = group // TOK_DEV
    flat, slot = jax.vmap(lambda rows: expert_slots(rows, experts))(route_rows.reshape(devices, TOK_DEV, TOP))
    source = jnp.arange(devices, dtype=jnp.int32)[:, None]
    index = ((flat * devices + source) * CAP + slot).reshape(-1).astype(jnp.int32)
    rows_in = low_back(jnp.broadcast_to(normed_two[:, None, :], (group, TOP, D))).reshape(group * TOP, D)
    buffer = jnp.zeros((experts * devices * CAP, D), jnp.float32).at[index].set(rows_in)
    per_expert = buffer.reshape(experts, devices * CAP, D)

    def run_expert(pieces):
        rows, weight_gate, weight_up, weight_down = pieces
        gate_value = low_back(matmul(rows, weight_gate))
        up_value = low_back(matmul(rows, weight_up))
        hidden = low(jax.nn.silu(gate_value) * up_value)
        return low(low_back(matmul_t(hidden, weight_down)))
    produced = lax.map(run_expert, (per_expert, expert_gate, expert_up, expert_down))
    returned = produced.reshape(-1, D)[index].reshape(group, TOP, D)
    routed = lax.optimization_barrier(jnp.sum(gates[:, :, None] * returned, 1))
    return residual + routed + shared_out

def reference(tokens, cotangent, lengths, token_order, routes, first_gain, latent_gain, query_weight, compress_weight, expand_weight, output_weight, second_gain, router_weight, shared_gate, shared_up, shared_down, expert_gate, expert_up, expert_down):
    masters = (first_gain, latent_gain, query_weight, compress_weight, expand_weight, output_weight, second_gain, router_weight, shared_gate, shared_up, shared_down, expert_gate, expert_up, expert_down)
    located = [placement(lengths[group_id], token_order[group_id]) for group_id in range(N_FSDP)]

    def forward(hidden, *weights):
        lowered = tuple((low(weight) for weight in weights))
        return jnp.stack([group_forward(hidden[group_id], located[group_id][0], located[group_id][1], routes[group_id], lowered) for group_id in range(N_FSDP)])
    output, pullback = jax.vjp(forward, tokens.astype(jnp.float32), *masters)
    grads = pullback(cotangent.astype(jnp.float32))
    return (output, grads[0], grads[1], grads[2], grads[3], grads[4], grads[5], grads[6], grads[7], grads[8], grads[9], grads[10], grads[11], grads[12], grads[13], grads[14])
```

```python
import functools

import jax
import jax.numpy as jnp
from jax import lax
from jax.experimental import pallas as pl
from jax.experimental.pallas import tpu as pltpu
from jax.sharding import PartitionSpec as P

D = 2048
HEADS = 16
NOPE = 128
ROPE = 64
VDIM = 128
LATENT = 512
TOP = 6
EPS = 1e-06
NEGATIVE = -1e30
BF = jnp.bfloat16
F32 = jnp.float32


def matmul(left, right):
    return jnp.dot(left, right, preferred_element_type=F32)


def contract_last(left, right):
    return lax.dot_general(left, right, (((1,), (1,)), ((), ())), preferred_element_type=F32)


def leading_contraction(left, right):
    return lax.dot_general(left, right, (((0,), (0,)), ((), ())), preferred_element_type=F32)


def norm_scale(value):
    return lax.rsqrt(jnp.mean(value * value, -1, keepdims=True) + EPS)


def norm_back(value, scale, gain, grad):
    lifted = grad * gain
    return scale * lifted - value * (scale**3 * jnp.mean(lifted * value, -1, keepdims=True))


def turn(value, cosine, sine):
    half = value.shape[-1] // 2
    first, second = value[..., :half], value[..., half:]
    return jnp.concatenate([first * cosine - second * sine, first * sine + second * cosine], -1)


def swiglu_parts(gate, up):
    sigmoid = 1.0 / (1.0 + jnp.exp(-gate))
    act = gate * sigmoid
    return act, sigmoid * (1.0 + gate * (1.0 - sigmoid))


def box_of(count):
    dims = [2, 2]
    count //= 4
    while count > 1:
        side = 4 if count % 4 == 0 else 2
        dims.insert(0, side)
        count //= side
    return dims


class Box:
    def __init__(self):
        self.count = lax.axis_size("ctx")
        self.dims = box_of(self.count)
        self.strides = []
        stride = self.count
        for side in self.dims:
            stride //= side
            self.strides.append(stride)

    def shift(self, value, dim, by):
        side, stride = self.dims[dim], self.strides[dim]

        def target(i):
            here = i // stride % side
            return i + ((here + by) % side - here) * stride

        return lax.ppermute(value, "ctx", [(i, target(i)) for i in range(self.count)])

    def owners(self):
        me = lax.axis_index("ctx")
        owner = jnp.zeros((1,), jnp.int32)
        for side, stride in zip(self.dims, self.strides):
            here = me // stride % side
            offset = (here - jnp.arange(side, dtype=jnp.int32)) % side * stride
            owner = (offset[:, None] + owner[None, :]).reshape(-1)
        return owner

    def gather_step(self, held, dim):
        shifted = [self.shift(held, dim, k) for k in range(1, self.dims[dim])]
        return jnp.concatenate([held] + shifted, 0)

    def gather(self, held):
        for dim in range(len(self.dims)):
            held = self.gather_step(held, dim)
        return held

    def scatter_step(self, held, dim):
        parts = jnp.split(held, self.dims[dim], 0)
        total = parts[0].astype(F32)
        for k in range(1, self.dims[dim]):
            total = total + self.shift(parts[k], dim, -k).astype(F32)
        return total if dim == 0 else total.astype(held.dtype)

    def scatter(self, held):
        for dim in reversed(range(len(self.dims))):
            held = self.scatter_step(held, dim)
        return held


def after(event, *values):
    return lax.optimization_barrier((event,) + values)[1:]


def meet(*values):
    return lax.optimization_barrier(values)


MESH = pl.DeviceIdType.MESH
DMA = pltpu.SemaphoreType.DMA


def sides(count, both=False):
    found, stride, held = [], count, 1
    for side in box_of(count):
        stride //= side
        found.append(("ctx", side, stride, held))
        held *= side
    return found + ([("fsdp", 2, 1, held)] if both else [])


def moved(me, side, stride, by):
    here = me // stride % side
    return me + ((here + by) % side - here) * stride


def offset_of(count, me, owner):
    total = 0
    for _, side, stride, held in sides(count):
        total = total + (me // stride % side + side - owner // stride % side) % side * held
    return total


def remote(src, dst, send, recv, axis, target):
    return pltpu.make_async_remote_copy(
        src_ref=src,
        dst_ref=dst,
        send_sem=send,
        recv_sem=recv,
        device_id={axis: target},
        device_id_type=MESH,
    )


class Gather:
    def __init__(self, count, value, chunks):
        self.count, self.chunks = count, chunks
        self.out = jax.ShapeDtypeStruct((count,) + value.shape, value.dtype)
        self.scratch = [DMA, DMA((count, chunks)), DMA((count, chunks))]
        self.space, self.out_space = pl.ANY, pl.ANY
        self.reach = "box"

    def bind(self, me, half, x_ref, out_ref, own_sem, send_sem, recv_sem):
        self.me, self.x, self.o = me, x_ref, out_ref
        self.sems = (send_sem, recv_sem)
        self.own = pltpu.make_async_copy(x_ref, out_ref.at[0], own_sem)
        self.sent = []
        self.dims = sides(self.count)

    def copy(self, block, chunk, dim, by):
        _, side, stride, held = self.dims[dim]
        step = self.x.shape[0] // self.chunks
        part = pl.ds(chunk * step, step)
        src = self.x.at[part] if block == 0 else self.o.at[block, part]
        to = by * held + block
        return remote(
            src,
            self.o.at[to, part],
            self.sems[0].at[to, chunk],
            self.sems[1].at[to, chunk],
            "ctx",
            moved(self.me, side, stride, by),
        )

    def forward(self, block, chunk, first):
        for dim in range(first, len(self.dims)):
            for by in range(1, self.dims[dim][1]):
                copy = self.copy(block, chunk, dim, by)
                copy.start()
                self.sent.append(copy)

    def start(self):
        self.own.start()
        for chunk in range(self.chunks):
            self.forward(0, chunk, 0)

    def arrive(self, chunk, dim):
        _, side, _, held = self.dims[dim]
        for by in range(1, side):
            for block in range(held):
                self.copy(block, chunk, dim, by).wait_recv()
                self.forward(by * held + block, chunk, dim + 1)

    def steps(self):
        found, last = [], len(self.dims)
        for wave in range(self.chunks + last - 1):
            for dim in range(last):
                if 0 <= wave - dim < self.chunks:
                    found.append(functools.partial(self.arrive, wave - dim, dim))
        return found

    def finish(self):
        for copy in self.sent:
            copy.wait_send()
        self.own.wait()


class GatherAll:
    def __init__(self, count, value):
        self.count = count
        self.out = jax.ShapeDtypeStruct((count, 2) + value.shape, value.dtype)
        self.scratch = [DMA, DMA((count, 2)), DMA((count, 2))]
        self.space, self.out_space = pl.ANY, pl.ANY
        self.reach = "box+half"

    def bind(self, me, half, x_ref, out_ref, own_sem, send_sem, recv_sem):
        self.me, self.half, self.x, self.o = me, half, x_ref, out_ref
        self.sems = (send_sem, recv_sem)
        self.own = pltpu.make_async_copy(x_ref, out_ref.at[me, half], own_sem)
        self.sent = []
        self.dims = sides(self.count)

    def owner(self, block):
        owner = self.me
        for _, side, stride, held in self.dims:
            owner = moved(owner, side, stride, -(block // held % side))
        return owner

    def copy(self, block, other, dim, by):
        _, side, stride, held = self.dims[dim]
        owner = self.owner(block)
        half = 1 - self.half if other else self.half
        src = self.x if block == 0 and not other else self.o.at[owner, half]
        to = by * held + block
        return remote(
            src,
            self.o.at[owner, half],
            self.sems[0].at[to, other],
            self.sems[1].at[to, other],
            "ctx",
            moved(self.me, side, stride, by),
        )

    def arrived(self, block, other, dim, by):
        _, side, stride, held = self.dims[dim]
        to = by * held + block
        half = 1 - self.half if other else self.half
        here = self.o.at[self.owner(to), half]
        return remote(
            here, here, self.sems[0].at[to, other], self.sems[1].at[to, other], "ctx",
            moved(self.me, side, stride, by),
        )

    def across(self, half):
        return remote(
            self.x, self.o.at[self.me, half], self.sems[0].at[0, 0], self.sems[1].at[0, 0],
            "fsdp", 1 - self.half,
        )

    def forward(self, block, other, first):
        for dim in range(first, len(self.dims)):
            for by in range(1, self.dims[dim][1]):
                copy = self.copy(block, other, dim, by)
                copy.start()
                self.sent.append(copy)

    def start(self):
        self.own.start()
        self.cross = self.across(self.half)
        self.cross.start()
        self.forward(0, 0, 0)

    def meet(self):
        self.across(1 - self.half).wait_recv()
        self.forward(0, 1, 0)

    def arrive(self, dim):
        _, side, _, held = self.dims[dim]
        for other in range(2):
            for by in range(1, side):
                for block in range(held):
                    self.arrived(block, other, dim, by).wait_recv()
                    self.forward(by * held + block, other, dim + 1)

    def steps(self):
        return [self.meet] + [functools.partial(self.arrive, d) for d in range(len(self.dims))]

    def finish(self):
        for copy in self.sent:
            copy.wait_send()
        self.cross.wait_send()
        self.own.wait()


class Deal:
    def __init__(self, count, value, both=False, pick=None, place=None):
        self.count, self.both = count, both
        self.pick = pick or (lambda me, to: to)
        self.place = place or (lambda me, to: me)
        shape = value.shape[:1] + ((2,) if both else ()) + value.shape[1:]
        self.out = jax.ShapeDtypeStruct(shape, value.dtype)
        self.scratch = [DMA, DMA((count, 2)), DMA((count, 2))]
        self.space, self.out_space = pl.ANY, pl.ANY
        self.reach = "all+half" if both else "all"

    def bind(self, me, half, x_ref, out_ref, own_sem, send_sem, recv_sem):
        self.me, self.half, self.x, self.o = me, half, x_ref, out_ref
        self.send, self.recv = send_sem, recv_sem
        self.sent = []
        self.own = pltpu.make_async_copy(
            x_ref.at[self.pick(me, me)], self.here(self.place(me, me), half), own_sem
        )

    def here(self, slot, half):
        return self.o.at[slot, half] if self.both else self.o.at[slot]

    def copy(self, by):
        to = (self.me + by) % self.count
        return remote(
            self.x.at[self.pick(self.me, to)],
            self.here(self.place(self.me, to), self.half),
            self.send.at[by, 0],
            self.recv.at[by, 0],
            "ctx",
            to,
        )

    def arrived(self, by):
        source = (self.me + self.count - by) % self.count
        slot = self.here(self.place(source, self.me), self.half)
        return remote(
            slot, slot, self.send.at[by, 0], self.recv.at[by, 0], "ctx", (self.me + by) % self.count
        )

    def across(self, by, half):
        source = (self.me + self.count - by) % self.count
        slot = self.here(self.place(source, self.me), half)
        src = self.x.at[self.pick(self.me, self.me)] if by == 0 else slot
        return remote(
            src, slot, self.send.at[by, 1], self.recv.at[by, 1], "fsdp", 1 - self.half
        )

    def start(self):
        self.own.start()
        for by in range(1, self.count):
            copy = self.copy(by)
            copy.start()
            self.sent.append(copy)
        if self.both:
            self.pass_on(0)

    def pass_on(self, by):
        copy = self.across(by, self.half)
        copy.start()
        self.sent.append(copy)

    def arrive(self, by):
        self.arrived(by).wait_recv()
        if self.both:
            self.pass_on(by)

    def rest(self):
        for by in range(self.count):
            self.across(by, 1 - self.half).wait_recv()

    def steps(self):
        return [functools.partial(self.arrive, by) for by in range(1, self.count)]

    def finish(self):
        if self.both:
            self.rest()
        for copy in self.sent:
            copy.wait_send()
        self.own.wait()


class Scatter:
    def __init__(self, count, value, chunks, both=False):
        self.count, self.chunks, self.both = count, chunks, both
        tail = value.shape[1:]
        self.out = jax.ShapeDtypeStruct(tail, F32)
        dims = sides(count, both)
        blocks = value.shape[0]
        self.scratch = [
            pltpu.VMEM(((side - 1) * held,) + tail, value.dtype) for _, side, _, held in dims
        ]
        self.scratch += [pltpu.VMEM((held,) + tail, value.dtype) for _, _, _, held in dims[1:]]
        self.scratch += [DMA((blocks, chunks)), DMA((blocks, chunks))]
        self.space, self.out_space = pltpu.VMEM, pltpu.VMEM
        self.reach = "box+half" if both else "box"

    def bind(self, me, half, x_ref, out_ref, *scratch):
        self.me, self.half, self.o = me, half, out_ref
        self.blocks = x_ref.shape[0]
        self.dims = sides(self.count, self.both)
        levels = len(self.dims)
        self.landed = scratch[:levels]
        self.held = scratch[levels : 2 * levels - 1] + (x_ref,)
        self.send, self.recv = scratch[2 * levels - 1 :]
        self.sent = []

    def part(self, chunk):
        step = self.o.shape[0] // self.chunks
        return pl.ds(chunk * step, step)

    def copy(self, dim, block, chunk):
        axis, side, stride, held = self.dims[dim]
        part = self.part(chunk)
        here = self.me if axis == "ctx" else self.half
        return remote(
            self.held[dim].at[block, part],
            self.landed[dim].at[block - held, part],
            self.send.at[block, chunk],
            self.recv.at[block, chunk],
            axis,
            moved(here, side, stride, -(block // held)),
        )

    def ready(self, dim, block, chunk):
        if block >= self.dims[dim][3]:
            copy = self.copy(dim, block, chunk)
            copy.start()
            self.sent.append(copy)

    def add(self, dim, chunk):
        _, side, _, held = self.dims[dim]
        part = self.part(chunk)
        for block in reversed(range(held)):
            total = self.held[dim][block, part].astype(F32)
            for by in range(1, side):
                self.copy(dim, by * held + block, chunk).wait_recv()
                total = total + self.landed[dim][(by - 1) * held + block, part].astype(F32)
            if dim == 0:
                self.o[part] = total
            else:
                self.held[dim - 1][block, part] = total.astype(self.held[dim - 1].dtype)
                self.ready(dim - 1, block, chunk)

    def start(self):
        last = len(self.dims) - 1
        for chunk in range(self.chunks):
            for block in reversed(range(self.dims[last][3], self.blocks)):
                self.ready(last, block, chunk)

    def steps(self):
        found, levels = [], len(self.dims)
        for wave in range(self.chunks + levels - 1):
            for dim in reversed(range(levels)):
                chunk = wave - (levels - 1 - dim)
                if 0 <= chunk < self.chunks:
                    found.append(functools.partial(self.add, dim, chunk))
        return found

    def finish(self):
        for copy in self.sent:
            copy.wait_send()


def exchange_kernel(count, plans, early, *refs):
    me, half = lax.axis_index("ctx"), lax.axis_index("fsdp")
    ins, refs = refs[: len(plans)], refs[len(plans) :]
    outs, refs = refs[: len(plans)], refs[len(plans) :]
    barrier = pltpu.get_barrier_semaphore()
    peers = []
    if any("all" in plan.reach for plan in plans):
        peers = [("ctx", (me + by) % count) for by in range(1, count)]
    else:
        for _, side, stride, _ in sides(count):
            peers += [("ctx", moved(me, side, stride, by)) for by in range(1, side)]
    if any("half" in plan.reach for plan in plans):
        peers.append(("fsdp", 1 - half))
    for axis, target in peers:
        pl.semaphore_signal(barrier, inc=1, device_id={axis: target}, device_id_type=MESH)
    pl.semaphore_wait(barrier, len(peers))
    for plan, x_ref, out_ref in zip(plans, ins, outs):
        mine, refs = refs[: len(plan.scratch)], refs[len(plan.scratch) :]
        plan.bind(me, half, x_ref, out_ref, *mine)
        plan.start()
    for plan in plans[:early]:
        for step in plan.steps():
            step()
    queues = [plan.steps() for plan in plans[early:]]
    longest = max(len(queue) for queue in queues)
    done = [0] * len(queues)
    for turn in range(longest):
        for i, queue in enumerate(queues):
            upto = (turn + 1) * len(queue) // longest
            for step in queue[done[i] : upto]:
                step()
            done[i] = upto
    for plan in plans:
        plan.finish()


def exchange(count, collective, values, plans, early=0):
    scratch = [ref for plan in plans for ref in plan.scratch]
    return pl.pallas_call(
        functools.partial(exchange_kernel, count, plans, early),
        out_shape=tuple(plan.out for plan in plans),
        in_specs=[pl.BlockSpec(memory_space=plan.space) for plan in plans],
        out_specs=tuple(pl.BlockSpec(memory_space=plan.out_space) for plan in plans),
        scratch_shapes=scratch,
        compiler_params=pltpu.CompilerParams(
            collective_id=collective, has_side_effects=True, vmem_limit_bytes=56 << 20
        ),
        cost_estimate=pl.CostEstimate(flops=0, bytes_accessed=100 << 20, transcendentals=0),
    )(*values)


def placement(lengths_row, order_row):
    ends = jnp.cumsum(lengths_row)
    starts = ends - lengths_row
    sequence = jnp.sum((order_row[:, None] >= ends[None, :]).astype(jnp.int32), 1)
    chosen = sequence[:, None] == jnp.arange(lengths_row.shape[0], dtype=jnp.int32)[None, :]
    offset = jnp.sum(jnp.where(chosen, starts[None, :], 0), 1)
    return (sequence, order_row - offset)


def spread(weight, count, repeat):
    rows = weight.shape[0]
    parts = jnp.transpose(weight.astype(BF).reshape(rows, count // repeat, -1), (1, 0, 2))
    return jnp.repeat(parts, repeat, 0) if repeat > 1 else parts


def pad_last(value, width):
    return jnp.pad(value, [(0, 0)] * (value.ndim - 1) + [(0, width - value.shape[-1])])


def up_to(width, unit=128):
    return -(-width // unit) * unit


def local(
    tokens,
    cotangent,
    lengths,
    token_order,
    routes,
    first_gain,
    latent_gain,
    query_weight,
    compress_weight,
    expand_weight,
    output_weight,
    second_gain,
    router_weight,
    shared_gate,
    shared_up,
    shared_down,
    expert_gate,
    expert_up,
    expert_down,
):
    box = Box()
    count = box.count
    repeat = max(1, count // HEADS)
    rows = tokens.shape[1]
    group = rows * count
    asked = group // repeat
    experts = router_weight.shape[1]
    shard = query_weight.shape[0]
    width = NOPE + ROPE
    me = lax.axis_index("ctx")
    both = ("ctx", "fsdp")
    all_devices = count * lax.axis_size("fsdp")

    half = lax.axis_index("fsdp")
    small_vmem = count * rows * D * 2 <= 12 << 20

    def reduce_blocks(collective, value, *more):
        if small_vmem:
            plans = [plan for _, plan in more] + [Scatter(count, value, 4)]
            got = exchange(count, collective, [v for v, _ in more] + [value], plans)
            return (got[-1],) + tuple(got[:-1])
        rest = exchange(count, collective, [v for v, _ in more], [p for _, p in more]) if more else ()
        return (box.scatter(value)[0],) + tuple(rest)

    def across(value):
        return lax.ppermute(value, "fsdp", [(0, 1), (1, 0)])

    def both_halves(value):
        other = across(value)
        first, second = jnp.where(half == 0, value, other), jnp.where(half == 0, other, value)
        return jnp.stack([first, second], 1)

    def halves_sent(parts):
        own = lax.dynamic_index_in_dim(parts, half, 1, keepdims=False)
        other = lax.dynamic_index_in_dim(parts, 1 - half, 1, keepdims=False)
        return own, across(other.astype(BF))

    def halves_summed(parts):
        own, got = halves_sent(parts)
        return own.astype(F32) + got.astype(F32)

    owners = box.owners()

    small_cols = compress_weight.shape[1] + experts + 3
    lat_rows = latent_gain.shape[0]
    small = jnp.concatenate(
        [
            compress_weight,
            router_weight,
            first_gain[:, None],
            second_gain[:, None],
            jnp.pad(latent_gain, (0, shard - lat_rows))[:, None],
        ],
        1,
    ).astype(BF)
    small = pad_last(small, up_to(small_cols))
    query_parts = spread(query_weight, count, repeat)
    expand_parts = spread(expand_weight, count, repeat)
    small_all = lax.all_gather(small, both, axis=0, tiled=True)
    gate_expert = lax.all_gather(expert_gate[0].astype(BF), "fsdp", axis=0, tiled=True)
    query_own, expand_own, token_all = exchange(
        count,
        0,
        [query_parts, expand_parts, tokens[0]],
        [
            Deal(count, query_parts, both=True),
            Deal(count, expand_parts, both=True),
            Gather(count, tokens[0], 4),
        ],
        early=2,
    )
    token_all = token_all.reshape(group, D)
    query_own = query_own.reshape(D, -1)
    expand_own = expand_own.reshape(LATENT, -1)
    edge = compress_weight.shape[1]
    compress_full = small_all[:, :edge]
    router_full = small_all[:, edge : edge + experts]
    gain_first = small_all[:, edge + experts].astype(F32)
    gain_second = small_all[:, edge + experts + 1].astype(F32)
    gain_latent = small_all[:, edge + experts + 2].reshape(all_devices, shard)[:, :lat_rows]
    gain_latent = gain_latent.reshape(-1).astype(F32)

    output_cast, up_cast, down_cast = after(
        token_all, output_weight, expert_up[0], expert_down[0]
    )
    output_full = lax.all_gather(output_cast.astype(BF), both, axis=0, tiled=True)
    up_expert = lax.all_gather(up_cast.astype(BF), "fsdp", axis=0, tiled=True)
    down_expert = lax.all_gather(down_cast.astype(BF), "fsdp", axis=0, tiled=True)

    cot_low, route_own, gate_cols, up_cols, down_cols = after(
        token_all, cotangent[0].astype(BF), routes[0], shared_gate, shared_up, shared_down
    )
    fs = shared_gate.shape[1] // count
    fp = up_to(fs)
    rest = jnp.concatenate(
        [spread(gate_cols, count, 1), spread(up_cols, count, 1), spread(down_cols, count, 1)], -1
    )
    rest = pad_last(rest, up_to(3 * fs))
    rest = lax.all_to_all(rest, "ctx", split_axis=0, concat_axis=0, tiled=True)
    order_all = jnp.take(token_order[0].reshape(count, rows), owners, axis=0).reshape(-1)
    sequence, position = placement(lengths[0], order_all)
    turns = ROPE // 2
    freq = 10000.0 ** (-jnp.arange(turns, dtype=F32) / turns)
    angle = position.astype(F32)[:, None] * freq[None, :]
    cosine, sine = jnp.cos(angle), jnp.sin(angle)

    hidden_all = token_all.astype(F32)
    normed_all = (hidden_all * norm_scale(hidden_all) * gain_first).astype(BF)
    query_raw = matmul(normed_all[:asked], query_own)
    query = jnp.concatenate(
        [query_raw[:, :NOPE], turn(query_raw[:, NOPE:], cosine[:asked], sine[:asked])], -1
    ).astype(BF)
    compressed = matmul(normed_all, compress_full)
    compressed, rest = meet(compressed, rest)
    rest = both_halves(rest).reshape(D, -1)
    rest_own = rest
    sgate_own = pad_last(rest_own[:, :fs], fp)
    sup_own = pad_last(rest_own[:, fs : 2 * fs], fp)
    sdown_own = pad_last(rest_own[:, 2 * fs : 3 * fs], fp)
    low_part = compressed[:, :LATENT]
    latent_scale = norm_scale(low_part)
    latent = (low_part * latent_scale * gain_latent).astype(BF)
    expanded = matmul(latent, expand_own)
    keys = jnp.concatenate(
        [expanded[:, :NOPE], turn(compressed[:, LATENT:], cosine, sine)], -1
    ).astype(BF)
    values = expanded[:, NOPE:].astype(BF)
    keys, gate_expert = meet(keys, gate_expert)
    scale = width ** (-0.5)
    visible = (sequence[:asked, None] == sequence[None, :]) & (
        position[None, :] <= position[:asked, None]
    )
    scores = jnp.where(visible, contract_last(query, keys) * scale, NEGATIVE)
    peak = jnp.max(scores, -1, keepdims=True)
    weights = jnp.where(visible, jnp.exp(scores - peak), 0.0)
    total = jnp.sum(weights, -1, keepdims=True)
    mixed_f = matmul(weights.astype(BF), values) / total
    logsum = peak + jnp.log(total)

    def to_owner(value):
        if repeat > 1:
            value = jnp.pad(value, ((0, group - asked), (0, 0)))
        value = value.reshape(count, rows, -1)
        plan = Deal(count, value, pick=lambda me, to: offset_of(count, me, to))
        (got,) = exchange(count, 1, [value], [plan])
        if repeat > 1:
            got = jnp.sum(got.reshape(HEADS, repeat, rows, -1).astype(F32), 1).astype(BF)
        return jnp.transpose(got, (1, 0, 2)).reshape(rows, -1)

    def to_head(value):
        value = jnp.transpose(value.reshape(rows, HEADS, -1), (1, 0, 2))
        if repeat > 1:
            value = jnp.repeat(value, repeat, 0)
        plan = Deal(count, value, place=lambda me, to: offset_of(count, to, me))
        (got,) = exchange(count, 4, [value], [plan])
        return got.reshape(group, -1)[:asked]

    mixed = to_owner(mixed_f.astype(BF))
    hidden = tokens[0].astype(F32)
    residual = hidden + contract_last(mixed, output_full)

    residual_scale = norm_scale(residual)
    normed_two = (residual * residual_scale * gain_second).astype(BF)
    (two_all,) = exchange(count, 2, [normed_two], [Gather(count, normed_two, 4)])
    two_all = two_all.reshape(group, D)
    route_all = box.gather(route_own)
    two_all, up_expert, cot_low = meet(two_all, up_expert, cot_low)
    cot_held = box.gather_step(cot_low, 0)
    probs_all = jax.nn.softmax(matmul(two_all, router_full), -1)
    mine = jnp.any(route_all == me, -1)
    capacity = rows * TOP * 4 // (3 * experts) * count
    slot = jnp.where(mine, jnp.cumsum(mine.astype(jnp.int32)) - 1, -1)
    slots = jnp.arange(capacity, dtype=jnp.int32)
    chosen = slots[:, None] == slot[None, :]
    pick = chosen.astype(BF)
    column = jnp.arange(experts, dtype=jnp.int32)[None, :] == me
    gate_tok = jnp.where(mine, jnp.sum(jnp.where(column, probs_all, 0.0), -1), 0.0)
    gate_row = jnp.sum(jnp.where(chosen, gate_tok[None, :], 0.0), 1)
    rows_in = matmul(pick, two_all).astype(BF)

    gate_val = matmul(rows_in, gate_expert)
    up_val = matmul(rows_in, up_expert)
    gate_val, cot_held = meet(gate_val, cot_held)
    for dim in range(1, len(box.dims) - 1):
        cot_held = box.gather_step(cot_held, dim)
    act, slope = swiglu_parts(gate_val, up_val)
    expert_hidden = (act * up_val).astype(BF)
    produced = contract_last(expert_hidden, down_expert).astype(BF)
    sg = matmul(two_all, sgate_own)
    su = matmul(two_all, sup_own)
    sact, sslope = swiglu_parts(sg, su)
    shared_hidden = (sact * su).astype(BF)
    out_two = (
        gate_tok[:, None] * leading_contraction(pick, produced)
        + contract_last(shared_hidden, sdown_own)
    ).astype(BF)

    out_two, cot_held = meet(out_two, cot_held)
    cot_all = box.gather_step(cot_held, len(box.dims) - 1)
    out_held = box.scatter_step(out_two, len(box.dims) - 1)
    cot_rows = matmul(pick, cot_all)
    grad_in = (gate_row[:, None] * cot_rows).astype(BF)
    grad_hidden = matmul(grad_in, down_expert)
    grad_hidden, out_held = meet(grad_hidden, out_held)
    for dim in reversed(range(1, len(box.dims) - 1)):
        out_held = box.scatter_step(out_held, dim)
    grad_eg = (grad_hidden * up_val * slope).astype(BF)
    grad_eu = (grad_hidden * act).astype(BF)
    grad_rows = (contract_last(grad_eg, gate_expert) + contract_last(grad_eu, up_expert)).astype(BF)
    gg_row = jnp.sum(cot_rows * produced.astype(F32), -1)
    gg_tok = jnp.sum(jnp.where(chosen, gg_row[:, None], 0.0), 0)
    grad_sh = matmul(cot_all, sdown_own)
    grad_sg = (grad_sh * su * sslope).astype(BF)
    grad_su = (grad_sh * sact).astype(BF)
    grad_two_part = (
        leading_contraction(pick, grad_rows)
        + contract_last(grad_sg, sgate_own)
        + contract_last(grad_su, sup_own)
    ).astype(BF)
    gg_part = jnp.where(column, gg_tok[:, None], 0.0)
    grad_two_part, out_held = meet(grad_two_part, out_held)
    output = residual + box.scatter_step(out_held, 0)
    d_gate = leading_contraction(rows_in, grad_eg).astype(BF)
    d_up = leading_contraction(rows_in, grad_eu).astype(BF)
    d_down = leading_contraction(grad_in, expert_hidden).astype(BF)
    d_experts = [
        lax.psum_scatter(v, "fsdp", scatter_dimension=0, tiled=True).astype(F32)[None]
        for v in (d_gate, d_up, d_down)
    ]
    d_rest = jnp.concatenate(
        [
            leading_contraction(two_all, grad_sg)[:, :fs],
            leading_contraction(two_all, grad_su)[:, :fs],
            leading_contraction(cot_all, shared_hidden)[:, :fs],
        ],
        1,
    ).astype(BF)
    d_rest = pad_last(d_rest, up_to(3 * fs)).reshape(count, 2, shard, -1)
    grad_two_part, gg_part, d_rest, d_gate, d_up, d_down, output = meet(
        grad_two_part, gg_part, d_rest, d_gate, d_up, d_down, output
    )
    rest_mine, rest_got = halves_sent(d_rest)
    grad_two, grad_gates = reduce_blocks(
        3,
        grad_two_part.reshape(count, rows, D),
        (gg_part.reshape(count, rows, -1), Scatter(count, gg_part.reshape(count, rows, -1), 1)),
    )

    probs = probs_all[:rows]
    grad_logits = probs * (grad_gates - jnp.sum(probs * grad_gates, -1, keepdims=True))
    grad_logits = grad_logits.astype(BF)
    grad_two = grad_two + contract_last(grad_logits, router_full)
    d_router = leading_contraction(normed_two, grad_logits)
    d_second = jnp.sum(grad_two * residual * residual_scale, 0)
    grad_residual = cotangent[0] + norm_back(residual, residual_scale, gain_second, grad_two)

    attended = grad_residual.astype(BF)
    grad_mixed = to_head(matmul(attended, output_full).astype(BF))
    by_owner = jnp.take(attended.reshape(rows, count, -1), owners, axis=1).reshape(rows, -1)
    grad_mixed, rest_mine, rest_got = meet(grad_mixed, rest_mine, rest_got)
    d_rest = (rest_mine.astype(F32) + rest_got.astype(F32)).astype(BF)
    d_rest = lax.all_to_all(d_rest, "ctx", split_axis=0, concat_axis=0, tiled=True).astype(F32)

    d_output = leading_contraction(by_owner, mixed).astype(BF)
    d_output = box.scatter_step(d_output, len(box.dims) - 1)
    delta = jnp.sum(grad_mixed.astype(F32) * mixed_f, -1, keepdims=True)
    probs_a = jnp.where(visible, jnp.exp(contract_last(query, keys) * scale - logsum), 0.0)
    grad_probs = contract_last(grad_mixed, values)
    grad_scores = (probs_a * (grad_probs - delta)).astype(BF)
    grad_scores, d_output = meet(grad_scores, d_output)
    for dim in reversed(range(1, len(box.dims) - 1)):
        d_output = box.scatter_step(d_output, dim)
    grad_query = matmul(grad_scores, keys) * scale
    grad_keys = leading_contraction(grad_scores, query) * scale
    grad_values = leading_contraction(probs_a.astype(BF), grad_mixed)
    grad_expanded = jnp.concatenate([grad_keys[:, :NOPE], grad_values], -1).astype(BF)
    grad_latent = contract_last(grad_expanded, expand_own)
    d_expand = leading_contraction(latent, grad_expanded)
    d_latent = jnp.sum(grad_latent * low_part * latent_scale, 0)
    grad_comp = jnp.concatenate(
        [
            norm_back(low_part, latent_scale, gain_latent, grad_latent),
            turn(grad_keys[:, NOPE:], cosine, -sine),
        ],
        -1,
    ).astype(BF)
    grad_qraw = jnp.concatenate(
        [grad_query[:, :NOPE], turn(grad_query[:, NOPE:], cosine[:asked], -sine[:asked])], -1
    ).astype(BF)
    grad_comp, d_output = meet(grad_comp, d_output)
    d_output = box.scatter_step(d_output, 0)
    d_query = leading_contraction(normed_all[:asked], grad_qraw)
    d_compress = leading_contraction(normed_all, grad_comp)
    d_first = (
        jnp.sum(d_query * query_own.astype(F32), 1) + jnp.sum(d_compress * compress_full.astype(F32), 1)
    ) / gain_first

    d_q = halves_summed(d_query.reshape(count, 2, shard, -1)).astype(BF)
    d_e = halves_summed(d_expand.reshape(count, 2, -1, d_expand.shape[-1])).astype(BF)
    d_lat = jnp.pad(d_latent.reshape(all_devices, lat_rows), ((0, 0), (0, shard - lat_rows)))
    d_small = jnp.concatenate(
        [d_compress, d_router, d_first[:, None], d_second[:, None], d_lat.reshape(-1)[:, None]], 1
    ).astype(BF)
    d_small = pad_last(d_small, up_to(small_cols)).reshape(count, 2, shard, -1)
    d_small = jnp.take(d_small, owners, axis=0)
    d_small = jnp.where(half == 0, d_small, d_small[:, ::-1])
    d_small = jnp.transpose(d_small, (1, 0, 2, 3)).reshape(2 * count, shard, -1)
    from_query = contract_last(grad_qraw, query_own)
    if repeat > 1:
        from_query = jnp.pad(from_query, ((0, group - asked), (0, 0)))
    grad_norm_part = (from_query + contract_last(grad_comp, compress_full)).astype(BF)
    grad_norm_part, d_output, d_rest = meet(grad_norm_part, d_output, d_rest)
    output_mine, output_got = halves_sent(d_output.reshape(1, 2, shard, -1))
    grad_norm, d_small, d_q, d_e = reduce_blocks(
        5,
        grad_norm_part.reshape(count, rows, D),
        (d_small, Scatter(count, d_small, 1, both=True)),
        (d_q, Deal(count, d_q)),
        (d_e, Deal(count, d_e)),
    )
    output_mine, output_got = after(grad_norm, output_mine, output_got)
    d_output = (output_mine.astype(F32) + output_got.astype(F32))[0]
    grad_tokens = grad_residual + norm_back(hidden, norm_scale(hidden), gain_first, grad_norm)

    def joined(parts, times):
        if times > 1:
            parts = jnp.sum(parts.astype(F32).reshape(count // times, times, *parts.shape[1:]), 1)
        return jnp.transpose(parts.astype(F32), (1, 0, 2)).reshape(parts.shape[1], -1)

    return (
        output[None],
        grad_tokens[None],
        d_small[:, edge + experts],
        d_small[:lat_rows, edge + experts + 2],
        joined(d_q, repeat),
        d_small[:, :edge],
        joined(d_e, repeat),
        d_output,
        d_small[:, edge + experts + 1],
        d_small[:, edge : edge + experts],
        joined(d_rest[:, :, :fs], 1),
        joined(d_rest[:, :, fs : 2 * fs], 1),
        joined(d_rest[:, :, 2 * fs : 3 * fs], 1),
        *d_experts,
    )


def shifted(shard, axis, by):
    devices = lax.axis_size(axis)
    return lax.ppermute(shard, axis, [(i, (i + by) % devices) for i in range(devices)])


def rms_norm(value, gain):
    return value * lax.rsqrt(jnp.mean(value * value, -1, keepdims=True) + EPS) * gain


def rotate(value, position):
    half = value.shape[-1] // 2
    freq = 10000.0 ** (-jnp.arange(half, dtype=jnp.float32) / half)
    angle = position.astype(jnp.float32)[:, None] * freq[None, :]
    cosine = jnp.cos(angle)[:, None, :]
    sine = jnp.sin(angle)[:, None, :]
    first = value[..., :half]
    second = value[..., half:]
    return jnp.concatenate([first * cosine - second * sine, first * sine + second * cosine], -1)


def expert_slots(route_rows, experts):
    flat = route_rows.reshape(-1)
    onehot = (flat[:, None] == jnp.arange(experts, dtype=jnp.int32)[None, :]).astype(jnp.int32)
    before = jnp.cumsum(onehot, 0) - onehot
    return (flat, jnp.sum(before * onehot, 1))


def swiglu(gate_value, up_value):
    return jax.nn.silu(gate_value) * up_value


def softmax_last(value):
    return jax.nn.softmax(value, -1)


def local_gathered(
    tokens,
    cotangent,
    lengths,
    token_order,
    routes,
    first_gain,
    latent_gain,
    query_weight,
    compress_weight,
    expand_weight,
    output_weight,
    second_gain,
    router_weight,
    shared_gate,
    shared_up,
    shared_down,
    expert_gate,
    expert_up,
    expert_down,
):
    (
        gain_first,
        gain_latent,
        query_full,
        compress_full,
        expand_full,
        output_full,
        gain_second,
        router_full,
        shared_gate_full,
        shared_up_full,
        shared_down_full,
    ) = (
        lax.all_gather(first_gain.astype(jnp.bfloat16), ("ctx", "fsdp"), axis=0, tiled=True),
        lax.all_gather(latent_gain.astype(jnp.bfloat16), ("ctx", "fsdp"), axis=0, tiled=True),
        lax.all_gather(query_weight.astype(jnp.bfloat16), ("ctx", "fsdp"), axis=0, tiled=True),
        lax.all_gather(compress_weight.astype(jnp.bfloat16), ("ctx", "fsdp"), axis=0, tiled=True),
        lax.all_gather(expand_weight.astype(jnp.bfloat16), ("ctx", "fsdp"), axis=0, tiled=True),
        lax.all_gather(output_weight.astype(jnp.bfloat16), ("ctx", "fsdp"), axis=0, tiled=True),
        lax.all_gather(second_gain.astype(jnp.bfloat16), ("ctx", "fsdp"), axis=0, tiled=True),
        lax.all_gather(router_weight.astype(jnp.bfloat16), ("ctx", "fsdp"), axis=0, tiled=True),
        lax.all_gather(shared_gate.astype(jnp.bfloat16), ("ctx", "fsdp"), axis=0, tiled=True),
        lax.all_gather(shared_up.astype(jnp.bfloat16), ("ctx", "fsdp"), axis=0, tiled=True),
        lax.all_gather(shared_down.astype(jnp.bfloat16), ("ctx", "fsdp"), axis=0, tiled=True),
    )
    gate_expert, up_expert, down_expert = (
        lax.all_gather(expert_gate.astype(jnp.bfloat16), "fsdp", axis=1, tiled=True),
        lax.all_gather(expert_up.astype(jnp.bfloat16), "fsdp", axis=1, tiled=True),
        lax.all_gather(expert_down.astype(jnp.bfloat16), "fsdp", axis=1, tiled=True),
    )
    gate_expert = gate_expert[0]
    up_expert = up_expert[0]
    down_expert = down_expert[0]
    rows = tokens.shape[1]
    place = lax.axis_index("ctx")
    devices = lax.axis_size("ctx")
    query_width = NOPE + ROPE
    sequence, position = placement(lengths[0], token_order[0])
    own_seq = lax.dynamic_slice_in_dim(sequence, place * rows, rows)
    own_pos = lax.dynamic_slice_in_dim(position, place * rows, rows)

    def visible_mask(start, count):
        key_seq = lax.dynamic_slice_in_dim(sequence, start, count)
        key_pos = lax.dynamic_slice_in_dim(position, start, count)
        return (own_seq[:, None] == key_seq[None, :]) & (key_pos[None, :] <= own_pos[:, None])

    def turn_query(part):
        return rotate(part, own_pos)

    def turn_key(part):
        return rotate(part[:, None, :], own_pos)[:, 0, :]

    hidden = tokens[0].astype(jnp.float32)
    normed_f, norm_pull = jax.vjp(rms_norm, hidden, gain_first.astype(jnp.float32))
    normed = normed_f.astype(jnp.bfloat16)
    query_raw = matmul(normed, query_full).reshape(rows, HEADS, query_width)
    query_rotated, query_pull = jax.vjp(turn_query, query_raw[..., NOPE:])
    query = jnp.concatenate([query_raw[..., :NOPE], query_rotated], -1).astype(jnp.bfloat16)
    compressed = matmul(normed, compress_full)
    latent_f, latent_pull = jax.vjp(
        rms_norm, compressed[:, :LATENT], gain_latent.astype(jnp.float32)
    )
    latent = latent_f.astype(jnp.bfloat16)
    expanded = matmul(latent, expand_full).reshape(rows, HEADS, NOPE + VDIM)
    key_rot, key_pull = jax.vjp(turn_key, compressed[:, LATENT:])
    keys = jnp.concatenate(
        [expanded[..., :NOPE], jnp.broadcast_to(key_rot[:, None, :], (rows, HEADS, ROPE))], -1
    )
    keys = keys.astype(jnp.bfloat16).reshape(rows, HEADS * query_width)
    values = expanded[..., NOPE:].astype(jnp.bfloat16).reshape(rows, HEADS * VDIM)
    scale = query_width ** (-0.5)
    running = jnp.full((HEADS, rows), NEGATIVE, jnp.float32)
    key_piece = lax.all_gather(keys, "ctx", axis=0, tiled=True)
    value_piece = lax.all_gather(values, "ctx", axis=0, tiled=True)
    count = key_piece.shape[0]
    scores = (
        jnp.einsum(
            "qhd,khd->hqk",
            query,
            key_piece.reshape(count, HEADS, query_width),
            preferred_element_type=jnp.float32,
        )
        * scale
    )
    visible = visible_mask(jnp.int32(0), count)[None]
    masked = jnp.where(visible, scores, NEGATIVE)
    newest = jnp.maximum(running, jnp.max(masked, -1))
    weights = jnp.where(visible, jnp.exp(masked - newest[..., None]), 0.0)
    total = jnp.sum(weights, -1)
    summed = jnp.einsum(
        "hqk,khd->qhd",
        weights.astype(jnp.bfloat16),
        value_piece.reshape(count, HEADS, VDIM),
        preferred_element_type=jnp.float32,
    )
    running, total, summed = (newest, total, summed)
    mixed_f = summed / jnp.transpose(total)[:, :, None]
    logsum = running + jnp.log(total)
    mixed = mixed_f.astype(jnp.bfloat16).reshape(rows, HEADS * VDIM)
    residual = hidden + contract_last(mixed, output_full)
    normed_two_f, norm_two_pull = jax.vjp(rms_norm, residual, gain_second.astype(jnp.float32))
    normed_two = normed_two_f.astype(jnp.bfloat16)
    logits = matmul(normed_two, router_full)
    experts = router_full.shape[1]
    route_rows = routes[0]
    pick = (route_rows[:, :, None] == jnp.arange(experts, dtype=jnp.int32)[None, None, :]).astype(
        jnp.float32
    )
    router_probs, gate_pull = jax.vjp(softmax_last, logits)
    gates = jnp.sum(pick * router_probs[:, None, :], -1)
    shared_gate_val = matmul(normed_two, shared_gate_full)
    shared_up_val = matmul(normed_two, shared_up_full)
    shared_hidden = swiglu(shared_gate_val, shared_up_val).astype(jnp.bfloat16)
    shared_out = contract_last(shared_hidden, shared_down_full)
    capacity = rows * TOP * 4 // (3 * experts)
    flat, slot = expert_slots(route_rows, experts)
    anchor = jnp.arange(rows * TOP, dtype=jnp.int32) // TOP
    outgoing = (
        jnp.zeros((experts, capacity, D), jnp.bfloat16).at[flat, slot].set(normed_two[anchor])
    )
    arrived = lax.all_to_all(outgoing, "ctx", split_axis=0, concat_axis=0, tiled=True)
    received_rows = arrived.reshape(-1, D)
    gate_val = matmul(received_rows, gate_expert)
    up_val = matmul(received_rows, up_expert)
    expert_hidden = swiglu(gate_val, up_val).astype(jnp.bfloat16)
    produced = contract_last(expert_hidden, down_expert).astype(jnp.bfloat16).reshape(arrived.shape)
    returned = lax.all_to_all(produced, "ctx", split_axis=0, concat_axis=0, tiled=True)
    route_out = returned[flat, slot].astype(jnp.float32).reshape(rows, TOP, D)
    routed = jnp.sum(gates[:, :, None] * route_out, 1)
    output = residual + routed + shared_out
    grad_out = cotangent[0]
    grad_low = grad_out.astype(jnp.bfloat16)
    grad_shared_hidden = matmul(grad_low, shared_down_full)
    grad_sdown = leading_contraction(grad_low, shared_hidden)
    grad_sg, grad_su = jax.vjp(swiglu, shared_gate_val, shared_up_val)[1](grad_shared_hidden)
    grad_sg = grad_sg.astype(jnp.bfloat16)
    grad_su = grad_su.astype(jnp.bfloat16)
    grad_sgate = leading_contraction(normed_two, grad_sg)
    grad_sup = leading_contraction(normed_two, grad_su)
    grad_normed_two = contract_last(grad_sg, shared_gate_full) + contract_last(
        grad_su, shared_up_full
    )
    grad_gates = jnp.sum(grad_out[:, None, :] * route_out, -1)
    grad_route = (
        (gates[:, :, None] * grad_out[:, None, :]).astype(jnp.bfloat16).reshape(rows * TOP, D)
    )
    grad_outgoing = jnp.zeros((experts, capacity, D), jnp.bfloat16).at[flat, slot].set(grad_route)
    grad_arrived = lax.all_to_all(
        grad_outgoing, "ctx", split_axis=0, concat_axis=0, tiled=True
    ).reshape(-1, D)
    grad_expert_hidden = matmul(grad_arrived, down_expert)
    grad_edown = leading_contraction(grad_arrived, expert_hidden)
    grad_eg, grad_expert_up_value = jax.vjp(swiglu, gate_val, up_val)[1](grad_expert_hidden)
    grad_eg = grad_eg.astype(jnp.bfloat16)
    grad_expert_up_value = grad_expert_up_value.astype(jnp.bfloat16)
    grad_egate = leading_contraction(received_rows, grad_eg)
    grad_expert_up_partial = leading_contraction(received_rows, grad_expert_up_value)
    grad_rows = (
        contract_last(grad_eg, gate_expert) + contract_last(grad_expert_up_value, up_expert)
    ).astype(jnp.bfloat16)
    grad_back = lax.all_to_all(
        grad_rows.reshape(arrived.shape), "ctx", split_axis=0, concat_axis=0, tiled=True
    )
    grad_normed_two = grad_normed_two + jnp.sum(
        grad_back[flat, slot].astype(jnp.float32).reshape(rows, TOP, D), 1
    )
    expert_parts = (
        lax.psum_scatter(
            grad_egate[None].astype(jnp.bfloat16), "fsdp", scatter_dimension=1, tiled=True
        ).astype(jnp.float32),
        lax.psum_scatter(
            grad_expert_up_partial[None].astype(jnp.bfloat16),
            "fsdp",
            scatter_dimension=1,
            tiled=True,
        ).astype(jnp.float32),
        lax.psum_scatter(
            grad_edown[None].astype(jnp.bfloat16), "fsdp", scatter_dimension=1, tiled=True
        ).astype(jnp.float32),
    )
    grad_router_probs = jnp.sum(pick * grad_gates[:, :, None], 1)
    grad_logits = gate_pull(grad_router_probs)[0].astype(jnp.bfloat16)
    grad_normed_two = grad_normed_two + contract_last(grad_logits, router_full)
    grad_router = leading_contraction(normed_two, grad_logits)
    grad_residual_norm, grad_gain_second = norm_two_pull(grad_normed_two)
    grad_residual = grad_out + grad_residual_norm
    grad_attended = grad_residual.astype(jnp.bfloat16)
    grad_mixed = matmul(grad_attended, output_full).astype(jnp.bfloat16).reshape(rows, HEADS, VDIM)
    grad_output_w = leading_contraction(grad_attended, mixed)
    delta = jnp.transpose(jnp.sum(grad_mixed.astype(jnp.float32) * mixed_f, -1))

    def rotation_loop_step(step, carry):
        key_block, value_block, grad_key, grad_value, grad_query = carry
        start = (place - step) % devices * rows
        keyed = key_block.reshape(rows, HEADS, query_width)
        valued = value_block.reshape(rows, HEADS, VDIM)
        scores = (
            jnp.einsum("qhd,khd->hqk", query, keyed, preferred_element_type=jnp.float32) * scale
        )
        visible = visible_mask(start, rows)[None]
        weights = jnp.where(visible, jnp.exp(scores - logsum[:, :, None]), 0.0)
        weights_low = weights.astype(jnp.bfloat16)
        grad_weights = jnp.einsum(
            "qhd,khd->hqk", grad_mixed, valued, preferred_element_type=jnp.float32
        )
        grad_scores = (weights * (grad_weights - delta[:, :, None])).astype(jnp.bfloat16)
        grad_query = grad_query + scale * jnp.einsum(
            "hqk,khd->qhd", grad_scores, keyed, preferred_element_type=jnp.float32
        )
        grad_key = grad_key + scale * jnp.einsum(
            "hqk,qhd->khd", grad_scores, query, preferred_element_type=jnp.float32
        )
        grad_value = grad_value + jnp.einsum(
            "hqk,qhd->khd", weights_low, grad_mixed, preferred_element_type=jnp.float32
        )
        grad_key, grad_value = (
            shifted(grad_key.astype(jnp.bfloat16), "ctx", 1).astype(grad_key.dtype),
            shifted(grad_value.astype(jnp.bfloat16), "ctx", 1).astype(grad_value.dtype),
        )
        key_block, value_block = shifted((key_block, value_block), "ctx", 1)
        return (key_block, value_block, grad_key, grad_value, grad_query)

    cycle_start = (
        keys,
        values,
        jnp.zeros((rows, HEADS, query_width), jnp.float32),
        jnp.zeros((rows, HEADS, VDIM), jnp.float32),
        jnp.zeros((rows, HEADS, query_width), jnp.float32),
    )
    cycle_end = lax.fori_loop(0, devices, rotation_loop_step, cycle_start)
    grad_key = cycle_end[2]
    grad_value = cycle_end[3]
    grad_query = cycle_end[4]
    grad_key_rotary = jnp.sum(grad_key[..., NOPE:], 1)
    grad_expanded_latent = jnp.concatenate([grad_key[..., :NOPE], grad_value], -1)
    grad_expanded_latent = grad_expanded_latent.reshape(rows, HEADS * (NOPE + VDIM)).astype(
        jnp.bfloat16
    )
    grad_latent = contract_last(grad_expanded_latent, expand_full)
    grad_expand_w = leading_contraction(latent, grad_expanded_latent)
    grad_comp_latent, grad_gain_latent = latent_pull(grad_latent)
    grad_comp_rope = key_pull(grad_key_rotary)[0]
    grad_compressed = jnp.concatenate([grad_comp_latent, grad_comp_rope], -1).astype(jnp.bfloat16)
    grad_query_rope = query_pull(grad_query[..., NOPE:])[0]
    grad_query_raw = jnp.concatenate([grad_query[..., :NOPE], grad_query_rope], -1)
    grad_query_raw = grad_query_raw.reshape(rows, HEADS * query_width).astype(jnp.bfloat16)
    grad_normed = contract_last(grad_query_raw, query_full) + contract_last(
        grad_compressed, compress_full
    )
    grad_query_w = leading_contraction(normed, grad_query_raw)
    grad_compress_w = leading_contraction(normed, grad_compressed)
    grad_hidden_norm, grad_gain_first = norm_pull(grad_normed)
    grad_input = grad_residual + grad_hidden_norm
    dense_parts = (
        lax.psum_scatter(grad_gain_first, ("ctx", "fsdp"), scatter_dimension=0, tiled=True),
        lax.psum_scatter(grad_gain_latent, ("ctx", "fsdp"), scatter_dimension=0, tiled=True),
        lax.psum_scatter(grad_query_w, ("ctx", "fsdp"), scatter_dimension=0, tiled=True),
        lax.psum_scatter(grad_compress_w, ("ctx", "fsdp"), scatter_dimension=0, tiled=True),
        lax.psum_scatter(grad_expand_w, ("ctx", "fsdp"), scatter_dimension=0, tiled=True),
        lax.psum_scatter(grad_output_w, ("ctx", "fsdp"), scatter_dimension=0, tiled=True),
        lax.psum_scatter(grad_gain_second, ("ctx", "fsdp"), scatter_dimension=0, tiled=True),
        lax.psum_scatter(grad_router, ("ctx", "fsdp"), scatter_dimension=0, tiled=True),
        lax.psum_scatter(grad_sgate, ("ctx", "fsdp"), scatter_dimension=0, tiled=True),
        lax.psum_scatter(grad_sup, ("ctx", "fsdp"), scatter_dimension=0, tiled=True),
        lax.psum_scatter(grad_sdown, ("ctx", "fsdp"), scatter_dimension=0, tiled=True),
    )
    return (
        output[None],
        grad_input[None],
        dense_parts[0],
        dense_parts[1],
        dense_parts[2],
        dense_parts[3],
        dense_parts[4],
        dense_parts[5],
        dense_parts[6],
        dense_parts[7],
        dense_parts[8],
        dense_parts[9],
        dense_parts[10],
        expert_parts[0],
        expert_parts[1],
        expert_parts[2],
    )


def solution(mesh):
    token_spec = P("fsdp", "ctx", None)
    vector = P(("ctx", "fsdp"))
    matrix = P(("ctx", "fsdp"), None)
    expert = P("ctx", "fsdp", None)
    weights = (vector, vector, matrix, matrix, matrix, matrix, vector, matrix, matrix, matrix, matrix)
    weights = weights + (expert,) * 3
    return jax.shard_map(
        local if mesh.shape["ctx"] == HEADS else local_gathered,
        mesh=mesh,
        in_specs=(token_spec, token_spec, P("fsdp", None), P("fsdp", None), token_spec) + weights,
        out_specs=(token_spec, token_spec) + weights,
        check_vma=False,
    )
```

```python
import functools

import jax
import jax.numpy as jnp
from jax import lax
from jax.experimental import pallas as pl
from jax.experimental.pallas import tpu as pltpu
from jax.sharding import PartitionSpec as P

D = 2048
HEADS = 16
NOPE = 128
ROPE = 64
VDIM = 128
LATENT = 512
TOP = 6
EPS = 1e-06
NEGATIVE = -1e30
BF = jnp.bfloat16
F32 = jnp.float32


def matmul(left, right):
    return jnp.dot(left, right, preferred_element_type=F32)


def contract_last(left, right):
    return lax.dot_general(left, right, (((1,), (1,)), ((), ())), preferred_element_type=F32)


def leading_contraction(left, right):
    return lax.dot_general(left, right, (((0,), (0,)), ((), ())), preferred_element_type=F32)


def norm_scale(value):
    return lax.rsqrt(jnp.mean(value * value, -1, keepdims=True) + EPS)


def norm_back(value, scale, gain, grad):
    lifted = grad * gain
    return scale * lifted - value * (scale**3 * jnp.mean(lifted * value, -1, keepdims=True))


def turn(value, cosine, sine):
    half = value.shape[-1] // 2
    first, second = value[..., :half], value[..., half:]
    return jnp.concatenate([first * cosine - second * sine, first * sine + second * cosine], -1)


def swiglu_parts(gate, up):
    sigmoid = 1.0 / (1.0 + jnp.exp(-gate))
    act = gate * sigmoid
    return act, sigmoid * (1.0 + gate * (1.0 - sigmoid))


def box_of(count):
    dims = [2, 2]
    count //= 4
    while count > 1:
        side = 4 if count % 4 == 0 else 2
        dims.insert(0, side)
        count //= side
    return dims


class Box:
    def __init__(self):
        self.count = lax.axis_size("ctx")
        self.dims = box_of(self.count)
        self.strides = []
        stride = self.count
        for side in self.dims:
            stride //= side
            self.strides.append(stride)

    def shift(self, value, dim, by):
        side, stride = self.dims[dim], self.strides[dim]

        def target(i):
            here = i // stride % side
            return i + ((here + by) % side - here) * stride

        return lax.ppermute(value, "ctx", [(i, target(i)) for i in range(self.count)])

    def owners(self):
        me = lax.axis_index("ctx")
        owner = jnp.zeros((1,), jnp.int32)
        for side, stride in zip(self.dims, self.strides):
            here = me // stride % side
            offset = (here - jnp.arange(side, dtype=jnp.int32)) % side * stride
            owner = (offset[:, None] + owner[None, :]).reshape(-1)
        return owner

    def spread(self, held, dim):
        return [held] + [self.shift(held, dim, k) for k in range(1, self.dims[dim])]

    def gather(self, held):
        for dim in range(len(self.dims)):
            held = jnp.concatenate(self.spread(held, dim), 0)
        return held

    def share(self, held, dim):
        parts = jnp.split(held, self.dims[dim], 0)
        return parts[:1] + [self.shift(parts[k], dim, -k) for k in range(1, self.dims[dim])]


def joined(parts):
    return jnp.concatenate(parts, 0)


def summed(parts, dtype):
    total = parts[0].astype(F32)
    for part in parts[1:]:
        total = total + part.astype(F32)
    return total.astype(dtype)


MESH = pl.DeviceIdType.MESH
DMA = pltpu.SemaphoreType.DMA


def sides(count, both=False):
    found, stride, held = [], count, 1
    for side in box_of(count):
        stride //= side
        found.append(("ctx", side, stride, held))
        held *= side
    if both:
        found = [("fsdp", 2, 1, 1)] + [(axis, n, by, held * 2) for axis, n, by, held in found]
    return found


def moved(me, side, stride, by):
    here = me // stride % side
    return me + ((here + by) % side - here) * stride


def offset_of(count, me, owner):
    total = 0
    for _, side, stride, held in sides(count):
        total = total + (me // stride % side + side - owner // stride % side) % side * held
    return total


def remote(src, dst, send, recv, axis, target):
    return pltpu.make_async_remote_copy(
        src_ref=src,
        dst_ref=dst,
        send_sem=send,
        recv_sem=recv,
        device_id={axis: target},
        device_id_type=MESH,
    )


class Gather:
    def __init__(self, count, value, chunks):
        self.count, self.chunks = count, chunks
        self.taken, self.outs = 1, [jax.ShapeDtypeStruct((count,) + value.shape, value.dtype)]
        self.scratch = [DMA, DMA((count, chunks)), DMA((count, chunks))]
        self.space, self.out_space = pl.ANY, pl.ANY
        self.reach = "box"

    def bind(self, me, half, x_ref, out_ref, own_sem, send_sem, recv_sem):
        self.me, self.x, self.o = me, x_ref, out_ref
        self.sems = (send_sem, recv_sem)
        self.own = pltpu.make_async_copy(x_ref, out_ref.at[0], own_sem)
        self.sent = []
        self.dims = sides(self.count)

    def copy(self, block, chunk, dim, by):
        _, side, stride, held = self.dims[dim]
        step = self.x.shape[0] // self.chunks
        part = pl.ds(chunk * step, step)
        src = self.x.at[part] if block == 0 else self.o.at[block, part]
        to = by * held + block
        return remote(
            src,
            self.o.at[to, part],
            self.sems[0].at[to, chunk],
            self.sems[1].at[to, chunk],
            "ctx",
            moved(self.me, side, stride, by),
        )

    def forward(self, block, chunk, first):
        for dim in range(first, len(self.dims)):
            for by in range(1, self.dims[dim][1]):
                copy = self.copy(block, chunk, dim, by)
                copy.start()
                self.sent.append(copy)

    def start(self):
        self.own.start()
        for chunk in range(self.chunks):
            self.forward(0, chunk, 0)

    def arrive(self, chunk, dim):
        _, side, _, held = self.dims[dim]
        for by in range(1, side):
            for block in range(held):
                self.copy(block, chunk, dim, by).wait_recv()
                self.forward(by * held + block, chunk, dim + 1)

    def steps(self):
        found, last = [], len(self.dims)
        for wave in range(self.chunks + last - 1):
            for dim in range(last):
                if 0 <= wave - dim < self.chunks:
                    found.append(functools.partial(self.arrive, wave - dim, dim))
        return found

    def finish(self):
        for copy in self.sent:
            copy.wait_send()
        self.own.wait()


class GatherAll:
    def __init__(self, count, value):
        self.count = count
        self.taken, self.outs = 1, [jax.ShapeDtypeStruct((count, 2) + value.shape, value.dtype)]
        self.scratch = [DMA, DMA((count, 2)), DMA((count, 2))]
        self.space, self.out_space = pl.ANY, pl.ANY
        self.reach = "box+half"

    def bind(self, me, half, x_ref, out_ref, own_sem, send_sem, recv_sem):
        self.me, self.half, self.x, self.o = me, half, x_ref, out_ref
        self.sems = (send_sem, recv_sem)
        self.own = pltpu.make_async_copy(x_ref, out_ref.at[me, half], own_sem)
        self.sent = []
        self.dims = sides(self.count)

    def owner(self, block):
        owner = self.me
        for _, side, stride, held in self.dims:
            owner = moved(owner, side, stride, -(block // held % side))
        return owner

    def copy(self, block, other, dim, by):
        _, side, stride, held = self.dims[dim]
        owner = self.owner(block)
        half = 1 - self.half if other else self.half
        src = self.x if block == 0 and not other else self.o.at[owner, half]
        to = by * held + block
        return remote(
            src,
            self.o.at[owner, half],
            self.sems[0].at[to, other],
            self.sems[1].at[to, other],
            "ctx",
            moved(self.me, side, stride, by),
        )

    def arrived(self, block, other, dim, by):
        _, side, stride, held = self.dims[dim]
        to = by * held + block
        half = 1 - self.half if other else self.half
        here = self.o.at[self.owner(to), half]
        return remote(
            here, here, self.sems[0].at[to, other], self.sems[1].at[to, other], "ctx",
            moved(self.me, side, stride, by),
        )

    def across(self, half):
        return remote(
            self.x, self.o.at[self.me, half], self.sems[0].at[0, 0], self.sems[1].at[0, 0],
            "fsdp", 1 - self.half,
        )

    def forward(self, block, other, first):
        for dim in range(first, len(self.dims)):
            for by in range(1, self.dims[dim][1]):
                copy = self.copy(block, other, dim, by)
                copy.start()
                self.sent.append(copy)

    def start(self):
        self.own.start()
        self.cross = self.across(self.half)
        self.cross.start()
        self.forward(0, 0, 0)

    def meet(self):
        self.across(1 - self.half).wait_recv()
        self.forward(0, 1, 0)

    def arrive(self, dim):
        _, side, _, held = self.dims[dim]
        for other in range(2):
            for by in range(1, side):
                for block in range(held):
                    self.arrived(block, other, dim, by).wait_recv()
                    self.forward(by * held + block, other, dim + 1)

    def steps(self):
        return [self.meet] + [functools.partial(self.arrive, d) for d in range(len(self.dims))]

    def finish(self):
        for copy in self.sent:
            copy.wait_send()
        self.cross.wait_send()
        self.own.wait()


class Deal:
    def __init__(self, count, value, both=False, pick=None, place=None):
        self.count, self.both = count, both
        self.pick = pick or (lambda me, to: to)
        self.place = place or (lambda me, to: me)
        shape = value.shape[:1] + ((2,) if both else ()) + value.shape[1:]
        self.taken, self.outs = 1, [jax.ShapeDtypeStruct(shape, value.dtype)]
        self.scratch = [DMA, DMA((count, 2)), DMA((count, 2))]
        self.space, self.out_space = pl.ANY, pl.ANY
        self.reach = "all+half" if both else "all"

    def bind(self, me, half, x_ref, out_ref, own_sem, send_sem, recv_sem):
        self.me, self.half, self.x, self.o = me, half, x_ref, out_ref
        self.send, self.recv = send_sem, recv_sem
        self.sent = []
        self.own = pltpu.make_async_copy(
            x_ref.at[self.pick(me, me)], self.here(self.place(me, me), half), own_sem
        )

    def here(self, slot, half):
        return self.o.at[slot, half] if self.both else self.o.at[slot]

    def copy(self, by):
        to = (self.me + by) % self.count
        return remote(
            self.x.at[self.pick(self.me, to)],
            self.here(self.place(self.me, to), self.half),
            self.send.at[by, 0],
            self.recv.at[by, 0],
            "ctx",
            to,
        )

    def arrived(self, by):
        source = (self.me + self.count - by) % self.count
        slot = self.here(self.place(source, self.me), self.half)
        return remote(
            slot, slot, self.send.at[by, 0], self.recv.at[by, 0], "ctx", (self.me + by) % self.count
        )

    def across(self, by, half):
        source = (self.me + self.count - by) % self.count
        slot = self.here(self.place(source, self.me), half)
        src = self.x.at[self.pick(self.me, self.me)] if by == 0 else slot
        return remote(
            src, slot, self.send.at[by, 1], self.recv.at[by, 1], "fsdp", 1 - self.half
        )

    def start(self):
        self.own.start()
        for by in range(1, self.count):
            copy = self.copy(by)
            copy.start()
            self.sent.append(copy)
        if self.both:
            self.pass_on(0)

    def pass_on(self, by):
        copy = self.across(by, self.half)
        copy.start()
        self.sent.append(copy)

    def arrive(self, by):
        self.arrived(by).wait_recv()
        if self.both:
            self.pass_on(by)

    def rest(self):
        for by in range(self.count):
            self.across(by, 1 - self.half).wait_recv()

    def steps(self):
        return [functools.partial(self.arrive, by) for by in range(1, self.count)]

    def finish(self):
        if self.both:
            self.rest()
        for copy in self.sent:
            copy.wait_send()
        self.own.wait()


class DealSum:
    def __init__(self, count, value):
        self.count = count
        shape = value.shape[:1] + value.shape[2:]
        self.taken, self.outs = 1, [jax.ShapeDtypeStruct(shape, value.dtype)]
        self.scratch = [pltpu.VMEM(shape, value.dtype), pltpu.VMEM(shape, value.dtype)]
        self.scratch += [DMA, DMA((count, 2)), DMA((count, 2))]
        self.space, self.out_space = pltpu.VMEM, pl.ANY
        self.reach = "all+half"

    def bind(self, me, half, x_ref, out_ref, landed, total, own_sem, send_sem, recv_sem):
        self.me, self.half, self.x, self.o = me, half, x_ref, out_ref
        self.landed, self.total = landed, total
        self.send, self.recv = send_sem, recv_sem
        self.own = pltpu.make_async_copy(total.at[me], out_ref.at[me], own_sem)
        self.sent = []

    def cross(self, part):
        return remote(
            self.x.at[part, 1 - self.half], self.landed.at[part], self.send.at[part, 1],
            self.recv.at[part, 1], "fsdp", 1 - self.half,
        )

    def copy(self, by):
        to = (self.me + by) % self.count
        return remote(
            self.total.at[to], self.o.at[self.me], self.send.at[by, 0], self.recv.at[by, 0],
            "ctx", to,
        )

    def start(self):
        for part in range(self.count):
            copy = self.cross(part)
            copy.start()
            self.sent.append(copy)

    def add(self):
        for part in range(self.count):
            self.cross(part).wait_recv()
            mine = self.x[part, self.half].astype(F32) + self.landed[part].astype(F32)
            self.total[part] = mine.astype(self.total.dtype)
        self.own.start()
        for by in range(1, self.count):
            copy = self.copy(by)
            copy.start()
            self.sent.append(copy)

    def steps(self):
        return [self.add]

    def finish(self):
        for by in range(1, self.count):
            source = (self.me + self.count - by) % self.count
            slot = self.o.at[source]
            remote(
                slot, slot, self.send.at[by, 0], self.recv.at[by, 0], "ctx",
                (self.me + by) % self.count,
            ).wait_recv()
        for copy in self.sent:
            copy.wait_send()
        self.own.wait()


class Scatter:
    def __init__(self, count, value, chunks, both=False):
        self.count, self.chunks, self.both = count, chunks, both
        tail = value.shape[2:] if both else value.shape[1:]
        self.taken, self.outs = 1, [jax.ShapeDtypeStruct(tail, F32)]
        dims = sides(count, both)
        blocks = count * 2 if both else count
        self.scratch = [
            pltpu.VMEM(((side - 1) * held,) + tail, value.dtype) for _, side, _, held in dims
        ]
        self.scratch += [pltpu.VMEM((held,) + tail, value.dtype) for _, _, _, held in dims[1:]]
        self.scratch += [DMA((blocks, chunks)), DMA((blocks, chunks))]
        self.space, self.out_space = pltpu.VMEM, pltpu.VMEM
        self.reach = "box+half" if both else "box"

    def bind(self, me, half, x_ref, out_ref, *scratch):
        self.me, self.half, self.o = me, half, out_ref
        self.blocks = self.count * 2 if self.both else self.count
        self.dims = sides(self.count, self.both)
        levels = len(self.dims)
        self.landed = scratch[:levels]
        self.held = scratch[levels : 2 * levels - 1] + (x_ref,)
        self.send, self.recv = scratch[2 * levels - 1 :]
        self.sent = []

    def part(self, chunk):
        step = self.o.shape[0] // self.chunks
        return pl.ds(chunk * step, step)

    def copy(self, dim, block, chunk):
        axis, side, stride, held = self.dims[dim]
        part = self.part(chunk)
        here = self.me if axis == "ctx" else self.half
        return remote(
            self.held[dim].at[self.at(dim, block) + (part,)],
            self.landed[dim].at[block - held, part],
            self.send.at[block, chunk],
            self.recv.at[block, chunk],
            axis,
            moved(here, side, stride, -(block // held)),
        )

    def at(self, dim, block):
        if not self.both or dim < len(self.dims) - 1:
            return (block,)
        owner = self.me
        for _, side, stride, held in self.dims[1:]:
            owner = moved(owner, side, stride, -(block // held % side))
        return (owner, self.half if block % 2 == 0 else 1 - self.half)

    def ready(self, dim, block, chunk):
        if block >= self.dims[dim][3]:
            copy = self.copy(dim, block, chunk)
            copy.start()
            self.sent.append(copy)

    def add(self, dim, chunk):
        _, side, _, held = self.dims[dim]
        part = self.part(chunk)
        for block in reversed(range(held)):
            total = self.held[dim][self.at(dim, block) + (part,)].astype(F32)
            for by in range(1, side):
                self.copy(dim, by * held + block, chunk).wait_recv()
                total = total + self.landed[dim][(by - 1) * held + block, part].astype(F32)
            if dim == 0:
                self.o[part] = total
            else:
                self.held[dim - 1][block, part] = total.astype(self.held[dim - 1].dtype)
                self.ready(dim - 1, block, chunk)

    def start(self):
        last = len(self.dims) - 1
        for chunk in range(self.chunks):
            for block in reversed(range(self.dims[last][3], self.blocks)):
                self.ready(last, block, chunk)

    def steps(self):
        found, levels = [], len(self.dims)
        for wave in range(self.chunks + levels - 1):
            for dim in reversed(range(levels)):
                chunk = wave - (levels - 1 - dim)
                if 0 <= chunk < self.chunks:
                    found.append(functools.partial(self.add, dim, chunk))
        return found

    def finish(self):
        for copy in self.sent:
            copy.wait_send()


class Products:
    def __init__(self, values, pairs):
        self.values, self.pairs = values, pairs
        self.taken = len(values)
        self.outs = [
            jax.ShapeDtypeStruct((values[a].shape[1], values[b].shape[1]), BF) for a, b in pairs
        ]
        widest = max(out.shape[1] for out in self.outs)
        self.scratch = [pltpu.VMEM(v.shape, v.dtype) for v in values]
        self.scratch += [pltpu.VMEM((2, TILE, widest), BF), DMA((len(values),)), DMA((2,))]
        self.space, self.out_space = pl.ANY, pl.ANY
        self.reach = ""

    def bind(self, me, half, *refs):
        n, m = len(self.values), len(self.pairs)
        self.held = refs[n + m : n + m + n]
        self.tile, self.in_sem, self.out_sem = refs[n + m + n :]
        self.o = refs[n : n + m]
        self.loads = [
            pltpu.make_async_copy(refs[i], self.held[i], self.in_sem.at[i]) for i in range(n)
        ]
        self.stores = []
        self.loaded = set()

    def start(self):
        for load in self.loads:
            load.start()

    def step(self, pair, row):
        for i in self.pairs[pair]:
            if i not in self.loaded:
                self.loads[i].wait()
                self.loaded.add(i)
        left, right = (self.held[i] for i in self.pairs[pair])
        slot = len(self.stores) % 2
        if len(self.stores) >= 2:
            self.stores[-2].wait()
        part = pl.ds(row * TILE, TILE)
        out = self.o[pair]
        place = self.tile.at[slot, :, pl.ds(0, out.shape[1])]
        place[...] = leading_contraction(left[:, part], right[...]).astype(BF)
        store = pltpu.make_async_copy(place, out.at[part], self.out_sem.at[slot])
        store.start()
        self.stores.append(store)

    def steps(self):
        return [
            functools.partial(self.step, pair, row)
            for pair in range(len(self.pairs))
            for row in range(self.outs[pair].shape[0] // TILE)
        ]

    def finish(self):
        for store in self.stores[-2:]:
            store.wait()


def exchange_kernel(count, plans, spans, needed, carried, *refs):
    me, half = lax.axis_index("ctx"), lax.axis_index("fsdp")
    taken = sum(plan.taken for plan in plans)
    ins, refs = refs[:taken], refs[taken + needed + carried :]
    given = sum(len(plan.outs) for plan in plans)
    outs, refs = refs[:given], refs[given + carried :]
    barrier = pltpu.get_barrier_semaphore()
    peers = []
    if any("all" in plan.reach for plan in plans):
        peers = [("ctx", (me + by) % count) for by in range(1, count)]
    else:
        for _, side, stride, _ in sides(count):
            peers += [("ctx", moved(me, side, stride, by)) for by in range(1, side)]
    if any("half" in plan.reach for plan in plans):
        peers.append(("fsdp", 1 - half))
    for axis, target in peers:
        pl.semaphore_signal(barrier, inc=1, device_id={axis: target}, device_id_type=MESH)
    pl.semaphore_wait(barrier, len(peers))
    for plan in plans:
        mine, refs = refs[: len(plan.scratch)], refs[len(plan.scratch) :]
        plan.bind(me, half, *ins[: plan.taken], *outs[: len(plan.outs)], *mine)
        ins, outs = ins[plan.taken :], outs[len(plan.outs) :]
        plan.start()
    timed = []
    for plan, (first, last) in zip(plans, spans):
        steps = plan.steps()
        for i, step in enumerate(steps):
            timed.append((first + (last - first) * (i + 1) / len(steps), step))
    for _, step in sorted(timed, key=lambda entry: entry[0]):
        step()
    for plan in plans:
        plan.finish()


def exchange(count, collective, values, plans, spans=None, needs=(), carry=()):
    spans = spans or [(0.0, 1.0)] * len(plans)
    scratch = [ref for plan in plans for ref in plan.scratch]
    values = [v for value in values for v in (value if isinstance(value, list) else [value])]
    outs = [out for plan in plans for out in plan.outs]
    first = len(values) + len(needs)
    spot = pl.BlockSpec(memory_space=pl.ANY)
    in_specs = [pl.BlockSpec(memory_space=p.space) for p in plans for _ in range(p.taken)]
    out_specs = [pl.BlockSpec(memory_space=p.out_space) for p in plans for _ in p.outs]
    return pl.pallas_call(
        functools.partial(exchange_kernel, count, plans, spans, len(needs), len(carry)),
        out_shape=tuple(outs) + tuple(jax.ShapeDtypeStruct(v.shape, v.dtype) for v in carry),
        in_specs=in_specs + [spot] * (len(needs) + len(carry)),
        out_specs=tuple(out_specs + [spot] * len(carry)),
        input_output_aliases={first + i: len(outs) + i for i in range(len(carry))},
        scratch_shapes=scratch,
        compiler_params=pltpu.CompilerParams(
            collective_id=collective, has_side_effects=True, vmem_limit_bytes=60 << 20
        ),
        cost_estimate=pl.CostEstimate(flops=0, bytes_accessed=100 << 20, transcendentals=0),
    )(*values, *needs, *carry)


TILE = 256


def hot_rows(slots, first):
    count = slots.shape[1]
    return (lax.broadcasted_iota(jnp.int32, (TILE, count), 0) + first == slots).astype(BF)


def hot_cols(slots, first):
    count = slots.shape[0]
    return (lax.broadcasted_iota(jnp.int32, (count, TILE), 1) + first == slots).astype(BF)


def meets(starts, tokens, slots):
    return (starts[tokens] < (slots + 1) * TILE) & (starts[tokens + 1] > slots * TILE)


def split_of(info, width):
    own = pl.multiple_of(info * (width // 2), 128)
    other = pl.multiple_of((1 - info) * (width // 2), 128)
    return pl.ds(own, width // 2), pl.ds(other, width // 2)


def pick_rows(starts, slot_ref, source_ref, total_ref, tile):
    total_ref[...] = jnp.zeros_like(total_ref)
    for j in range(source_ref.shape[0] // TILE):

        @pl.when(meets(starts, j, tile))
        def _():
            part = pl.ds(j * TILE, TILE)
            total_ref[...] += matmul(hot_rows(slot_ref[:, part], tile * TILE), source_ref[part])


def expert_in_kernel(info, starts, slot, two, g0, u0, rows, gate, up, hidden, total):
    pick_rows(starts, slot, two, total, pl.program_id(0))
    rows[...] = total[...].astype(BF)
    gate[...] = matmul(rows[...], g0[...])
    up[...] = matmul(rows[...], u0[...])
    value = gate[...]
    hidden[...] = (value / (1.0 + jnp.exp(-value)) * up[...]).astype(BF)


def expert_out_kernel(
    info, starts, hidden, d0, d1, slot, weight, shared, sdown, produced, out, held, total
):
    step, tiles = pl.program_id(0), held.shape[0] // TILE

    @pl.when(step < tiles)
    def _():
        own, other = split_of(info[0], held.shape[1])
        produced[:, own] = contract_last(hidden[...], d0[...]).astype(BF)
        produced[:, other] = contract_last(hidden[...], d1[...]).astype(BF)
        held[pl.ds(pl.multiple_of(step * TILE, TILE), TILE)] = produced[...]

    @pl.when(step >= tiles)
    def _():
        token = step - tiles
        total[...] = jnp.zeros_like(total)
        for i in range(tiles):

            @pl.when(meets(starts, token, i))
            def _():
                total[...] += matmul(hot_cols(slot[...], i * TILE), held[pl.ds(i * TILE, TILE)])

        out[...] = (weight[...] * total[...] + contract_last(shared[...], sdown[...])).astype(BF)


def expert_back_kernel(
    info, starts, slot, weight, cot, produced, gate, up, g0, u0, d0, d1,
    grad_in, grad_gate, grad_up, grad_rows, dots, total,
):
    tile = pl.program_id(0)
    total[...] = jnp.zeros_like(total)
    dots[...] = jnp.zeros_like(dots)
    for j in range(cot.shape[0] // TILE):

        @pl.when(meets(starts, j, tile))
        def _():
            part = pl.ds(j * TILE, TILE)
            hot = hot_rows(slot[:, part], tile * TILE)
            total[...] += matmul(hot, cot[part])
            dots[...] += jnp.sum(hot.astype(F32) * weight[:, part], 1, keepdims=True)

    grad_in[...] = (dots[...] * total[...]).astype(BF)
    dots[...] = jnp.sum(total[...] * produced[...].astype(F32), 1, keepdims=True)
    own, other = split_of(info[0], grad_in.shape[1])
    grad_hidden = matmul(grad_in[:, own], d0[...]) + matmul(grad_in[:, other], d1[...])
    act, slope = swiglu_parts(gate[...], up[...])
    grad_gate[...] = (grad_hidden * up[...] * slope).astype(BF)
    grad_up[...] = (grad_hidden * act).astype(BF)
    back = contract_last(grad_gate[...], g0[...]) + contract_last(grad_up[...], u0[...])
    grad_rows[...] = back.astype(BF)


def shared_in_kernel(two, sgate, sup, gate, up, hidden):
    gate[...] = matmul(two[...], sgate[...])
    up[...] = matmul(two[...], sup[...])
    value = gate[...]
    hidden[...] = (value / (1.0 + jnp.exp(-value)) * up[...]).astype(BF)


def tokens_back_kernel(
    info, starts, slot, dots, grad_rows, cot, gate, up, sgate, sup, sdown,
    out, grad_gate, grad_up, gates, total,
):
    token = pl.program_id(0)
    grad_hidden = matmul(cot[...], sdown[...])
    act, slope = swiglu_parts(gate[...], up[...])
    grad_gate[...] = (grad_hidden * up[...] * slope).astype(BF)
    grad_up[...] = (grad_hidden * act).astype(BF)
    total[...] = contract_last(grad_gate[...], sgate[...]) + contract_last(grad_up[...], sup[...])
    gates[...] = jnp.zeros_like(gates)
    mine = lax.broadcasted_iota(jnp.int32, gates.shape, 1) == info[1]
    for i in range(grad_rows.shape[0] // TILE):

        @pl.when(meets(starts, token, i))
        def _():
            part = pl.ds(i * TILE, TILE)
            hot = hot_cols(slot[...], i * TILE)
            total[...] += matmul(hot, grad_rows[part])
            found = jnp.sum(hot.astype(F32) * dots[:, part], 1, keepdims=True)
            gates[...] += jnp.where(mine, found, 0.0)

    out[...] = total[...].astype(BF)


def whole(value):
    return pl.BlockSpec(value.shape, lambda *_: (0,) * value.ndim, pipeline_mode=pl.Buffered(1))


def tiled(value, index=lambda step: step):
    return pl.BlockSpec((TILE,) + value.shape[1:], lambda step, *_: (index(step), 0))


def run(kernel, steps, scalars, values, specs, outs, out_specs, scratch, flops, needs=(), carry=()):
    moved_bytes = sum(v.size * v.dtype.itemsize for v in list(values) + list(outs))
    first = len(scalars) + len(values)
    fenced = first + len(needs) + len(carry)

    def body(*refs):
        made = refs[fenced : fenced + len(outs)]
        kernel(*refs[:first], *made, *refs[fenced + len(outs) + len(carry) :])

    spot = pl.BlockSpec(memory_space=pl.ANY)
    specs = list(specs) + [spot] * (len(needs) + len(carry))
    out_specs = tuple(out_specs) + (spot,) * len(carry)
    handed = tuple(jax.ShapeDtypeStruct(v.shape, v.dtype) for v in carry)
    return pl.pallas_call(
        body,
        grid_spec=pltpu.PrefetchScalarGridSpec(
            num_scalar_prefetch=len(scalars),
            grid=(steps,),
            in_specs=specs,
            out_specs=out_specs,
            scratch_shapes=scratch,
        ),
        out_shape=tuple(outs) + handed,
        input_output_aliases={first + len(needs) + i: len(outs) + i for i in range(len(carry))},
        compiler_params=pltpu.CompilerParams(vmem_limit_bytes=60 << 20),
        cost_estimate=pl.CostEstimate(flops=flops, bytes_accessed=moved_bytes, transcendentals=0),
    )(*scalars, *values, *needs, *carry)


def like(rows, columns, dtype):
    return jax.ShapeDtypeStruct((rows, columns), dtype)


def expert_in(info, starts, slot_row, two, gates, ups, carry):
    capacity, width, hidden = slot_row[1], two.shape[1], gates.shape[1]
    slot_row = slot_row[0]
    outs = (
        like(capacity, width, BF),
        like(capacity, hidden, F32),
        like(capacity, hidden, F32),
        like(capacity, hidden, BF),
    )
    values = [slot_row, two, gates, ups]
    return run(
        expert_in_kernel, capacity // TILE, (info, starts), values, [whole(v) for v in values],
        outs, tuple(tiled(o) for o in outs), [pltpu.VMEM((TILE, width), F32)],
        capacity * width * hidden * 4,
        carry=carry,
    )


def expert_out(info, starts, hidden, downs, slot_col, weight_col, shared, sdown, needs):
    capacity, tokens, width = hidden.shape[0], slot_col.shape[0], sdown.shape[0]
    first = capacity // TILE
    outs = (like(capacity, width, BF), like(tokens, width, BF))
    rows_at = lambda step: jnp.minimum(step, first - 1)
    tokens_at = lambda step: jnp.maximum(step - first, 0)
    values = [hidden, *downs, slot_col, weight_col, shared, sdown]
    specs = [tiled(hidden, rows_at), whole(downs[0]), whole(downs[1])]
    specs += [tiled(slot_col, tokens_at), tiled(weight_col, tokens_at), tiled(shared, tokens_at)]
    specs += [whole(sdown)]
    return run(
        expert_out_kernel, first + tokens // TILE, (info, starts), values, specs, outs,
        (tiled(outs[0], rows_at), tiled(outs[1], tokens_at)),
        [pltpu.VMEM((capacity, width), BF), pltpu.VMEM((TILE, width), F32)],
        capacity * width * hidden.shape[1] * 3,
        needs,
    )


def expert_back(
    info, starts, slot_row, weight_row, cot, produced, gate, up, gates, ups, downs, needs
):
    capacity, hidden = gate.shape
    width = cot.shape[1]
    outs = (
        like(capacity, width, BF),
        like(capacity, hidden, BF),
        like(capacity, hidden, BF),
        like(capacity, width, BF),
        like(capacity, 1, F32),
    )
    values = [slot_row, weight_row, cot, produced, gate, up, gates, ups, *downs]
    specs = [whole(v) for v in values]
    specs[3:6] = [tiled(produced), tiled(gate), tiled(up)]
    return run(
        expert_back_kernel, capacity // TILE, (info, starts), values, specs, outs,
        tuple(tiled(o) for o in outs), [pltpu.VMEM((TILE, width), F32)],
        capacity * width * hidden * 6,
        needs,
    )


def shared_in(two, sgate, sup):
    tokens, hidden = two.shape[0], sgate.shape[1]
    outs = (like(tokens, hidden, F32), like(tokens, hidden, F32), like(tokens, hidden, BF))
    return run(
        shared_in_kernel, tokens // TILE, (), [two, sgate, sup],
        [tiled(two), whole(sgate), whole(sup)], outs, tuple(tiled(o) for o in outs), [],
        tokens * two.shape[1] * hidden * 4,
    )


def tokens_back(info, starts, slot_col, dots_row, grad_rows, cot, gate, up, sgate, sup, sdown, experts):
    tokens, width = cot.shape
    hidden = gate.shape[1]
    outs = (
        like(tokens, width, BF),
        like(tokens, hidden, BF),
        like(tokens, hidden, BF),
        like(tokens, experts, F32),
    )
    values = [slot_col, dots_row, grad_rows, cot, gate, up, sgate, sup, sdown]
    specs = [whole(v) for v in values]
    specs[0] = tiled(slot_col)
    specs[3:6] = [tiled(cot), tiled(gate), tiled(up)]
    return run(
        tokens_back_kernel, tokens // TILE, (info, starts), values, specs, outs,
        tuple(tiled(o) for o in outs), [pltpu.VMEM((TILE, width), F32)],
        tokens * width * hidden * 8,
    )


def columns_kernel(rest, query, expand, d_query, d_output, d_gate, d_up, d_down, d_expand):
    parts = rest.shape[0]
    fs = d_gate.shape[1] // parts
    for part in range(parts):
        for i, out in enumerate((d_gate, d_up, d_down)):
            block = rest[part, :, i * fs : (i + 1) * fs]
            out[:, part * fs : (part + 1) * fs] = block.astype(F32)
        width = NOPE + ROPE
        d_query[:, part * width : (part + 1) * width] = query[part, :, :width].astype(F32)
        block = query[part, :, width : width + VDIM]
        d_output[:, part * VDIM : (part + 1) * VDIM] = block.astype(F32)
        width = NOPE + VDIM
        d_expand[:, part * width : (part + 1) * width] = expand[part].astype(F32)


def columns_of(rest, query, expand, fs):
    count, shard = query.shape[:2]
    outs = (
        like(shard, count * (NOPE + ROPE), F32),
        like(shard, count * VDIM, F32),
        like(shard, count * fs, F32),
        like(shard, count * fs, F32),
        like(shard, count * fs, F32),
        like(expand.shape[1], count * (NOPE + VDIM), F32),
    )
    values = [rest, query, expand]
    specs = [whole(v) for v in values]
    return run(
        columns_kernel, 1, (), values, specs, outs, tuple(whole(o) for o in outs), [], 0
    )


def turned(value, cosine, sine):
    half = value.shape[1] // 2
    return value * cosine + jnp.concatenate([value[:, half:], value[:, :half]], 1) * sine


def before_kernel(
    token, gain, gain_latent, wq, wc, we, cosine, sine, normed, query, keys, values, latent, low
):
    hidden = token[...].astype(F32)
    normed[...] = (hidden * norm_scale(hidden) * gain[...]).astype(BF)
    raw = matmul(normed[...], wq[...])
    query[:, :NOPE] = raw[:, :NOPE].astype(BF)
    query[:, NOPE:] = turned(raw[:, NOPE:], cosine[...], sine[...]).astype(BF)
    compressed = matmul(normed[...], wc[...])
    low[...] = compressed[:, :LATENT]
    part = low[...]
    latent[...] = (part * norm_scale(part) * gain_latent[...]).astype(BF)
    expanded = matmul(latent[...], we[...])
    keys[:, :NOPE] = expanded[:, :NOPE].astype(BF)
    rope = compressed[:, LATENT : LATENT + ROPE]
    keys[:, NOPE:] = turned(rope, cosine[...], sine[...]).astype(BF)
    values[...] = expanded[:, NOPE:].astype(BF)


def before_attention(token, gain, gain_latent, wq, wc, we, cosine, sine):
    tokens, width = token.shape
    outs = (
        like(tokens, width, BF),
        like(tokens, NOPE + ROPE, BF),
        like(tokens, NOPE + ROPE, BF),
        like(tokens, VDIM, BF),
        like(tokens, LATENT, BF),
        like(tokens, LATENT, F32),
    )
    values = [token, gain, gain_latent, wq, wc, we, cosine, sine]
    specs = [whole(v) for v in values]
    specs[0], specs[6], specs[7] = tiled(token), tiled(cosine), tiled(sine)
    return run(
        before_kernel, tokens // TILE, (), values, specs, outs, tuple(tiled(o) for o in outs), [],
        tokens * width * 2000,
    )


def behind_kernel(
    gq, gk, gv, normed, latent, low, gain_latent, latent_col, gain_col, wq, wc, we, cosine, sine,
    extra, out, d_query, d_small, d_expand, d_latent, sum_q, sum_c, sum_e,
):
    step = pl.program_id(0)

    @pl.when(step == 0)
    def _():
        sum_q[...] = jnp.zeros_like(sum_q)
        sum_c[...] = jnp.zeros_like(sum_c)
        sum_e[...] = jnp.zeros_like(sum_e)

    scale = (NOPE + ROPE) ** (-0.5)
    query, keys = gq[...] * scale, gk[...] * scale
    back = -sine[...]
    grad_q = jnp.concatenate(
        [query[:, :NOPE], turned(query[:, NOPE:], cosine[...], back)], 1
    ).astype(BF)
    grad_e = jnp.concatenate([keys[:, :NOPE], gv[...]], 1).astype(BF)
    grad_latent = contract_last(grad_e, we[...])
    part = low[...]
    grad_low = norm_back(part, norm_scale(part), gain_latent[...], grad_latent)
    rope = turned(keys[:, NOPE:], cosine[...], back)
    fill = jnp.zeros((rope.shape[0], wc.shape[1] - LATENT - ROPE), F32)
    grad_c = jnp.concatenate([grad_low, rope, fill], 1).astype(BF)
    out[...] = (contract_last(grad_q, wq[...]) + contract_last(grad_c, wc[...])).astype(BF)
    sum_q[...] += leading_contraction(normed[...], grad_q)
    sum_c[...] += leading_contraction(normed[...], grad_c)
    sum_e[...] += leading_contraction(latent[...], grad_e)

    @pl.when(step == pl.num_programs(0) - 1)
    def _():
        first = jnp.sum(sum_q[...] * wq[...].astype(F32), 1, keepdims=True)
        first = first + jnp.sum(sum_c[...] * wc[...].astype(F32), 1, keepdims=True)
        d_query[...] = sum_q[...].astype(BF)
        edge = LATENT + ROPE
        lanes = lax.broadcasted_iota(jnp.int32, extra.shape, 1)
        more = extra[...] + jnp.where(lanes == 0, first / gain_col[...], 0.0)
        d_small[:, :edge] = sum_c[:, :edge].astype(BF)
        d_small[:, edge:] = more.astype(BF)
        d_expand[...] = sum_e[...].astype(BF)
        second = jnp.sum(sum_e[...] * we[...].astype(F32), 1, keepdims=True) / latent_col[...]
        d_latent[...] = second


def behind_attention(
    gq, gk, gv, normed, latent, low, gain_latent, gain_col, wq, wc, we, cosine, sine, extra, needs
):
    tokens, width = normed.shape
    outs = (
        like(tokens, width, BF),
        like(width, wq.shape[1], BF),
        like(width, wc.shape[1], BF),
        like(LATENT, we.shape[1], BF),
        like(LATENT, 1, F32),
    )
    values = [gq, gk, gv, normed, latent, low]
    values += [gain_latent, gain_latent.reshape(-1, 1), gain_col, wq, wc, we, cosine, sine, extra]
    specs = [tiled(v) for v in values[:6]] + [whole(v) for v in values[6:]]
    specs[12], specs[13] = tiled(cosine), tiled(sine)
    return run(
        behind_kernel, tokens // TILE, (), values, specs, outs,
        (tiled(outs[0]),) + tuple(whole(o) for o in outs[1:]),
        [
            pltpu.VMEM((width, wq.shape[1]), F32),
            pltpu.VMEM((width, wc.shape[1]), F32),
            pltpu.VMEM((LATENT, we.shape[1]), F32),
        ],
        tokens * width * 4000,
        needs,
    )


def placement(lengths_row, order_row):
    ends = jnp.cumsum(lengths_row)
    starts = ends - lengths_row
    sequence = jnp.sum((order_row[:, None] >= ends[None, :]).astype(jnp.int32), 1)
    chosen = sequence[:, None] == jnp.arange(lengths_row.shape[0], dtype=jnp.int32)[None, :]
    offset = jnp.sum(jnp.where(chosen, starts[None, :], 0), 1)
    return (sequence, order_row - offset)


def spread(weight, count, repeat):
    rows = weight.shape[0]
    parts = jnp.transpose(weight.astype(BF).reshape(rows, count // repeat, -1), (1, 0, 2))
    return jnp.repeat(parts, repeat, 0) if repeat > 1 else parts


def pad_last(value, width):
    return jnp.pad(value, [(0, 0)] * (value.ndim - 1) + [(0, width - value.shape[-1])])


def up_to(width, unit=128):
    return -(-width // unit) * unit


def local(
    tokens,
    cotangent,
    lengths,
    token_order,
    routes,
    first_gain,
    latent_gain,
    query_weight,
    compress_weight,
    expand_weight,
    output_weight,
    second_gain,
    router_weight,
    shared_gate,
    shared_up,
    shared_down,
    expert_gate,
    expert_up,
    expert_down,
):
    box = Box()
    count = box.count
    repeat = max(1, count // HEADS)
    rows = tokens.shape[1]
    group = rows * count
    asked = group // repeat
    experts = router_weight.shape[1]
    shard = query_weight.shape[0]
    width = NOPE + ROPE
    me = lax.axis_index("ctx")
    both = ("ctx", "fsdp")
    all_devices = count * lax.axis_size("fsdp")

    half = lax.axis_index("fsdp")

    def reduce_blocks(collective, value, more, needs=(), carry=()):
        plans = [Scatter(count, value, 4)] + [plan for _, plan, _ in more]
        spans = [(0.0, 1.0)] + [span for _, _, span in more]
        values = [value] + [v for v, _, _ in more]
        return exchange(count, collective, values, plans, spans, needs, carry)

    def across(value):
        return lax.ppermute(value, "fsdp", [(0, 1), (1, 0)])

    def halves_sent(parts):
        own = lax.dynamic_index_in_dim(parts, half, 1, keepdims=False)
        other = lax.dynamic_index_in_dim(parts, 1 - half, 1, keepdims=False)
        return own, across(other.astype(BF))

    owners = box.owners()

    small_cols = compress_weight.shape[1] + experts + 3
    lat_rows = latent_gain.shape[0]
    small = jnp.concatenate(
        [
            compress_weight,
            first_gain[:, None],
            second_gain[:, None],
            router_weight,
            jnp.pad(latent_gain, (0, shard - lat_rows))[:, None],
        ],
        1,
    ).astype(BF)
    small = pad_last(small, up_to(small_cols))
    query_parts = spread(query_weight, count, repeat)
    expand_parts = spread(expand_weight, count, repeat)
    small_all = lax.all_gather(small, both, axis=0, tiled=True)
    gates = lax.all_gather(expert_gate[0].astype(BF), "fsdp", axis=0, tiled=True)
    query_own, expand_own, token_all, cot_low = exchange(
        count,
        0,
        [query_parts, expand_parts, tokens[0]],
        [
            Deal(count, query_parts, both=True),
            Deal(count, expand_parts, both=True),
            Gather(count, tokens[0], 4),
        ],
        spans=[(-2, -1), (-1, 0), (0, 1)],
        carry=[cotangent[0].astype(BF)],
    )
    token_all = token_all.reshape(group, D)
    query_own = query_own.reshape(D, -1)
    expand_own = expand_own.reshape(LATENT, -1)
    edge = compress_weight.shape[1]
    compress_full = small_all[:, :edge]
    router_full = small_all[:, edge + 2 : edge + 2 + experts]
    gain_first = small_all[:, edge].astype(F32)
    gain_second = small_all[:, edge + 1].astype(F32)
    gain_latent = small_all[:, edge + experts + 2].reshape(all_devices, shard)[:, :lat_rows]
    gain_latent = gain_latent.reshape(-1).astype(F32)

    output_cast = output_weight
    output_full = lax.all_gather(output_cast.astype(BF), both, axis=0, tiled=True)
    route_own, gate_cols, up_cols, down_cols = routes[0], shared_gate, shared_up, shared_down
    fs = shared_gate.shape[1] // count
    fp = up_to(fs)
    rest = jnp.concatenate(
        [spread(gate_cols, count, 1), spread(up_cols, count, 1), spread(down_cols, count, 1)], -1
    )
    rest = pad_last(rest, up_to(3 * fs))
    cot_parts = box.spread(cot_low, 0)

    order_all = jnp.take(token_order[0].reshape(count, rows), owners, axis=0).reshape(-1)
    sequence, position = placement(lengths[0], order_all)
    turns = ROPE // 2
    freq = 10000.0 ** (-jnp.arange(turns, dtype=F32) / turns)
    angle = position.astype(F32)[:, None] * freq[None, :]
    cosine = jnp.tile(jnp.cos(angle), (1, 2))
    sine = jnp.sin(angle)
    sine = jnp.concatenate([-sine, sine], 1)

    normed_all, query, keys, values, latent, low_part = before_attention(
        token_all, gain_first[None, :], gain_latent[None, :], query_own, small_all, expand_own,
        cosine, sine,
    )
    up_cast, down_cast = expert_up[0], expert_down[0]
    ups = lax.all_gather(up_cast.astype(BF), "fsdp", axis=0, tiled=True)
    down_own = down_cast.astype(BF)
    downs = (down_own, across(down_own))
    scale = width ** (-0.5)
    visible = (sequence[:asked, None] == sequence[None, :]) & (
        position[None, :] <= position[:asked, None]
    )
    scores = jnp.where(visible, contract_last(query, keys) * scale, NEGATIVE)
    peak = jnp.max(scores, -1, keepdims=True)
    weights = jnp.where(visible, jnp.exp(scores - peak), 0.0)
    total = jnp.sum(weights, -1, keepdims=True)
    mixed_f = matmul(weights.astype(BF), values) / total
    logsum = peak + jnp.log(total)

    def to_owner(value, needs, carried):
        if repeat > 1:
            value = jnp.pad(value, ((0, group - asked), (0, 0)))
        value = value.reshape(count, rows, -1)
        plan = Deal(count, value, pick=lambda me, to: offset_of(count, me, to))
        got, rest_own, carried = exchange(
            count, 1, [value, rest], [plan, Deal(count, rest, both=True)],
            spans=[(0, 1), (1, 2)], needs=needs, carry=[carried],
        )
        if repeat > 1:
            got = jnp.sum(got.reshape(HEADS, repeat, rows, -1).astype(F32), 1).astype(BF)
        return jnp.transpose(got, (1, 0, 2)).reshape(rows, -1), rest_own, carried

    route_all = box.gather(route_own)
    mine = jnp.any(route_all == me, -1)
    capacity = rows * TOP * 4 // (3 * experts) * count
    counted = jnp.cumsum(mine.astype(jnp.int32))
    slot = jnp.where(mine, counted - 1, -1)
    starts = jnp.concatenate([jnp.zeros((1,), jnp.int32), counted[TILE - 1 :: TILE]])
    column = jnp.arange(experts, dtype=jnp.int32)[None, :] == me
    info = jnp.stack([half, me]).astype(jnp.int32)
    mixed, rest_own, cot_parts[0] = to_owner(mixed_f.astype(BF), [slot, gates], cot_parts[0])
    cot_held = joined(cot_parts)
    hidden = tokens[0].astype(F32)
    residual = hidden + contract_last(mixed, output_full)

    residual_scale = norm_scale(residual)
    normed_two = (residual * residual_scale * gain_second).astype(BF)
    two_all, cot_held = exchange(
        count, 2, [normed_two], [Gather(count, normed_two, 4)], carry=[cot_held]
    )
    two_all = two_all.reshape(group, D)
    cot_parts = box.spread(cot_held, 1)
    probs_all = jax.nn.softmax(matmul(two_all, router_full), -1)
    gate_col = jnp.sum(jnp.where(column & mine[:, None], probs_all, 0.0), -1, keepdims=True)
    rows_in, gate_val, up_val, expert_hidden, cot_parts[0] = expert_in(
        info, starts, (slot[None, :], capacity), two_all, gates, ups, [cot_parts[0]]
    )
    cot_held = joined(cot_parts)
    cot_all = joined(box.spread(cot_held, 2))
    rest_own = rest_own.reshape(D, -1)
    sgate_own = pad_last(rest_own[:, :fs], fp)
    sup_own = pad_last(rest_own[:, fs : 2 * fs], fp)
    sdown_own = pad_last(rest_own[:, 2 * fs : 3 * fs], fp)
    sg, su, shared_hidden = shared_in(two_all, sgate_own, sup_own)
    produced, out_two = expert_out(
        info, starts, expert_hidden, downs, slot[:, None], gate_col, shared_hidden, sdown_own,
        [cot_held],
    )

    out_held = summed(box.share(out_two, 2), BF)
    grad_in, grad_eg, grad_eu, grad_rows, dots = expert_back(
        info, starts, slot[None, :], gate_col.reshape(1, group), cot_all, produced, gate_val, up_val,
        gates, ups, downs, [out_held],
    )
    out_held = summed(box.share(out_held, 1), BF)
    grad_two_part, grad_sg, grad_su, gg_part = tokens_back(
        info, starts, slot[:, None], dots.reshape(1, capacity), grad_rows, cot_all, sg, su,
        sgate_own, sup_own, sdown_own, experts,
    )
    d_rest = [
        leading_contraction(two_all, grad_sg)[:, :fs],
        leading_contraction(two_all, grad_su)[:, :fs],
        leading_contraction(cot_all, shared_hidden)[:, :fs],
    ]
    d_rest = pad_last(jnp.concatenate(d_rest, 1).astype(BF), up_to(3 * fs))
    d_rest = d_rest.reshape(count, 2, shard, -1)
    rest_mine, rest_got = halves_sent(d_rest)
    d_down = leading_contraction(grad_in, expert_hidden).astype(BF)
    products = Products(
        [rows_in, grad_eg, grad_eu], [(0, 1), (0, 2)]
    )
    gg_part = gg_part.reshape(count, rows, -1)
    grad_two, d_gate, d_up, grad_gates = reduce_blocks(
        3,
        grad_two_part.reshape(count, rows, D),
        [
            (products.values, products, (0.0, 1.0)),
            (gg_part, Scatter(count, gg_part, 1), (0.3, 0.9)),
        ],
        [out_held, d_down],
    )

    d_experts = [
        lax.psum_scatter(v, "fsdp", scatter_dimension=0, tiled=True).astype(F32)[None]
        for v in (d_gate, d_up, d_down)
    ]

    probs = probs_all[:rows]
    grad_logits = probs * (grad_gates - jnp.sum(probs * grad_gates, -1, keepdims=True))
    grad_logits = grad_logits.astype(BF)
    grad_two = grad_two + contract_last(grad_logits, router_full)
    d_router = leading_contraction(normed_two, grad_logits)
    d_second = jnp.sum(grad_two * residual * residual_scale, 0)
    grad_residual = cotangent[0] + norm_back(residual, residual_scale, gain_second, grad_two)

    attended = grad_residual.astype(BF)
    output_own = lax.dynamic_slice_in_dim(output_full, me * VDIM, VDIM, 1)
    attended_all, out_held, rest_mine = exchange(
        count, 4, [attended], [Gather(count, attended, 4)], carry=[out_held, rest_mine]
    )
    d_rest = (rest_mine.astype(F32) + rest_got.astype(F32)).astype(BF)
    out_parts = box.share(out_held, 0)
    d_rest = lax.all_to_all(d_rest, "ctx", split_axis=0, concat_axis=0, tiled=True)
    attended_all = attended_all.reshape(group, D)
    mixed_own = mixed_f.astype(BF)
    d_output = leading_contraction(attended_all, mixed_own)
    grad_mixed = matmul(attended_all, output_own).astype(BF)
    delta = jnp.sum(grad_mixed.astype(F32) * mixed_f, -1, keepdims=True)
    probs_a = jnp.where(visible, jnp.exp(contract_last(query, keys) * scale - logsum), 0.0)
    grad_probs = contract_last(grad_mixed, values)
    grad_scores = (probs_a * (grad_probs - delta)).astype(BF)
    output = residual + summed(out_parts, F32)
    grad_query = matmul(grad_scores, keys)
    grad_keys = leading_contraction(grad_scores, query)
    grad_values = leading_contraction(probs_a.astype(BF), grad_mixed)
    extra = jnp.concatenate([jnp.zeros_like(d_second)[:, None], d_second[:, None], d_router], 1)
    extra = pad_last(extra, up_to(small_cols) - edge)
    grad_norm_part, d_query, d_small, d_expand, d_latent = behind_attention(
        grad_query, grad_keys, grad_values, normed_all, latent, low_part, gain_latent[None, :],
        gain_first[:, None], query_own, small_all, expand_own, cosine, sine, extra,
        [output],
    )

    d_latent = jnp.pad(d_latent.reshape(all_devices, lat_rows), ((0, 0), (0, shard - lat_rows)))
    d_query = jnp.concatenate([d_query, d_output.astype(BF), d_latent.reshape(-1, 1).astype(BF)], 1)
    d_q = d_query.reshape(count, 2, shard, -1)
    d_e = d_expand.reshape(count, 2, -1, d_expand.shape[-1])
    d_small = d_small.reshape(count, 2, shard, -1)
    grad_norm, d_q, d_e, d_small = reduce_blocks(
        5,
        grad_norm_part.reshape(count, rows, D),
        [
            (d_q, DealSum(count, d_q), (0.5, 0.55)),
            (d_e, DealSum(count, d_e), (0.5, 0.56)),
            (d_small, Scatter(count, d_small, 1, both=True), (0.25, 1.1)),
        ],
        [d_rest],
    )
    grad_tokens = grad_residual + norm_back(hidden, norm_scale(hidden), gain_first, grad_norm)

    d_query, d_output, d_sgate, d_sup, d_sdown, d_expand = columns_of(d_rest, d_q, d_e, fs)
    return (
        output[None],
        grad_tokens[None],
        d_small[:, edge],
        jnp.sum(d_q[:, :lat_rows, width + VDIM].astype(F32), 0),
        d_query,
        d_small[:, :edge],
        d_expand,
        d_output,
        d_small[:, edge + 1],
        d_small[:, edge + 2 : edge + 2 + experts],
        d_sgate,
        d_sup,
        d_sdown,
        *d_experts,
    )


def shifted(shard, axis, by):
    devices = lax.axis_size(axis)
    return lax.ppermute(shard, axis, [(i, (i + by) % devices) for i in range(devices)])


def rms_norm(value, gain):
    return value * lax.rsqrt(jnp.mean(value * value, -1, keepdims=True) + EPS) * gain


def rotate(value, position):
    half = value.shape[-1] // 2
    freq = 10000.0 ** (-jnp.arange(half, dtype=jnp.float32) / half)
    angle = position.astype(jnp.float32)[:, None] * freq[None, :]
    cosine = jnp.cos(angle)[:, None, :]
    sine = jnp.sin(angle)[:, None, :]
    first = value[..., :half]
    second = value[..., half:]
    return jnp.concatenate([first * cosine - second * sine, first * sine + second * cosine], -1)


def expert_slots(route_rows, experts):
    flat = route_rows.reshape(-1)
    onehot = (flat[:, None] == jnp.arange(experts, dtype=jnp.int32)[None, :]).astype(jnp.int32)
    before = jnp.cumsum(onehot, 0) - onehot
    return (flat, jnp.sum(before * onehot, 1))


def swiglu(gate_value, up_value):
    return jax.nn.silu(gate_value) * up_value


def softmax_last(value):
    return jax.nn.softmax(value, -1)


def local_gathered(
    tokens,
    cotangent,
    lengths,
    token_order,
    routes,
    first_gain,
    latent_gain,
    query_weight,
    compress_weight,
    expand_weight,
    output_weight,
    second_gain,
    router_weight,
    shared_gate,
    shared_up,
    shared_down,
    expert_gate,
    expert_up,
    expert_down,
):
    (
        gain_first,
        gain_latent,
        query_full,
        compress_full,
        expand_full,
        output_full,
        gain_second,
        router_full,
        shared_gate_full,
        shared_up_full,
        shared_down_full,
    ) = (
        lax.all_gather(first_gain.astype(jnp.bfloat16), ("ctx", "fsdp"), axis=0, tiled=True),
        lax.all_gather(latent_gain.astype(jnp.bfloat16), ("ctx", "fsdp"), axis=0, tiled=True),
        lax.all_gather(query_weight.astype(jnp.bfloat16), ("ctx", "fsdp"), axis=0, tiled=True),
        lax.all_gather(compress_weight.astype(jnp.bfloat16), ("ctx", "fsdp"), axis=0, tiled=True),
        lax.all_gather(expand_weight.astype(jnp.bfloat16), ("ctx", "fsdp"), axis=0, tiled=True),
        lax.all_gather(output_weight.astype(jnp.bfloat16), ("ctx", "fsdp"), axis=0, tiled=True),
        lax.all_gather(second_gain.astype(jnp.bfloat16), ("ctx", "fsdp"), axis=0, tiled=True),
        lax.all_gather(router_weight.astype(jnp.bfloat16), ("ctx", "fsdp"), axis=0, tiled=True),
        lax.all_gather(shared_gate.astype(jnp.bfloat16), ("ctx", "fsdp"), axis=0, tiled=True),
        lax.all_gather(shared_up.astype(jnp.bfloat16), ("ctx", "fsdp"), axis=0, tiled=True),
        lax.all_gather(shared_down.astype(jnp.bfloat16), ("ctx", "fsdp"), axis=0, tiled=True),
    )
    gate_expert, up_expert, down_expert = (
        lax.all_gather(expert_gate.astype(jnp.bfloat16), "fsdp", axis=1, tiled=True),
        lax.all_gather(expert_up.astype(jnp.bfloat16), "fsdp", axis=1, tiled=True),
        lax.all_gather(expert_down.astype(jnp.bfloat16), "fsdp", axis=1, tiled=True),
    )
    gate_expert = gate_expert[0]
    up_expert = up_expert[0]
    down_expert = down_expert[0]
    rows = tokens.shape[1]
    place = lax.axis_index("ctx")
    devices = lax.axis_size("ctx")
    query_width = NOPE + ROPE
    sequence, position = placement(lengths[0], token_order[0])
    own_seq = lax.dynamic_slice_in_dim(sequence, place * rows, rows)
    own_pos = lax.dynamic_slice_in_dim(position, place * rows, rows)

    def visible_mask(start, count):
        key_seq = lax.dynamic_slice_in_dim(sequence, start, count)
        key_pos = lax.dynamic_slice_in_dim(position, start, count)
        return (own_seq[:, None] == key_seq[None, :]) & (key_pos[None, :] <= own_pos[:, None])

    def turn_query(part):
        return rotate(part, own_pos)

    def turn_key(part):
        return rotate(part[:, None, :], own_pos)[:, 0, :]

    hidden = tokens[0].astype(jnp.float32)
    normed_f, norm_pull = jax.vjp(rms_norm, hidden, gain_first.astype(jnp.float32))
    normed = normed_f.astype(jnp.bfloat16)
    query_raw = matmul(normed, query_full).reshape(rows, HEADS, query_width)
    query_rotated, query_pull = jax.vjp(turn_query, query_raw[..., NOPE:])
    query = jnp.concatenate([query_raw[..., :NOPE], query_rotated], -1).astype(jnp.bfloat16)
    compressed = matmul(normed, compress_full)
    latent_f, latent_pull = jax.vjp(
        rms_norm, compressed[:, :LATENT], gain_latent.astype(jnp.float32)
    )
    latent = latent_f.astype(jnp.bfloat16)
    expanded = matmul(latent, expand_full).reshape(rows, HEADS, NOPE + VDIM)
    key_rot, key_pull = jax.vjp(turn_key, compressed[:, LATENT:])
    keys = jnp.concatenate(
        [expanded[..., :NOPE], jnp.broadcast_to(key_rot[:, None, :], (rows, HEADS, ROPE))], -1
    )
    keys = keys.astype(jnp.bfloat16).reshape(rows, HEADS * query_width)
    values = expanded[..., NOPE:].astype(jnp.bfloat16).reshape(rows, HEADS * VDIM)
    scale = query_width ** (-0.5)
    running = jnp.full((HEADS, rows), NEGATIVE, jnp.float32)
    key_piece = lax.all_gather(keys, "ctx", axis=0, tiled=True)
    value_piece = lax.all_gather(values, "ctx", axis=0, tiled=True)
    count = key_piece.shape[0]
    scores = (
        jnp.einsum(
            "qhd,khd->hqk",
            query,
            key_piece.reshape(count, HEADS, query_width),
            preferred_element_type=jnp.float32,
        )
        * scale
    )
    visible = visible_mask(jnp.int32(0), count)[None]
    masked = jnp.where(visible, scores, NEGATIVE)
    newest = jnp.maximum(running, jnp.max(masked, -1))
    weights = jnp.where(visible, jnp.exp(masked - newest[..., None]), 0.0)
    total = jnp.sum(weights, -1)
    summed = jnp.einsum(
        "hqk,khd->qhd",
        weights.astype(jnp.bfloat16),
        value_piece.reshape(count, HEADS, VDIM),
        preferred_element_type=jnp.float32,
    )
    running, total, summed = (newest, total, summed)
    mixed_f = summed / jnp.transpose(total)[:, :, None]
    logsum = running + jnp.log(total)
    mixed = mixed_f.astype(jnp.bfloat16).reshape(rows, HEADS * VDIM)
    residual = hidden + contract_last(mixed, output_full)
    normed_two_f, norm_two_pull = jax.vjp(rms_norm, residual, gain_second.astype(jnp.float32))
    normed_two = normed_two_f.astype(jnp.bfloat16)
    logits = matmul(normed_two, router_full)
    experts = router_full.shape[1]
    route_rows = routes[0]
    pick = (route_rows[:, :, None] == jnp.arange(experts, dtype=jnp.int32)[None, None, :]).astype(
        jnp.float32
    )
    router_probs, gate_pull = jax.vjp(softmax_last, logits)
    gates = jnp.sum(pick * router_probs[:, None, :], -1)
    shared_gate_val = matmul(normed_two, shared_gate_full)
    shared_up_val = matmul(normed_two, shared_up_full)
    shared_hidden = swiglu(shared_gate_val, shared_up_val).astype(jnp.bfloat16)
    shared_out = contract_last(shared_hidden, shared_down_full)
    capacity = rows * TOP * 4 // (3 * experts)
    flat, slot = expert_slots(route_rows, experts)
    anchor = jnp.arange(rows * TOP, dtype=jnp.int32) // TOP
    outgoing = (
        jnp.zeros((experts, capacity, D), jnp.bfloat16).at[flat, slot].set(normed_two[anchor])
    )
    arrived = lax.all_to_all(outgoing, "ctx", split_axis=0, concat_axis=0, tiled=True)
    received_rows = arrived.reshape(-1, D)
    gate_val = matmul(received_rows, gate_expert)
    up_val = matmul(received_rows, up_expert)
    expert_hidden = swiglu(gate_val, up_val).astype(jnp.bfloat16)
    produced = contract_last(expert_hidden, down_expert).astype(jnp.bfloat16).reshape(arrived.shape)
    returned = lax.all_to_all(produced, "ctx", split_axis=0, concat_axis=0, tiled=True)
    route_out = returned[flat, slot].astype(jnp.float32).reshape(rows, TOP, D)
    routed = jnp.sum(gates[:, :, None] * route_out, 1)
    output = residual + routed + shared_out
    grad_out = cotangent[0]
    grad_low = grad_out.astype(jnp.bfloat16)
    grad_shared_hidden = matmul(grad_low, shared_down_full)
    grad_sdown = leading_contraction(grad_low, shared_hidden)
    grad_sg, grad_su = jax.vjp(swiglu, shared_gate_val, shared_up_val)[1](grad_shared_hidden)
    grad_sg = grad_sg.astype(jnp.bfloat16)
    grad_su = grad_su.astype(jnp.bfloat16)
    grad_sgate = leading_contraction(normed_two, grad_sg)
    grad_sup = leading_contraction(normed_two, grad_su)
    grad_normed_two = contract_last(grad_sg, shared_gate_full) + contract_last(
        grad_su, shared_up_full
    )
    grad_gates = jnp.sum(grad_out[:, None, :] * route_out, -1)
    grad_route = (
        (gates[:, :, None] * grad_out[:, None, :]).astype(jnp.bfloat16).reshape(rows * TOP, D)
    )
    grad_outgoing = jnp.zeros((experts, capacity, D), jnp.bfloat16).at[flat, slot].set(grad_route)
    grad_arrived = lax.all_to_all(
        grad_outgoing, "ctx", split_axis=0, concat_axis=0, tiled=True
    ).reshape(-1, D)
    grad_expert_hidden = matmul(grad_arrived, down_expert)
    grad_edown = leading_contraction(grad_arrived, expert_hidden)
    grad_eg, grad_expert_up_value = jax.vjp(swiglu, gate_val, up_val)[1](grad_expert_hidden)
    grad_eg = grad_eg.astype(jnp.bfloat16)
    grad_expert_up_value = grad_expert_up_value.astype(jnp.bfloat16)
    grad_egate = leading_contraction(received_rows, grad_eg)
    grad_expert_up_partial = leading_contraction(received_rows, grad_expert_up_value)
    grad_rows = (
        contract_last(grad_eg, gate_expert) + contract_last(grad_expert_up_value, up_expert)
    ).astype(jnp.bfloat16)
    grad_back = lax.all_to_all(
        grad_rows.reshape(arrived.shape), "ctx", split_axis=0, concat_axis=0, tiled=True
    )
    grad_normed_two = grad_normed_two + jnp.sum(
        grad_back[flat, slot].astype(jnp.float32).reshape(rows, TOP, D), 1
    )
    expert_parts = (
        lax.psum_scatter(
            grad_egate[None].astype(jnp.bfloat16), "fsdp", scatter_dimension=1, tiled=True
        ).astype(jnp.float32),
        lax.psum_scatter(
            grad_expert_up_partial[None].astype(jnp.bfloat16),
            "fsdp",
            scatter_dimension=1,
            tiled=True,
        ).astype(jnp.float32),
        lax.psum_scatter(
            grad_edown[None].astype(jnp.bfloat16), "fsdp", scatter_dimension=1, tiled=True
        ).astype(jnp.float32),
    )
    grad_router_probs = jnp.sum(pick * grad_gates[:, :, None], 1)
    grad_logits = gate_pull(grad_router_probs)[0].astype(jnp.bfloat16)
    grad_normed_two = grad_normed_two + contract_last(grad_logits, router_full)
    grad_router = leading_contraction(normed_two, grad_logits)
    grad_residual_norm, grad_gain_second = norm_two_pull(grad_normed_two)
    grad_residual = grad_out + grad_residual_norm
    grad_attended = grad_residual.astype(jnp.bfloat16)
    grad_mixed = matmul(grad_attended, output_full).astype(jnp.bfloat16).reshape(rows, HEADS, VDIM)
    grad_output_w = leading_contraction(grad_attended, mixed)
    delta = jnp.transpose(jnp.sum(grad_mixed.astype(jnp.float32) * mixed_f, -1))

    def rotation_loop_step(step, carry):
        key_block, value_block, grad_key, grad_value, grad_query = carry
        start = (place - step) % devices * rows
        keyed = key_block.reshape(rows, HEADS, query_width)
        valued = value_block.reshape(rows, HEADS, VDIM)
        scores = (
            jnp.einsum("qhd,khd->hqk", query, keyed, preferred_element_type=jnp.float32) * scale
        )
        visible = visible_mask(start, rows)[None]
        weights = jnp.where(visible, jnp.exp(scores - logsum[:, :, None]), 0.0)
        weights_low = weights.astype(jnp.bfloat16)
        grad_weights = jnp.einsum(
            "qhd,khd->hqk", grad_mixed, valued, preferred_element_type=jnp.float32
        )
        grad_scores = (weights * (grad_weights - delta[:, :, None])).astype(jnp.bfloat16)
        grad_query = grad_query + scale * jnp.einsum(
            "hqk,khd->qhd", grad_scores, keyed, preferred_element_type=jnp.float32
        )
        grad_key = grad_key + scale * jnp.einsum(
            "hqk,qhd->khd", grad_scores, query, preferred_element_type=jnp.float32
        )
        grad_value = grad_value + jnp.einsum(
            "hqk,qhd->khd", weights_low, grad_mixed, preferred_element_type=jnp.float32
        )
        grad_key, grad_value = (
            shifted(grad_key.astype(jnp.bfloat16), "ctx", 1).astype(grad_key.dtype),
            shifted(grad_value.astype(jnp.bfloat16), "ctx", 1).astype(grad_value.dtype),
        )
        key_block, value_block = shifted((key_block, value_block), "ctx", 1)
        return (key_block, value_block, grad_key, grad_value, grad_query)

    cycle_start = (
        keys,
        values,
        jnp.zeros((rows, HEADS, query_width), jnp.float32),
        jnp.zeros((rows, HEADS, VDIM), jnp.float32),
        jnp.zeros((rows, HEADS, query_width), jnp.float32),
    )
    cycle_end = lax.fori_loop(0, devices, rotation_loop_step, cycle_start)
    grad_key = cycle_end[2]
    grad_value = cycle_end[3]
    grad_query = cycle_end[4]
    grad_key_rotary = jnp.sum(grad_key[..., NOPE:], 1)
    grad_expanded_latent = jnp.concatenate([grad_key[..., :NOPE], grad_value], -1)
    grad_expanded_latent = grad_expanded_latent.reshape(rows, HEADS * (NOPE + VDIM)).astype(
        jnp.bfloat16
    )
    grad_latent = contract_last(grad_expanded_latent, expand_full)
    grad_expand_w = leading_contraction(latent, grad_expanded_latent)
    grad_comp_latent, grad_gain_latent = latent_pull(grad_latent)
    grad_comp_rope = key_pull(grad_key_rotary)[0]
    grad_compressed = jnp.concatenate([grad_comp_latent, grad_comp_rope], -1).astype(jnp.bfloat16)
    grad_query_rope = query_pull(grad_query[..., NOPE:])[0]
    grad_query_raw = jnp.concatenate([grad_query[..., :NOPE], grad_query_rope], -1)
    grad_query_raw = grad_query_raw.reshape(rows, HEADS * query_width).astype(jnp.bfloat16)
    grad_normed = contract_last(grad_query_raw, query_full) + contract_last(
        grad_compressed, compress_full
    )
    grad_query_w = leading_contraction(normed, grad_query_raw)
    grad_compress_w = leading_contraction(normed, grad_compressed)
    grad_hidden_norm, grad_gain_first = norm_pull(grad_normed)
    grad_input = grad_residual + grad_hidden_norm
    dense_parts = (
        lax.psum_scatter(grad_gain_first, ("ctx", "fsdp"), scatter_dimension=0, tiled=True),
        lax.psum_scatter(grad_gain_latent, ("ctx", "fsdp"), scatter_dimension=0, tiled=True),
        lax.psum_scatter(grad_query_w, ("ctx", "fsdp"), scatter_dimension=0, tiled=True),
        lax.psum_scatter(grad_compress_w, ("ctx", "fsdp"), scatter_dimension=0, tiled=True),
        lax.psum_scatter(grad_expand_w, ("ctx", "fsdp"), scatter_dimension=0, tiled=True),
        lax.psum_scatter(grad_output_w, ("ctx", "fsdp"), scatter_dimension=0, tiled=True),
        lax.psum_scatter(grad_gain_second, ("ctx", "fsdp"), scatter_dimension=0, tiled=True),
        lax.psum_scatter(grad_router, ("ctx", "fsdp"), scatter_dimension=0, tiled=True),
        lax.psum_scatter(grad_sgate, ("ctx", "fsdp"), scatter_dimension=0, tiled=True),
        lax.psum_scatter(grad_sup, ("ctx", "fsdp"), scatter_dimension=0, tiled=True),
        lax.psum_scatter(grad_sdown, ("ctx", "fsdp"), scatter_dimension=0, tiled=True),
    )
    return (
        output[None],
        grad_input[None],
        dense_parts[0],
        dense_parts[1],
        dense_parts[2],
        dense_parts[3],
        dense_parts[4],
        dense_parts[5],
        dense_parts[6],
        dense_parts[7],
        dense_parts[8],
        dense_parts[9],
        dense_parts[10],
        expert_parts[0],
        expert_parts[1],
        expert_parts[2],
    )


def solution(mesh):
    token_spec = P("fsdp", "ctx", None)
    vector = P(("ctx", "fsdp"))
    matrix = P(("ctx", "fsdp"), None)
    expert = P("ctx", "fsdp", None)
    weights = (vector, vector, matrix, matrix, matrix, matrix, vector, matrix, matrix, matrix, matrix)
    weights = weights + (expert,) * 3
    return jax.shard_map(
        local if mesh.shape["ctx"] == HEADS else local_gathered,
        mesh=mesh,
        in_specs=(token_spec, token_spec, P("fsdp", None), P("fsdp", None), token_spec) + weights,
        out_specs=(token_spec, token_spec) + weights,
        check_vma=False,
    )
```

```python
import functools

import jax
import jax.numpy as jnp
from jax import lax
from jax.experimental import pallas as pl
from jax.experimental.pallas import tpu as pltpu
from jax.sharding import PartitionSpec as P

D = 2048
HEADS = 16
NOPE = 128
ROPE = 64
VDIM = 128
LATENT = 512
TOP = 6
EPS = 1e-06
NEGATIVE = -1e30
BF = jnp.bfloat16
F32 = jnp.float32


def matmul(left, right):
    return jnp.dot(left, right, preferred_element_type=F32)


def contract_last(left, right):
    return lax.dot_general(left, right, (((1,), (1,)), ((), ())), preferred_element_type=F32)


def leading_contraction(left, right):
    return lax.dot_general(left, right, (((0,), (0,)), ((), ())), preferred_element_type=F32)


def norm_scale(value):
    return lax.rsqrt(jnp.mean(value * value, -1, keepdims=True) + EPS)


def norm_back(value, scale, gain, grad):
    lifted = grad * gain
    return scale * lifted - value * (scale**3 * jnp.mean(lifted * value, -1, keepdims=True))


def turn(value, cosine, sine):
    half = value.shape[-1] // 2
    first, second = value[..., :half], value[..., half:]
    return jnp.concatenate([first * cosine - second * sine, first * sine + second * cosine], -1)


def swiglu_parts(gate, up):
    sigmoid = 1.0 / (1.0 + jnp.exp(-gate))
    act = gate * sigmoid
    return act, sigmoid * (1.0 + gate * (1.0 - sigmoid))


def box_of(count):
    dims = [2, 2]
    count //= 4
    while count > 1:
        side = 4 if count % 4 == 0 else 2
        dims.insert(0, side)
        count //= side
    return dims


class Box:
    def __init__(self):
        self.count = lax.axis_size("ctx")
        self.dims = box_of(self.count)
        self.strides = []
        stride = self.count
        for side in self.dims:
            stride //= side
            self.strides.append(stride)

    def shift(self, value, dim, by):
        side, stride = self.dims[dim], self.strides[dim]

        def target(i):
            here = i // stride % side
            return i + ((here + by) % side - here) * stride

        return lax.ppermute(value, "ctx", [(i, target(i)) for i in range(self.count)])

    def owners(self):
        me = lax.axis_index("ctx")
        owner = jnp.zeros((1,), jnp.int32)
        for side, stride in zip(self.dims, self.strides):
            here = me // stride % side
            offset = (here - jnp.arange(side, dtype=jnp.int32)) % side * stride
            owner = (offset[:, None] + owner[None, :]).reshape(-1)
        return owner

    def spread(self, held, dim):
        return [held] + [self.shift(held, dim, k) for k in range(1, self.dims[dim])]

    def gather(self, held):
        for dim in range(len(self.dims)):
            held = jnp.concatenate(self.spread(held, dim), 0)
        return held

    def share(self, held, dim):
        parts = jnp.split(held, self.dims[dim], 0)
        return parts[:1] + [self.shift(parts[k], dim, -k) for k in range(1, self.dims[dim])]


def joined(parts):
    return jnp.concatenate(parts, 0)


def summed(parts, dtype):
    total = parts[0].astype(F32)
    for part in parts[1:]:
        total = total + part.astype(F32)
    return total.astype(dtype)


MESH = pl.DeviceIdType.MESH
DMA = pltpu.SemaphoreType.DMA


def sides(count, both=False):
    found, stride, held = [], count, 1
    for side in box_of(count):
        stride //= side
        found.append(("ctx", side, stride, held))
        held *= side
    if both:
        found = [("fsdp", 2, 1, 1)] + [(axis, n, by, held * 2) for axis, n, by, held in found]
    return found


def moved(me, side, stride, by):
    here = me // stride % side
    return me + ((here + by) % side - here) * stride


def offset_of(count, me, owner):
    total = 0
    for _, side, stride, held in sides(count):
        total = total + (me // stride % side + side - owner // stride % side) % side * held
    return total


def remote(src, dst, send, recv, axis, target):
    return pltpu.make_async_remote_copy(
        src_ref=src,
        dst_ref=dst,
        send_sem=send,
        recv_sem=recv,
        device_id={axis: target},
        device_id_type=MESH,
    )


class Gather:
    def __init__(self, count, value, chunks):
        self.count, self.chunks = count, chunks
        self.taken, self.outs = 1, [jax.ShapeDtypeStruct((count,) + value.shape, value.dtype)]
        self.scratch = [DMA, DMA((count, chunks)), DMA((count, chunks))]
        self.space, self.out_space = pl.ANY, pl.ANY
        self.reach = "box"

    def bind(self, me, half, x_ref, out_ref, own_sem, send_sem, recv_sem):
        self.me, self.x, self.o = me, x_ref, out_ref
        self.sems = (send_sem, recv_sem)
        self.own = pltpu.make_async_copy(x_ref, out_ref.at[0], own_sem)
        self.sent = []
        self.dims = sides(self.count)

    def copy(self, block, chunk, dim, by):
        _, side, stride, held = self.dims[dim]
        step = self.x.shape[0] // self.chunks
        part = pl.ds(chunk * step, step)
        src = self.x.at[part] if block == 0 else self.o.at[block, part]
        to = by * held + block
        return remote(
            src,
            self.o.at[to, part],
            self.sems[0].at[to, chunk],
            self.sems[1].at[to, chunk],
            "ctx",
            moved(self.me, side, stride, by),
        )

    def forward(self, block, chunk, first):
        for dim in range(first, len(self.dims)):
            for by in range(1, self.dims[dim][1]):
                copy = self.copy(block, chunk, dim, by)
                copy.start()
                self.sent.append(copy)

    def start(self):
        self.own.start()
        for chunk in range(self.chunks):
            self.forward(0, chunk, 0)

    def arrive(self, chunk, dim):
        _, side, _, held = self.dims[dim]
        for by in range(1, side):
            for block in range(held):
                self.copy(block, chunk, dim, by).wait_recv()
                self.forward(by * held + block, chunk, dim + 1)

    def steps(self):
        found, last = [], len(self.dims)
        for wave in range(self.chunks + last - 1):
            for dim in range(last):
                if 0 <= wave - dim < self.chunks:
                    found.append(functools.partial(self.arrive, wave - dim, dim))
        return found

    def finish(self):
        for copy in self.sent:
            copy.wait_send()
        self.own.wait()


class GatherAll:
    def __init__(self, count, value):
        self.count = count
        self.taken, self.outs = 1, [jax.ShapeDtypeStruct((count, 2) + value.shape, value.dtype)]
        self.scratch = [DMA, DMA((count, 2)), DMA((count, 2))]
        self.space, self.out_space = pl.ANY, pl.ANY
        self.reach = "box+half"

    def bind(self, me, half, x_ref, out_ref, own_sem, send_sem, recv_sem):
        self.me, self.half, self.x, self.o = me, half, x_ref, out_ref
        self.sems = (send_sem, recv_sem)
        self.own = pltpu.make_async_copy(x_ref, out_ref.at[me, half], own_sem)
        self.sent = []
        self.dims = sides(self.count)

    def owner(self, block):
        owner = self.me
        for _, side, stride, held in self.dims:
            owner = moved(owner, side, stride, -(block // held % side))
        return owner

    def copy(self, block, other, dim, by):
        _, side, stride, held = self.dims[dim]
        owner = self.owner(block)
        half = 1 - self.half if other else self.half
        src = self.x if block == 0 and not other else self.o.at[owner, half]
        to = by * held + block
        return remote(
            src,
            self.o.at[owner, half],
            self.sems[0].at[to, other],
            self.sems[1].at[to, other],
            "ctx",
            moved(self.me, side, stride, by),
        )

    def arrived(self, block, other, dim, by):
        _, side, stride, held = self.dims[dim]
        to = by * held + block
        half = 1 - self.half if other else self.half
        here = self.o.at[self.owner(to), half]
        return remote(
            here, here, self.sems[0].at[to, other], self.sems[1].at[to, other], "ctx",
            moved(self.me, side, stride, by),
        )

    def across(self, half):
        return remote(
            self.x, self.o.at[self.me, half], self.sems[0].at[0, 0], self.sems[1].at[0, 0],
            "fsdp", 1 - self.half,
        )

    def forward(self, block, other, first):
        for dim in range(first, len(self.dims)):
            for by in range(1, self.dims[dim][1]):
                copy = self.copy(block, other, dim, by)
                copy.start()
                self.sent.append(copy)

    def start(self):
        self.own.start()
        self.cross = self.across(self.half)
        self.cross.start()
        self.forward(0, 0, 0)

    def meet(self):
        self.across(1 - self.half).wait_recv()
        self.forward(0, 1, 0)

    def arrive(self, dim):
        _, side, _, held = self.dims[dim]
        for other in range(2):
            for by in range(1, side):
                for block in range(held):
                    self.arrived(block, other, dim, by).wait_recv()
                    self.forward(by * held + block, other, dim + 1)

    def steps(self):
        return [self.meet] + [functools.partial(self.arrive, d) for d in range(len(self.dims))]

    def finish(self):
        for copy in self.sent:
            copy.wait_send()
        self.cross.wait_send()
        self.own.wait()


class Deal:
    def __init__(self, count, value, both=False, pick=None, place=None):
        self.count, self.both = count, both
        self.pick = pick or (lambda me, to: to)
        self.place = place or (lambda me, to: me)
        shape = value.shape[:1] + ((2,) if both else ()) + value.shape[1:]
        self.taken, self.outs = 1, [jax.ShapeDtypeStruct(shape, value.dtype)]
        self.scratch = [DMA, DMA((count, 2)), DMA((count, 2))]
        self.space, self.out_space = pl.ANY, pl.ANY
        self.reach = "all+half" if both else "all"

    def bind(self, me, half, x_ref, out_ref, own_sem, send_sem, recv_sem):
        self.me, self.half, self.x, self.o = me, half, x_ref, out_ref
        self.send, self.recv = send_sem, recv_sem
        self.sent = []
        self.own = pltpu.make_async_copy(
            x_ref.at[self.pick(me, me)], self.here(self.place(me, me), half), own_sem
        )

    def here(self, slot, half):
        return self.o.at[slot, half] if self.both else self.o.at[slot]

    def copy(self, by):
        to = (self.me + by) % self.count
        return remote(
            self.x.at[self.pick(self.me, to)],
            self.here(self.place(self.me, to), self.half),
            self.send.at[by, 0],
            self.recv.at[by, 0],
            "ctx",
            to,
        )

    def arrived(self, by):
        source = (self.me + self.count - by) % self.count
        slot = self.here(self.place(source, self.me), self.half)
        return remote(
            slot, slot, self.send.at[by, 0], self.recv.at[by, 0], "ctx", (self.me + by) % self.count
        )

    def across(self, by, half):
        source = (self.me + self.count - by) % self.count
        slot = self.here(self.place(source, self.me), half)
        src = self.x.at[self.pick(self.me, self.me)] if by == 0 else slot
        return remote(
            src, slot, self.send.at[by, 1], self.recv.at[by, 1], "fsdp", 1 - self.half
        )

    def start(self):
        self.own.start()
        for by in range(1, self.count):
            copy = self.copy(by)
            copy.start()
            self.sent.append(copy)
        if self.both:
            self.pass_on(0)

    def pass_on(self, by):
        copy = self.across(by, self.half)
        copy.start()
        self.sent.append(copy)

    def arrive(self, by):
        self.arrived(by).wait_recv()
        if self.both:
            self.pass_on(by)

    def rest(self):
        for by in range(self.count):
            self.across(by, 1 - self.half).wait_recv()

    def steps(self):
        return [functools.partial(self.arrive, by) for by in range(1, self.count)]

    def finish(self):
        if self.both:
            self.rest()
        for copy in self.sent:
            copy.wait_send()
        self.own.wait()


class DealSum:
    def __init__(self, count, value):
        self.count = count
        shape = value.shape[:1] + value.shape[2:]
        self.taken, self.outs = 1, [jax.ShapeDtypeStruct(shape, value.dtype)]
        self.scratch = [pltpu.VMEM(shape, value.dtype), pltpu.VMEM(shape, value.dtype)]
        self.scratch += [DMA, DMA((count, 2)), DMA((count, 2))]
        self.space, self.out_space = pltpu.VMEM, pl.ANY
        self.reach = "all+half"

    def bind(self, me, half, x_ref, out_ref, landed, total, own_sem, send_sem, recv_sem):
        self.me, self.half, self.x, self.o = me, half, x_ref, out_ref
        self.landed, self.total = landed, total
        self.send, self.recv = send_sem, recv_sem
        self.own = pltpu.make_async_copy(total.at[me], out_ref.at[me], own_sem)
        self.sent = []

    def cross(self, part):
        return remote(
            self.x.at[part, 1 - self.half], self.landed.at[part], self.send.at[part, 1],
            self.recv.at[part, 1], "fsdp", 1 - self.half,
        )

    def copy(self, by):
        to = (self.me + by) % self.count
        return remote(
            self.total.at[to], self.o.at[self.me], self.send.at[by, 0], self.recv.at[by, 0],
            "ctx", to,
        )

    def start(self):
        for part in range(self.count):
            copy = self.cross(part)
            copy.start()
            self.sent.append(copy)

    def add(self):
        for part in range(self.count):
            self.cross(part).wait_recv()
            mine = self.x[part, self.half].astype(F32) + self.landed[part].astype(F32)
            self.total[part] = mine.astype(self.total.dtype)
        self.own.start()
        for by in range(1, self.count):
            copy = self.copy(by)
            copy.start()
            self.sent.append(copy)

    def steps(self):
        return [self.add]

    def finish(self):
        for by in range(1, self.count):
            source = (self.me + self.count - by) % self.count
            slot = self.o.at[source]
            remote(
                slot, slot, self.send.at[by, 0], self.recv.at[by, 0], "ctx",
                (self.me + by) % self.count,
            ).wait_recv()
        for copy in self.sent:
            copy.wait_send()
        self.own.wait()


class Scatter:
    def __init__(self, count, value, chunks, both=False):
        self.count, self.chunks, self.both = count, chunks, both
        tail = value.shape[2:] if both else value.shape[1:]
        self.taken, self.outs = 1, [jax.ShapeDtypeStruct(tail, F32)]
        dims = sides(count, both)
        blocks = count * 2 if both else count
        self.scratch = [
            pltpu.VMEM(((side - 1) * held,) + tail, value.dtype) for _, side, _, held in dims
        ]
        self.scratch += [pltpu.VMEM((held,) + tail, value.dtype) for _, _, _, held in dims[1:]]
        self.scratch += [DMA((blocks, chunks)), DMA((blocks, chunks))]
        self.space, self.out_space = pltpu.VMEM, pltpu.VMEM
        self.reach = "box+half" if both else "box"

    def bind(self, me, half, x_ref, out_ref, *scratch):
        self.me, self.half, self.o = me, half, out_ref
        self.blocks = self.count * 2 if self.both else self.count
        self.dims = sides(self.count, self.both)
        levels = len(self.dims)
        self.landed = scratch[:levels]
        self.held = scratch[levels : 2 * levels - 1] + (x_ref,)
        self.send, self.recv = scratch[2 * levels - 1 :]
        self.sent = []

    def part(self, chunk):
        step = self.o.shape[0] // self.chunks
        return pl.ds(chunk * step, step)

    def copy(self, dim, block, chunk):
        axis, side, stride, held = self.dims[dim]
        part = self.part(chunk)
        here = self.me if axis == "ctx" else self.half
        return remote(
            self.held[dim].at[self.at(dim, block) + (part,)],
            self.landed[dim].at[block - held, part],
            self.send.at[block, chunk],
            self.recv.at[block, chunk],
            axis,
            moved(here, side, stride, -(block // held)),
        )

    def at(self, dim, block):
        if not self.both or dim < len(self.dims) - 1:
            return (block,)
        owner = self.me
        for _, side, stride, held in self.dims[1:]:
            owner = moved(owner, side, stride, -(block // held % side))
        return (owner, self.half if block % 2 == 0 else 1 - self.half)

    def ready(self, dim, block, chunk):
        if block >= self.dims[dim][3]:
            copy = self.copy(dim, block, chunk)
            copy.start()
            self.sent.append(copy)

    def add(self, dim, chunk):
        _, side, _, held = self.dims[dim]
        part = self.part(chunk)
        for block in reversed(range(held)):
            total = self.held[dim][self.at(dim, block) + (part,)].astype(F32)
            for by in range(1, side):
                self.copy(dim, by * held + block, chunk).wait_recv()
                total = total + self.landed[dim][(by - 1) * held + block, part].astype(F32)
            if dim == 0:
                self.o[part] = total
            else:
                self.held[dim - 1][block, part] = total.astype(self.held[dim - 1].dtype)
                self.ready(dim - 1, block, chunk)

    def start(self):
        last = len(self.dims) - 1
        for chunk in range(self.chunks):
            for block in reversed(range(self.dims[last][3], self.blocks)):
                self.ready(last, block, chunk)

    def steps(self):
        found, levels = [], len(self.dims)
        for wave in range(self.chunks + levels - 1):
            for dim in reversed(range(levels)):
                chunk = wave - (levels - 1 - dim)
                if 0 <= chunk < self.chunks:
                    found.append(functools.partial(self.add, dim, chunk))
        return found

    def finish(self):
        for copy in self.sent:
            copy.wait_send()


class Products:
    def __init__(self, values, pairs):
        self.values, self.pairs = values, pairs
        self.taken = len(values)
        self.outs = [
            jax.ShapeDtypeStruct((values[a].shape[1], values[b].shape[1]), BF) for a, b in pairs
        ]
        widest = max(out.shape[1] for out in self.outs)
        self.scratch = [pltpu.VMEM(v.shape, v.dtype) for v in values]
        self.scratch += [pltpu.VMEM((2, TILE, widest), BF), DMA((len(values),)), DMA((2,))]
        self.space, self.out_space = pl.ANY, pl.ANY
        self.reach = ""

    def bind(self, me, half, *refs):
        n, m = len(self.values), len(self.pairs)
        self.held = refs[n + m : n + m + n]
        self.tile, self.in_sem, self.out_sem = refs[n + m + n :]
        self.o = refs[n : n + m]
        self.loads = [
            pltpu.make_async_copy(refs[i], self.held[i], self.in_sem.at[i]) for i in range(n)
        ]
        self.stores = []
        self.loaded = set()

    def start(self):
        for load in self.loads:
            load.start()

    def step(self, pair, row):
        for i in self.pairs[pair]:
            if i not in self.loaded:
                self.loads[i].wait()
                self.loaded.add(i)
        left, right = (self.held[i] for i in self.pairs[pair])
        slot = len(self.stores) % 2
        if len(self.stores) >= 2:
            self.stores[-2].wait()
        part = pl.ds(row * TILE, TILE)
        out = self.o[pair]
        place = self.tile.at[slot, :, pl.ds(0, out.shape[1])]
        place[...] = leading_contraction(left[:, part], right[...]).astype(BF)
        store = pltpu.make_async_copy(place, out.at[part], self.out_sem.at[slot])
        store.start()
        self.stores.append(store)

    def steps(self):
        return [
            functools.partial(self.step, pair, row)
            for pair in range(len(self.pairs))
            for row in range(self.outs[pair].shape[0] // TILE)
        ]

    def finish(self):
        for store in self.stores[-2:]:
            store.wait()


def exchange_kernel(count, plans, spans, needed, carried, *refs):
    me, half = lax.axis_index("ctx"), lax.axis_index("fsdp")
    taken = sum(plan.taken for plan in plans)
    ins, refs = refs[:taken], refs[taken + needed + carried :]
    given = sum(len(plan.outs) for plan in plans)
    outs, refs = refs[:given], refs[given + carried :]
    barrier = pltpu.get_barrier_semaphore()
    peers = []
    if any("all" in plan.reach for plan in plans):
        peers = [("ctx", (me + by) % count) for by in range(1, count)]
    else:
        for _, side, stride, _ in sides(count):
            peers += [("ctx", moved(me, side, stride, by)) for by in range(1, side)]
    if any("half" in plan.reach for plan in plans):
        peers.append(("fsdp", 1 - half))
    for axis, target in peers:
        pl.semaphore_signal(barrier, inc=1, device_id={axis: target}, device_id_type=MESH)
    pl.semaphore_wait(barrier, len(peers))
    for plan in plans:
        mine, refs = refs[: len(plan.scratch)], refs[len(plan.scratch) :]
        plan.bind(me, half, *ins[: plan.taken], *outs[: len(plan.outs)], *mine)
        ins, outs = ins[plan.taken :], outs[len(plan.outs) :]
        plan.start()
    timed = []
    for plan, (first, last) in zip(plans, spans):
        steps = plan.steps()
        for i, step in enumerate(steps):
            timed.append((first + (last - first) * (i + 1) / len(steps), step))
    for _, step in sorted(timed, key=lambda entry: entry[0]):
        step()
    for plan in plans:
        plan.finish()


def exchange(count, collective, values, plans, spans=None, needs=(), carry=()):
    spans = spans or [(0.0, 1.0)] * len(plans)
    scratch = [ref for plan in plans for ref in plan.scratch]
    values = [v for value in values for v in (value if isinstance(value, list) else [value])]
    outs = [out for plan in plans for out in plan.outs]
    first = len(values) + len(needs)
    spot = pl.BlockSpec(memory_space=pl.ANY)
    in_specs = [pl.BlockSpec(memory_space=p.space) for p in plans for _ in range(p.taken)]
    out_specs = [pl.BlockSpec(memory_space=p.out_space) for p in plans for _ in p.outs]
    return pl.pallas_call(
        functools.partial(exchange_kernel, count, plans, spans, len(needs), len(carry)),
        out_shape=tuple(outs) + tuple(jax.ShapeDtypeStruct(v.shape, v.dtype) for v in carry),
        in_specs=in_specs + [spot] * (len(needs) + len(carry)),
        out_specs=tuple(out_specs + [spot] * len(carry)),
        input_output_aliases={first + i: len(outs) + i for i in range(len(carry))},
        scratch_shapes=scratch,
        compiler_params=pltpu.CompilerParams(
            collective_id=collective, has_side_effects=True, vmem_limit_bytes=60 << 20
        ),
        cost_estimate=pl.CostEstimate(flops=0, bytes_accessed=100 << 20, transcendentals=0),
    )(*values, *needs, *carry)


TILE = 256


def hot_rows(slots, first):
    count = slots.shape[1]
    return (lax.broadcasted_iota(jnp.int32, (TILE, count), 0) + first == slots).astype(BF)


def hot_cols(slots, first):
    count = slots.shape[0]
    return (lax.broadcasted_iota(jnp.int32, (count, TILE), 1) + first == slots).astype(BF)


def meets(starts, tokens, slots):
    return (starts[tokens] < (slots + 1) * TILE) & (starts[tokens + 1] > slots * TILE)


def split_of(info, width):
    own = pl.multiple_of(info * (width // 2), 128)
    other = pl.multiple_of((1 - info) * (width // 2), 128)
    return pl.ds(own, width // 2), pl.ds(other, width // 2)


def pick_rows(starts, slot_ref, source_ref, total_ref, tile):
    total_ref[...] = jnp.zeros_like(total_ref)
    for j in range(source_ref.shape[0] // TILE):

        @pl.when(meets(starts, j, tile))
        def _():
            part = pl.ds(j * TILE, TILE)
            total_ref[...] += matmul(hot_rows(slot_ref[:, part], tile * TILE), source_ref[part])


def expert_in_kernel(info, starts, slot, two, g0, u0, u1, rows, gate, up, hidden, total):
    pick_rows(starts, slot, two, total, pl.program_id(0))
    rows[...] = total[...].astype(BF)
    gate[...] = matmul(rows[...], g0[...])
    own, other = split_of(info[0], rows.shape[1])
    up[...] = matmul(rows[:, own], u0[...]) + matmul(rows[:, other], u1[...])
    value = gate[...]
    hidden[...] = (value / (1.0 + jnp.exp(-value)) * up[...]).astype(BF)


def expert_out_kernel(
    info, starts, hidden, d0, d1, slot, weight, shared, sdown, produced, out, held, total
):
    step, tiles = pl.program_id(0), held.shape[0] // TILE

    @pl.when(step < tiles)
    def _():
        own, other = split_of(info[0], held.shape[1])
        produced[:, own] = contract_last(hidden[...], d0[...]).astype(BF)
        produced[:, other] = contract_last(hidden[...], d1[...]).astype(BF)
        held[pl.ds(pl.multiple_of(step * TILE, TILE), TILE)] = produced[...]

    @pl.when(step >= tiles)
    def _():
        token = step - tiles
        total[...] = jnp.zeros_like(total)
        for i in range(tiles):

            @pl.when(meets(starts, token, i))
            def _():
                total[...] += matmul(hot_cols(slot[...], i * TILE), held[pl.ds(i * TILE, TILE)])

        out[...] = (weight[...] * total[...] + contract_last(shared[...], sdown[...])).astype(BF)


def expert_back_kernel(
    info, starts, slot, weight, cot, produced, gate, up, g0, u0, u1, d0, d1,
    grad_in, grad_gate, grad_up, grad_rows, dots, total,
):
    tile = pl.program_id(0)
    total[...] = jnp.zeros_like(total)
    dots[...] = jnp.zeros_like(dots)
    for j in range(cot.shape[0] // TILE):

        @pl.when(meets(starts, j, tile))
        def _():
            part = pl.ds(j * TILE, TILE)
            hot = hot_rows(slot[:, part], tile * TILE)
            total[...] += matmul(hot, cot[part])
            dots[...] += jnp.sum(hot.astype(F32) * weight[:, part], 1, keepdims=True)

    grad_in[...] = (dots[...] * total[...]).astype(BF)
    dots[...] = jnp.sum(total[...] * produced[...].astype(F32), 1, keepdims=True)
    own, other = split_of(info[0], grad_in.shape[1])
    grad_hidden = matmul(grad_in[:, own], d0[...]) + matmul(grad_in[:, other], d1[...])
    act, slope = swiglu_parts(gate[...], up[...])
    grad_gate[...] = (grad_hidden * up[...] * slope).astype(BF)
    grad_up[...] = (grad_hidden * act).astype(BF)
    total[...] = contract_last(grad_gate[...], g0[...])
    for part, ups in ((own, u0), (other, u1)):
        grad_rows[:, part] = (total[:, part] + contract_last(grad_up[...], ups[...])).astype(BF)


def shared_in_kernel(two, sgate, sup, gate, up, hidden):
    gate[...] = matmul(two[...], sgate[...])
    up[...] = matmul(two[...], sup[...])
    value = gate[...]
    hidden[...] = (value / (1.0 + jnp.exp(-value)) * up[...]).astype(BF)


def tokens_back_kernel(
    info, starts, slot, dots, grad_rows, cot, gate, up, sgate, sup, sdown,
    out, grad_gate, grad_up, gates, total,
):
    token = pl.program_id(0)
    grad_hidden = matmul(cot[...], sdown[...])
    act, slope = swiglu_parts(gate[...], up[...])
    grad_gate[...] = (grad_hidden * up[...] * slope).astype(BF)
    grad_up[...] = (grad_hidden * act).astype(BF)
    total[...] = contract_last(grad_gate[...], sgate[...]) + contract_last(grad_up[...], sup[...])
    gates[...] = jnp.zeros_like(gates)
    mine = lax.broadcasted_iota(jnp.int32, gates.shape, 1) == info[1]
    for i in range(grad_rows.shape[0] // TILE):

        @pl.when(meets(starts, token, i))
        def _():
            part = pl.ds(i * TILE, TILE)
            hot = hot_cols(slot[...], i * TILE)
            total[...] += matmul(hot, grad_rows[part])
            found = jnp.sum(hot.astype(F32) * dots[:, part], 1, keepdims=True)
            gates[...] += jnp.where(mine, found, 0.0)

    out[...] = total[...].astype(BF)


def whole(value):
    return pl.BlockSpec(value.shape, lambda *_: (0,) * value.ndim, pipeline_mode=pl.Buffered(1))


def tiled(value, index=lambda step: step):
    return pl.BlockSpec((TILE,) + value.shape[1:], lambda step, *_: (index(step), 0))


def run(kernel, steps, scalars, values, specs, outs, out_specs, scratch, flops, needs=(), carry=()):
    moved_bytes = sum(v.size * v.dtype.itemsize for v in list(values) + list(outs))
    first = len(scalars) + len(values)
    fenced = first + len(needs) + len(carry)

    def body(*refs):
        made = refs[fenced : fenced + len(outs)]
        kernel(*refs[:first], *made, *refs[fenced + len(outs) + len(carry) :])

    spot = pl.BlockSpec(memory_space=pl.ANY)
    specs = list(specs) + [spot] * (len(needs) + len(carry))
    out_specs = tuple(out_specs) + (spot,) * len(carry)
    handed = tuple(jax.ShapeDtypeStruct(v.shape, v.dtype) for v in carry)
    return pl.pallas_call(
        body,
        grid_spec=pltpu.PrefetchScalarGridSpec(
            num_scalar_prefetch=len(scalars),
            grid=(steps,),
            in_specs=specs,
            out_specs=out_specs,
            scratch_shapes=scratch,
        ),
        out_shape=tuple(outs) + handed,
        input_output_aliases={first + len(needs) + i: len(outs) + i for i in range(len(carry))},
        compiler_params=pltpu.CompilerParams(vmem_limit_bytes=60 << 20),
        cost_estimate=pl.CostEstimate(flops=flops, bytes_accessed=moved_bytes, transcendentals=0),
    )(*scalars, *values, *needs, *carry)


def like(rows, columns, dtype):
    return jax.ShapeDtypeStruct((rows, columns), dtype)


def expert_in(info, starts, slot_row, two, gates, ups, carry):
    capacity, width, hidden = slot_row[1], two.shape[1], gates.shape[1]
    slot_row = slot_row[0]
    outs = (
        like(capacity, width, BF),
        like(capacity, hidden, F32),
        like(capacity, hidden, F32),
        like(capacity, hidden, BF),
    )
    values = [slot_row, two, gates, *ups]
    return run(
        expert_in_kernel, capacity // TILE, (info, starts), values, [whole(v) for v in values],
        outs, tuple(tiled(o) for o in outs), [pltpu.VMEM((TILE, width), F32)],
        capacity * width * hidden * 4,
        carry=carry,
    )


def expert_out(info, starts, hidden, downs, slot_col, weight_col, shared, sdown, needs):
    capacity, tokens, width = hidden.shape[0], slot_col.shape[0], sdown.shape[0]
    first = capacity // TILE
    outs = (like(capacity, width, BF), like(tokens, width, BF))
    rows_at = lambda step: jnp.minimum(step, first - 1)
    tokens_at = lambda step: jnp.maximum(step - first, 0)
    values = [hidden, *downs, slot_col, weight_col, shared, sdown]
    specs = [tiled(hidden, rows_at), whole(downs[0]), whole(downs[1])]
    specs += [tiled(slot_col, tokens_at), tiled(weight_col, tokens_at), tiled(shared, tokens_at)]
    specs += [whole(sdown)]
    return run(
        expert_out_kernel, first + tokens // TILE, (info, starts), values, specs, outs,
        (tiled(outs[0], rows_at), tiled(outs[1], tokens_at)),
        [pltpu.VMEM((capacity, width), BF), pltpu.VMEM((TILE, width), F32)],
        capacity * width * hidden.shape[1] * 3,
        needs,
    )


def expert_back(
    info, starts, slot_row, weight_row, cot, produced, gate, up, gates, ups, downs, needs
):
    capacity, hidden = gate.shape
    width = cot.shape[1]
    outs = (
        like(capacity, width, BF),
        like(capacity, hidden, BF),
        like(capacity, hidden, BF),
        like(capacity, width, BF),
        like(capacity, 1, F32),
    )
    values = [slot_row, weight_row, cot, produced, gate, up, gates, *ups, *downs]
    specs = [whole(v) for v in values]
    specs[3:6] = [tiled(produced), tiled(gate), tiled(up)]
    return run(
        expert_back_kernel, capacity // TILE, (info, starts), values, specs, outs,
        tuple(tiled(o) for o in outs), [pltpu.VMEM((TILE, width), F32)],
        capacity * width * hidden * 6,
        needs,
    )


def shared_in(two, sgate, sup):
    tokens, hidden = two.shape[0], sgate.shape[1]
    outs = (like(tokens, hidden, F32), like(tokens, hidden, F32), like(tokens, hidden, BF))
    return run(
        shared_in_kernel, tokens // TILE, (), [two, sgate, sup],
        [tiled(two), whole(sgate), whole(sup)], outs, tuple(tiled(o) for o in outs), [],
        tokens * two.shape[1] * hidden * 4,
    )


def tokens_back(info, starts, slot_col, dots_row, grad_rows, cot, gate, up, sgate, sup, sdown, experts):
    tokens, width = cot.shape
    hidden = gate.shape[1]
    outs = (
        like(tokens, width, BF),
        like(tokens, hidden, BF),
        like(tokens, hidden, BF),
        like(tokens, experts, F32),
    )
    values = [slot_col, dots_row, grad_rows, cot, gate, up, sgate, sup, sdown]
    specs = [whole(v) for v in values]
    specs[0] = tiled(slot_col)
    specs[3:6] = [tiled(cot), tiled(gate), tiled(up)]
    return run(
        tokens_back_kernel, tokens // TILE, (info, starts), values, specs, outs,
        tuple(tiled(o) for o in outs), [pltpu.VMEM((TILE, width), F32)],
        tokens * width * hidden * 8,
    )


def columns_kernel(rest, query, expand, d_query, d_output, d_gate, d_up, d_down, d_expand):
    parts = rest.shape[0]
    fs = d_gate.shape[1] // parts
    for part in range(parts):
        for i, out in enumerate((d_gate, d_up, d_down)):
            block = rest[part, :, i * fs : (i + 1) * fs]
            out[:, part * fs : (part + 1) * fs] = block.astype(F32)
        width = NOPE + ROPE
        d_query[:, part * width : (part + 1) * width] = query[part, :, :width].astype(F32)
        block = query[part, :, width : width + VDIM]
        d_output[:, part * VDIM : (part + 1) * VDIM] = block.astype(F32)
        width = NOPE + VDIM
        d_expand[:, part * width : (part + 1) * width] = expand[part].astype(F32)


def columns_of(rest, query, expand, fs):
    count, shard = query.shape[:2]
    outs = (
        like(shard, count * (NOPE + ROPE), F32),
        like(shard, count * VDIM, F32),
        like(shard, count * fs, F32),
        like(shard, count * fs, F32),
        like(shard, count * fs, F32),
        like(expand.shape[1], count * (NOPE + VDIM), F32),
    )
    values = [rest, query, expand]
    specs = [whole(v) for v in values]
    return run(
        columns_kernel, 1, (), values, specs, outs, tuple(whole(o) for o in outs), [], 0
    )


def turned(value, cosine, sine):
    half = value.shape[1] // 2
    return value * cosine + jnp.concatenate([value[:, half:], value[:, :half]], 1) * sine


def before_kernel(
    token, gain, gain_latent, wq, wc, we, cosine, sine, normed, query, keys, values, latent, low
):
    hidden = token[...].astype(F32)
    normed[...] = (hidden * norm_scale(hidden) * gain[...]).astype(BF)
    raw = matmul(normed[...], wq[...])
    query[:, :NOPE] = raw[:, :NOPE].astype(BF)
    query[:, NOPE:] = turned(raw[:, NOPE:], cosine[...], sine[...]).astype(BF)
    compressed = matmul(normed[...], wc[...])
    low[...] = compressed[:, :LATENT]
    part = low[...]
    latent[...] = (part * norm_scale(part) * gain_latent[...]).astype(BF)
    expanded = matmul(latent[...], we[...])
    keys[:, :NOPE] = expanded[:, :NOPE].astype(BF)
    rope = compressed[:, LATENT : LATENT + ROPE]
    keys[:, NOPE:] = turned(rope, cosine[...], sine[...]).astype(BF)
    values[...] = expanded[:, NOPE:].astype(BF)


def before_attention(token, gain, gain_latent, wq, wc, we, cosine, sine):
    tokens, width = token.shape
    outs = (
        like(tokens, width, BF),
        like(tokens, NOPE + ROPE, BF),
        like(tokens, NOPE + ROPE, BF),
        like(tokens, VDIM, BF),
        like(tokens, LATENT, BF),
        like(tokens, LATENT, F32),
    )
    values = [token, gain, gain_latent, wq, wc, we, cosine, sine]
    specs = [whole(v) for v in values]
    specs[0], specs[6], specs[7] = tiled(token), tiled(cosine), tiled(sine)
    return run(
        before_kernel, tokens // TILE, (), values, specs, outs, tuple(tiled(o) for o in outs), [],
        tokens * width * 2000,
    )


def behind_kernel(
    gq, gk, gv, normed, latent, low, gain_latent, latent_col, gain_col, wq, wc, we, cosine, sine,
    extra, out, d_query, d_small, d_expand, d_latent, sum_q, sum_c, sum_e,
):
    step = pl.program_id(0)

    @pl.when(step == 0)
    def _():
        sum_q[...] = jnp.zeros_like(sum_q)
        sum_c[...] = jnp.zeros_like(sum_c)
        sum_e[...] = jnp.zeros_like(sum_e)

    scale = (NOPE + ROPE) ** (-0.5)
    query, keys = gq[...] * scale, gk[...] * scale
    back = -sine[...]
    grad_q = jnp.concatenate(
        [query[:, :NOPE], turned(query[:, NOPE:], cosine[...], back)], 1
    ).astype(BF)
    grad_e = jnp.concatenate([keys[:, :NOPE], gv[...]], 1).astype(BF)
    grad_latent = contract_last(grad_e, we[...])
    part = low[...]
    grad_low = norm_back(part, norm_scale(part), gain_latent[...], grad_latent)
    rope = turned(keys[:, NOPE:], cosine[...], back)
    fill = jnp.zeros((rope.shape[0], wc.shape[1] - LATENT - ROPE), F32)
    grad_c = jnp.concatenate([grad_low, rope, fill], 1).astype(BF)
    out[...] = (contract_last(grad_q, wq[...]) + contract_last(grad_c, wc[...])).astype(BF)
    sum_q[...] += leading_contraction(normed[...], grad_q)
    sum_c[...] += leading_contraction(normed[...], grad_c)
    sum_e[...] += leading_contraction(latent[...], grad_e)

    @pl.when(step == pl.num_programs(0) - 1)
    def _():
        first = jnp.sum(sum_q[...] * wq[...].astype(F32), 1, keepdims=True)
        first = first + jnp.sum(sum_c[...] * wc[...].astype(F32), 1, keepdims=True)
        d_query[...] = sum_q[...].astype(BF)
        edge = LATENT + ROPE
        lanes = lax.broadcasted_iota(jnp.int32, extra.shape, 1)
        more = extra[...] + jnp.where(lanes == 0, first / gain_col[...], 0.0)
        d_small[:, :edge] = sum_c[:, :edge].astype(BF)
        d_small[:, edge:] = more.astype(BF)
        d_expand[...] = sum_e[...].astype(BF)
        second = jnp.sum(sum_e[...] * we[...].astype(F32), 1, keepdims=True) / latent_col[...]
        d_latent[...] = second


def behind_attention(
    gq, gk, gv, normed, latent, low, gain_latent, gain_col, wq, wc, we, cosine, sine, extra, needs
):
    tokens, width = normed.shape
    outs = (
        like(tokens, width, BF),
        like(width, wq.shape[1], BF),
        like(width, wc.shape[1], BF),
        like(LATENT, we.shape[1], BF),
        like(LATENT, 1, F32),
    )
    values = [gq, gk, gv, normed, latent, low]
    values += [gain_latent, gain_latent.reshape(-1, 1), gain_col, wq, wc, we, cosine, sine, extra]
    specs = [tiled(v) for v in values[:6]] + [whole(v) for v in values[6:]]
    specs[12], specs[13] = tiled(cosine), tiled(sine)
    return run(
        behind_kernel, tokens // TILE, (), values, specs, outs,
        (tiled(outs[0]),) + tuple(whole(o) for o in outs[1:]),
        [
            pltpu.VMEM((width, wq.shape[1]), F32),
            pltpu.VMEM((width, wc.shape[1]), F32),
            pltpu.VMEM((LATENT, we.shape[1]), F32),
        ],
        tokens * width * 4000,
        needs,
    )


def placement(lengths_row, order_row):
    ends = jnp.cumsum(lengths_row)
    starts = ends - lengths_row
    sequence = jnp.sum((order_row[:, None] >= ends[None, :]).astype(jnp.int32), 1)
    chosen = sequence[:, None] == jnp.arange(lengths_row.shape[0], dtype=jnp.int32)[None, :]
    offset = jnp.sum(jnp.where(chosen, starts[None, :], 0), 1)
    return (sequence, order_row - offset)


def spread(weight, count, repeat):
    rows = weight.shape[0]
    parts = jnp.transpose(weight.astype(BF).reshape(rows, count // repeat, -1), (1, 0, 2))
    return jnp.repeat(parts, repeat, 0) if repeat > 1 else parts


def pad_last(value, width):
    return jnp.pad(value, [(0, 0)] * (value.ndim - 1) + [(0, width - value.shape[-1])])


def up_to(width, unit=128):
    return -(-width // unit) * unit


def local(
    tokens,
    cotangent,
    lengths,
    token_order,
    routes,
    first_gain,
    latent_gain,
    query_weight,
    compress_weight,
    expand_weight,
    output_weight,
    second_gain,
    router_weight,
    shared_gate,
    shared_up,
    shared_down,
    expert_gate,
    expert_up,
    expert_down,
):
    box = Box()
    count = box.count
    repeat = max(1, count // HEADS)
    rows = tokens.shape[1]
    group = rows * count
    asked = group // repeat
    experts = router_weight.shape[1]
    shard = query_weight.shape[0]
    width = NOPE + ROPE
    me = lax.axis_index("ctx")
    both = ("ctx", "fsdp")
    all_devices = count * lax.axis_size("fsdp")

    half = lax.axis_index("fsdp")

    def reduce_blocks(collective, value, more, needs=(), carry=()):
        plans = [Scatter(count, value, 4)] + [plan for _, plan, _ in more]
        spans = [(0.0, 1.0)] + [span for _, _, span in more]
        values = [value] + [v for v, _, _ in more]
        return exchange(count, collective, values, plans, spans, needs, carry)

    def across(value):
        return lax.ppermute(value, "fsdp", [(0, 1), (1, 0)])

    def halves_sent(parts):
        own = lax.dynamic_index_in_dim(parts, half, 1, keepdims=False)
        other = lax.dynamic_index_in_dim(parts, 1 - half, 1, keepdims=False)
        return own, across(other.astype(BF))

    owners = box.owners()

    small_cols = compress_weight.shape[1] + experts + 3
    lat_rows = latent_gain.shape[0]
    small = jnp.concatenate(
        [
            compress_weight,
            first_gain[:, None],
            second_gain[:, None],
            router_weight,
            jnp.pad(latent_gain, (0, shard - lat_rows))[:, None],
        ],
        1,
    ).astype(BF)
    small = pad_last(small, up_to(small_cols))
    query_parts = spread(query_weight, count, repeat)
    expand_parts = spread(expand_weight, count, repeat)
    small_all = lax.all_gather(small, both, axis=0, tiled=True)
    gates = lax.all_gather(expert_gate[0].astype(BF), "fsdp", axis=0, tiled=True)
    fs = shared_gate.shape[1] // count
    fp = up_to(fs)
    rest = jnp.concatenate(
        [spread(shared_gate, count, 1), spread(shared_up, count, 1), spread(shared_down, count, 1)], -1
    )
    rest = pad_last(rest, up_to(3 * fs))
    query_own, expand_own, token_all, rest_own, cot_low, down_own = exchange(
        count,
        0,
        [query_parts, expand_parts, tokens[0], rest],
        [
            Deal(count, query_parts, both=True),
            Deal(count, expand_parts, both=True),
            Gather(count, tokens[0], 4),
            Deal(count, rest, both=True),
        ],
        spans=[(-2, -1), (-1, 0), (0, 1), (1, 2)],
        carry=[cotangent[0].astype(BF), expert_down[0].astype(BF)],
    )
    token_all = token_all.reshape(group, D)
    query_own = query_own.reshape(D, -1)
    expand_own = expand_own.reshape(LATENT, -1)
    edge = compress_weight.shape[1]
    compress_full = small_all[:, :edge]
    router_full = small_all[:, edge + 2 : edge + 2 + experts]
    gain_first = small_all[:, edge].astype(F32)
    gain_second = small_all[:, edge + 1].astype(F32)
    gain_latent = small_all[:, edge + experts + 2].reshape(all_devices, shard)[:, :lat_rows]
    gain_latent = gain_latent.reshape(-1).astype(F32)

    output_cast = output_weight
    output_full = lax.all_gather(output_cast.astype(BF), both, axis=0, tiled=True)
    route_own = routes[0]
    cot_parts = box.spread(cot_low, 0)

    order_all = jnp.take(token_order[0].reshape(count, rows), owners, axis=0).reshape(-1)
    sequence, position = placement(lengths[0], order_all)
    turns = ROPE // 2
    freq = 10000.0 ** (-jnp.arange(turns, dtype=F32) / turns)
    angle = position.astype(F32)[:, None] * freq[None, :]
    cosine = jnp.tile(jnp.cos(angle), (1, 2))
    sine = jnp.sin(angle)
    sine = jnp.concatenate([-sine, sine], 1)

    normed_all, query, keys, values, latent, low_part = before_attention(
        token_all, gain_first[None, :], gain_latent[None, :], query_own, small_all, expand_own,
        cosine, sine,
    )
    up_cast = expert_up[0]
    up_own = up_cast.astype(BF)
    ups = (up_own, across(up_own))
    downs = (down_own, across(down_own))
    scale = width ** (-0.5)
    visible = (sequence[:asked, None] == sequence[None, :]) & (
        position[None, :] <= position[:asked, None]
    )
    scores = jnp.where(visible, contract_last(query, keys) * scale, NEGATIVE)
    peak = jnp.max(scores, -1, keepdims=True)
    weights = jnp.where(visible, jnp.exp(scores - peak), 0.0)
    total = jnp.sum(weights, -1, keepdims=True)
    mixed_f = matmul(weights.astype(BF), values) / total
    logsum = peak + jnp.log(total)

    def to_owner(value, needs, carried):
        if repeat > 1:
            value = jnp.pad(value, ((0, group - asked), (0, 0)))
        value = value.reshape(count, rows, -1)
        plan = Deal(count, value, pick=lambda me, to: offset_of(count, me, to))
        got, carried = exchange(count, 1, [value], [plan], needs=needs, carry=[carried])
        if repeat > 1:
            got = jnp.sum(got.reshape(HEADS, repeat, rows, -1).astype(F32), 1).astype(BF)
        return jnp.transpose(got, (1, 0, 2)).reshape(rows, -1), carried

    route_all = box.gather(route_own)
    mine = jnp.any(route_all == me, -1)
    capacity = rows * TOP * 4 // (3 * experts) * count
    counted = jnp.cumsum(mine.astype(jnp.int32))
    slot = jnp.where(mine, counted - 1, -1)
    starts = jnp.concatenate([jnp.zeros((1,), jnp.int32), counted[TILE - 1 :: TILE]])
    column = jnp.arange(experts, dtype=jnp.int32)[None, :] == me
    info = jnp.stack([half, me]).astype(jnp.int32)
    mixed, cot_parts[0] = to_owner(mixed_f.astype(BF), [slot], cot_parts[0])
    cot_held = joined(cot_parts)
    hidden = tokens[0].astype(F32)
    residual = hidden + contract_last(mixed, output_full)

    residual_scale = norm_scale(residual)
    normed_two = (residual * residual_scale * gain_second).astype(BF)
    two_all, cot_held = exchange(
        count, 2, [normed_two], [Gather(count, normed_two, 4)], carry=[cot_held]
    )
    two_all = two_all.reshape(group, D)
    cot_parts = box.spread(cot_held, 1)
    probs_all = jax.nn.softmax(matmul(two_all, router_full), -1)
    gate_col = jnp.sum(jnp.where(column & mine[:, None], probs_all, 0.0), -1, keepdims=True)
    rows_in, gate_val, up_val, expert_hidden = expert_in(
        info, starts, (slot[None, :], capacity), two_all, gates, ups, []
    )
    cot_held = joined(cot_parts)
    cot_all = joined(box.spread(cot_held, 2))
    rest_own = rest_own.reshape(D, -1)
    sgate_own = pad_last(rest_own[:, :fs], fp)
    sup_own = pad_last(rest_own[:, fs : 2 * fs], fp)
    sdown_own = pad_last(rest_own[:, 2 * fs : 3 * fs], fp)
    sg, su, shared_hidden = shared_in(two_all, sgate_own, sup_own)
    produced, out_two = expert_out(
        info, starts, expert_hidden, downs, slot[:, None], gate_col, shared_hidden, sdown_own,
        [cot_held],
    )

    out_held = summed(box.share(out_two, 2), BF)
    grad_in, grad_eg, grad_eu, grad_rows, dots = expert_back(
        info, starts, slot[None, :], gate_col.reshape(1, group), cot_all, produced, gate_val, up_val,
        gates, ups, downs, [out_held],
    )
    out_held = summed(box.share(out_held, 1), BF)
    grad_two_part, grad_sg, grad_su, gg_part = tokens_back(
        info, starts, slot[:, None], dots.reshape(1, capacity), grad_rows, cot_all, sg, su,
        sgate_own, sup_own, sdown_own, experts,
    )
    d_rest = [
        leading_contraction(two_all, grad_sg)[:, :fs],
        leading_contraction(two_all, grad_su)[:, :fs],
        leading_contraction(cot_all, shared_hidden)[:, :fs],
    ]
    d_rest = pad_last(jnp.concatenate(d_rest, 1).astype(BF), up_to(3 * fs))
    d_rest = d_rest.reshape(count, 2, shard, -1)
    rest_mine, rest_got = halves_sent(d_rest)
    d_down = leading_contraction(grad_in, expert_hidden).astype(BF)
    products = Products(
        [rows_in, grad_eg, grad_eu], [(0, 1), (0, 2)]
    )
    gg_part = gg_part.reshape(count, rows, -1)
    grad_two, d_gate, d_up, grad_gates = reduce_blocks(
        3,
        grad_two_part.reshape(count, rows, D),
        [
            (products.values, products, (0.0, 1.0)),
            (gg_part, Scatter(count, gg_part, 1), (0.3, 0.9)),
        ],
        [out_held, d_down],
    )

    d_experts = [
        lax.psum_scatter(v, "fsdp", scatter_dimension=0, tiled=True).astype(F32)[None]
        for v in (d_gate, d_up, d_down)
    ]

    probs = probs_all[:rows]
    grad_logits = probs * (grad_gates - jnp.sum(probs * grad_gates, -1, keepdims=True))
    grad_logits = grad_logits.astype(BF)
    grad_two = grad_two + contract_last(grad_logits, router_full)
    d_router = leading_contraction(normed_two, grad_logits)
    d_second = jnp.sum(grad_two * residual * residual_scale, 0)
    grad_residual = cotangent[0] + norm_back(residual, residual_scale, gain_second, grad_two)

    attended = grad_residual.astype(BF)
    output_own = lax.dynamic_slice_in_dim(output_full, me * VDIM, VDIM, 1)
    attended_all, out_held, rest_mine = exchange(
        count, 4, [attended], [Gather(count, attended, 4)], carry=[out_held, rest_mine]
    )
    d_rest = (rest_mine.astype(F32) + rest_got.astype(F32)).astype(BF)
    out_parts = box.share(out_held, 0)
    d_rest = lax.all_to_all(d_rest, "ctx", split_axis=0, concat_axis=0, tiled=True)
    attended_all = attended_all.reshape(group, D)
    mixed_own = mixed_f.astype(BF)
    d_output = leading_contraction(attended_all, mixed_own)
    grad_mixed = matmul(attended_all, output_own).astype(BF)
    delta = jnp.sum(grad_mixed.astype(F32) * mixed_f, -1, keepdims=True)
    probs_a = jnp.where(visible, jnp.exp(contract_last(query, keys) * scale - logsum), 0.0)
    grad_probs = contract_last(grad_mixed, values)
    grad_scores = (probs_a * (grad_probs - delta)).astype(BF)
    output = residual + summed(out_parts, F32)
    grad_query = matmul(grad_scores, keys)
    grad_keys = leading_contraction(grad_scores, query)
    grad_values = leading_contraction(probs_a.astype(BF), grad_mixed)
    extra = jnp.concatenate([jnp.zeros_like(d_second)[:, None], d_second[:, None], d_router], 1)
    extra = pad_last(extra, up_to(small_cols) - edge)
    grad_norm_part, d_query, d_small, d_expand, d_latent = behind_attention(
        grad_query, grad_keys, grad_values, normed_all, latent, low_part, gain_latent[None, :],
        gain_first[:, None], query_own, small_all, expand_own, cosine, sine, extra,
        [output],
    )

    d_latent = jnp.pad(d_latent.reshape(all_devices, lat_rows), ((0, 0), (0, shard - lat_rows)))
    d_query = jnp.concatenate([d_query, d_output.astype(BF), d_latent.reshape(-1, 1).astype(BF)], 1)
    d_q = d_query.reshape(count, 2, shard, -1)
    d_e = d_expand.reshape(count, 2, -1, d_expand.shape[-1])
    d_small = d_small.reshape(count, 2, shard, -1)
    grad_norm, d_q, d_e, d_small = reduce_blocks(
        5,
        grad_norm_part.reshape(count, rows, D),
        [
            (d_q, DealSum(count, d_q), (0.5, 0.55)),
            (d_e, DealSum(count, d_e), (0.5, 0.56)),
            (d_small, Scatter(count, d_small, 1, both=True), (0.25, 1.1)),
        ],
        [d_rest],
    )
    grad_tokens = grad_residual + norm_back(hidden, norm_scale(hidden), gain_first, grad_norm)

    d_query, d_output, d_sgate, d_sup, d_sdown, d_expand = columns_of(d_rest, d_q, d_e, fs)
    return (
        output[None],
        grad_tokens[None],
        d_small[:, edge],
        jnp.sum(d_q[:, :lat_rows, width + VDIM].astype(F32), 0),
        d_query,
        d_small[:, :edge],
        d_expand,
        d_output,
        d_small[:, edge + 1],
        d_small[:, edge + 2 : edge + 2 + experts],
        d_sgate,
        d_sup,
        d_sdown,
        *d_experts,
    )


def shifted(shard, axis, by):
    devices = lax.axis_size(axis)
    return lax.ppermute(shard, axis, [(i, (i + by) % devices) for i in range(devices)])


def rms_norm(value, gain):
    return value * lax.rsqrt(jnp.mean(value * value, -1, keepdims=True) + EPS) * gain


def rotate(value, position):
    half = value.shape[-1] // 2
    freq = 10000.0 ** (-jnp.arange(half, dtype=jnp.float32) / half)
    angle = position.astype(jnp.float32)[:, None] * freq[None, :]
    cosine = jnp.cos(angle)[:, None, :]
    sine = jnp.sin(angle)[:, None, :]
    first = value[..., :half]
    second = value[..., half:]
    return jnp.concatenate([first * cosine - second * sine, first * sine + second * cosine], -1)


def expert_slots(route_rows, experts):
    flat = route_rows.reshape(-1)
    onehot = (flat[:, None] == jnp.arange(experts, dtype=jnp.int32)[None, :]).astype(jnp.int32)
    before = jnp.cumsum(onehot, 0) - onehot
    return (flat, jnp.sum(before * onehot, 1))


def swiglu(gate_value, up_value):
    return jax.nn.silu(gate_value) * up_value


def softmax_last(value):
    return jax.nn.softmax(value, -1)


def local_gathered(
    tokens,
    cotangent,
    lengths,
    token_order,
    routes,
    first_gain,
    latent_gain,
    query_weight,
    compress_weight,
    expand_weight,
    output_weight,
    second_gain,
    router_weight,
    shared_gate,
    shared_up,
    shared_down,
    expert_gate,
    expert_up,
    expert_down,
):
    (
        gain_first,
        gain_latent,
        query_full,
        compress_full,
        expand_full,
        output_full,
        gain_second,
        router_full,
        shared_gate_full,
        shared_up_full,
        shared_down_full,
    ) = (
        lax.all_gather(first_gain.astype(jnp.bfloat16), ("ctx", "fsdp"), axis=0, tiled=True),
        lax.all_gather(latent_gain.astype(jnp.bfloat16), ("ctx", "fsdp"), axis=0, tiled=True),
        lax.all_gather(query_weight.astype(jnp.bfloat16), ("ctx", "fsdp"), axis=0, tiled=True),
        lax.all_gather(compress_weight.astype(jnp.bfloat16), ("ctx", "fsdp"), axis=0, tiled=True),
        lax.all_gather(expand_weight.astype(jnp.bfloat16), ("ctx", "fsdp"), axis=0, tiled=True),
        lax.all_gather(output_weight.astype(jnp.bfloat16), ("ctx", "fsdp"), axis=0, tiled=True),
        lax.all_gather(second_gain.astype(jnp.bfloat16), ("ctx", "fsdp"), axis=0, tiled=True),
        lax.all_gather(router_weight.astype(jnp.bfloat16), ("ctx", "fsdp"), axis=0, tiled=True),
        lax.all_gather(shared_gate.astype(jnp.bfloat16), ("ctx", "fsdp"), axis=0, tiled=True),
        lax.all_gather(shared_up.astype(jnp.bfloat16), ("ctx", "fsdp"), axis=0, tiled=True),
        lax.all_gather(shared_down.astype(jnp.bfloat16), ("ctx", "fsdp"), axis=0, tiled=True),
    )
    gate_expert, up_expert, down_expert = (
        lax.all_gather(expert_gate.astype(jnp.bfloat16), "fsdp", axis=1, tiled=True),
        lax.all_gather(expert_up.astype(jnp.bfloat16), "fsdp", axis=1, tiled=True),
        lax.all_gather(expert_down.astype(jnp.bfloat16), "fsdp", axis=1, tiled=True),
    )
    gate_expert = gate_expert[0]
    up_expert = up_expert[0]
    down_expert = down_expert[0]
    rows = tokens.shape[1]
    place = lax.axis_index("ctx")
    devices = lax.axis_size("ctx")
    query_width = NOPE + ROPE
    sequence, position = placement(lengths[0], token_order[0])
    own_seq = lax.dynamic_slice_in_dim(sequence, place * rows, rows)
    own_pos = lax.dynamic_slice_in_dim(position, place * rows, rows)

    def visible_mask(start, count):
        key_seq = lax.dynamic_slice_in_dim(sequence, start, count)
        key_pos = lax.dynamic_slice_in_dim(position, start, count)
        return (own_seq[:, None] == key_seq[None, :]) & (key_pos[None, :] <= own_pos[:, None])

    def turn_query(part):
        return rotate(part, own_pos)

    def turn_key(part):
        return rotate(part[:, None, :], own_pos)[:, 0, :]

    hidden = tokens[0].astype(jnp.float32)
    normed_f, norm_pull = jax.vjp(rms_norm, hidden, gain_first.astype(jnp.float32))
    normed = normed_f.astype(jnp.bfloat16)
    query_raw = matmul(normed, query_full).reshape(rows, HEADS, query_width)
    query_rotated, query_pull = jax.vjp(turn_query, query_raw[..., NOPE:])
    query = jnp.concatenate([query_raw[..., :NOPE], query_rotated], -1).astype(jnp.bfloat16)
    compressed = matmul(normed, compress_full)
    latent_f, latent_pull = jax.vjp(
        rms_norm, compressed[:, :LATENT], gain_latent.astype(jnp.float32)
    )
    latent = latent_f.astype(jnp.bfloat16)
    expanded = matmul(latent, expand_full).reshape(rows, HEADS, NOPE + VDIM)
    key_rot, key_pull = jax.vjp(turn_key, compressed[:, LATENT:])
    keys = jnp.concatenate(
        [expanded[..., :NOPE], jnp.broadcast_to(key_rot[:, None, :], (rows, HEADS, ROPE))], -1
    )
    keys = keys.astype(jnp.bfloat16).reshape(rows, HEADS * query_width)
    values = expanded[..., NOPE:].astype(jnp.bfloat16).reshape(rows, HEADS * VDIM)
    scale = query_width ** (-0.5)
    running = jnp.full((HEADS, rows), NEGATIVE, jnp.float32)
    key_piece = lax.all_gather(keys, "ctx", axis=0, tiled=True)
    value_piece = lax.all_gather(values, "ctx", axis=0, tiled=True)
    count = key_piece.shape[0]
    scores = (
        jnp.einsum(
            "qhd,khd->hqk",
            query,
            key_piece.reshape(count, HEADS, query_width),
            preferred_element_type=jnp.float32,
        )
        * scale
    )
    visible = visible_mask(jnp.int32(0), count)[None]
    masked = jnp.where(visible, scores, NEGATIVE)
    newest = jnp.maximum(running, jnp.max(masked, -1))
    weights = jnp.where(visible, jnp.exp(masked - newest[..., None]), 0.0)
    total = jnp.sum(weights, -1)
    summed = jnp.einsum(
        "hqk,khd->qhd",
        weights.astype(jnp.bfloat16),
        value_piece.reshape(count, HEADS, VDIM),
        preferred_element_type=jnp.float32,
    )
    running, total, summed = (newest, total, summed)
    mixed_f = summed / jnp.transpose(total)[:, :, None]
    logsum = running + jnp.log(total)
    mixed = mixed_f.astype(jnp.bfloat16).reshape(rows, HEADS * VDIM)
    residual = hidden + contract_last(mixed, output_full)
    normed_two_f, norm_two_pull = jax.vjp(rms_norm, residual, gain_second.astype(jnp.float32))
    normed_two = normed_two_f.astype(jnp.bfloat16)
    logits = matmul(normed_two, router_full)
    experts = router_full.shape[1]
    route_rows = routes[0]
    pick = (route_rows[:, :, None] == jnp.arange(experts, dtype=jnp.int32)[None, None, :]).astype(
        jnp.float32
    )
    router_probs, gate_pull = jax.vjp(softmax_last, logits)
    gates = jnp.sum(pick * router_probs[:, None, :], -1)
    shared_gate_val = matmul(normed_two, shared_gate_full)
    shared_up_val = matmul(normed_two, shared_up_full)
    shared_hidden = swiglu(shared_gate_val, shared_up_val).astype(jnp.bfloat16)
    shared_out = contract_last(shared_hidden, shared_down_full)
    capacity = rows * TOP * 4 // (3 * experts)
    flat, slot = expert_slots(route_rows, experts)
    anchor = jnp.arange(rows * TOP, dtype=jnp.int32) // TOP
    outgoing = (
        jnp.zeros((experts, capacity, D), jnp.bfloat16).at[flat, slot].set(normed_two[anchor])
    )
    arrived = lax.all_to_all(outgoing, "ctx", split_axis=0, concat_axis=0, tiled=True)
    received_rows = arrived.reshape(-1, D)
    gate_val = matmul(received_rows, gate_expert)
    up_val = matmul(received_rows, up_expert)
    expert_hidden = swiglu(gate_val, up_val).astype(jnp.bfloat16)
    produced = contract_last(expert_hidden, down_expert).astype(jnp.bfloat16).reshape(arrived.shape)
    returned = lax.all_to_all(produced, "ctx", split_axis=0, concat_axis=0, tiled=True)
    route_out = returned[flat, slot].astype(jnp.float32).reshape(rows, TOP, D)
    routed = jnp.sum(gates[:, :, None] * route_out, 1)
    output = residual + routed + shared_out
    grad_out = cotangent[0]
    grad_low = grad_out.astype(jnp.bfloat16)
    grad_shared_hidden = matmul(grad_low, shared_down_full)
    grad_sdown = leading_contraction(grad_low, shared_hidden)
    grad_sg, grad_su = jax.vjp(swiglu, shared_gate_val, shared_up_val)[1](grad_shared_hidden)
    grad_sg = grad_sg.astype(jnp.bfloat16)
    grad_su = grad_su.astype(jnp.bfloat16)
    grad_sgate = leading_contraction(normed_two, grad_sg)
    grad_sup = leading_contraction(normed_two, grad_su)
    grad_normed_two = contract_last(grad_sg, shared_gate_full) + contract_last(
        grad_su, shared_up_full
    )
    grad_gates = jnp.sum(grad_out[:, None, :] * route_out, -1)
    grad_route = (
        (gates[:, :, None] * grad_out[:, None, :]).astype(jnp.bfloat16).reshape(rows * TOP, D)
    )
    grad_outgoing = jnp.zeros((experts, capacity, D), jnp.bfloat16).at[flat, slot].set(grad_route)
    grad_arrived = lax.all_to_all(
        grad_outgoing, "ctx", split_axis=0, concat_axis=0, tiled=True
    ).reshape(-1, D)
    grad_expert_hidden = matmul(grad_arrived, down_expert)
    grad_edown = leading_contraction(grad_arrived, expert_hidden)
    grad_eg, grad_expert_up_value = jax.vjp(swiglu, gate_val, up_val)[1](grad_expert_hidden)
    grad_eg = grad_eg.astype(jnp.bfloat16)
    grad_expert_up_value = grad_expert_up_value.astype(jnp.bfloat16)
    grad_egate = leading_contraction(received_rows, grad_eg)
    grad_expert_up_partial = leading_contraction(received_rows, grad_expert_up_value)
    grad_rows = (
        contract_last(grad_eg, gate_expert) + contract_last(grad_expert_up_value, up_expert)
    ).astype(jnp.bfloat16)
    grad_back = lax.all_to_all(
        grad_rows.reshape(arrived.shape), "ctx", split_axis=0, concat_axis=0, tiled=True
    )
    grad_normed_two = grad_normed_two + jnp.sum(
        grad_back[flat, slot].astype(jnp.float32).reshape(rows, TOP, D), 1
    )
    expert_parts = (
        lax.psum_scatter(
            grad_egate[None].astype(jnp.bfloat16), "fsdp", scatter_dimension=1, tiled=True
        ).astype(jnp.float32),
        lax.psum_scatter(
            grad_expert_up_partial[None].astype(jnp.bfloat16),
            "fsdp",
            scatter_dimension=1,
            tiled=True,
        ).astype(jnp.float32),
        lax.psum_scatter(
            grad_edown[None].astype(jnp.bfloat16), "fsdp", scatter_dimension=1, tiled=True
        ).astype(jnp.float32),
    )
    grad_router_probs = jnp.sum(pick * grad_gates[:, :, None], 1)
    grad_logits = gate_pull(grad_router_probs)[0].astype(jnp.bfloat16)
    grad_normed_two = grad_normed_two + contract_last(grad_logits, router_full)
    grad_router = leading_contraction(normed_two, grad_logits)
    grad_residual_norm, grad_gain_second = norm_two_pull(grad_normed_two)
    grad_residual = grad_out + grad_residual_norm
    grad_attended = grad_residual.astype(jnp.bfloat16)
    grad_mixed = matmul(grad_attended, output_full).astype(jnp.bfloat16).reshape(rows, HEADS, VDIM)
    grad_output_w = leading_contraction(grad_attended, mixed)
    delta = jnp.transpose(jnp.sum(grad_mixed.astype(jnp.float32) * mixed_f, -1))

    def rotation_loop_step(step, carry):
        key_block, value_block, grad_key, grad_value, grad_query = carry
        start = (place - step) % devices * rows
        keyed = key_block.reshape(rows, HEADS, query_width)
        valued = value_block.reshape(rows, HEADS, VDIM)
        scores = (
            jnp.einsum("qhd,khd->hqk", query, keyed, preferred_element_type=jnp.float32) * scale
        )
        visible = visible_mask(start, rows)[None]
        weights = jnp.where(visible, jnp.exp(scores - logsum[:, :, None]), 0.0)
        weights_low = weights.astype(jnp.bfloat16)
        grad_weights = jnp.einsum(
            "qhd,khd->hqk", grad_mixed, valued, preferred_element_type=jnp.float32
        )
        grad_scores = (weights * (grad_weights - delta[:, :, None])).astype(jnp.bfloat16)
        grad_query = grad_query + scale * jnp.einsum(
            "hqk,khd->qhd", grad_scores, keyed, preferred_element_type=jnp.float32
        )
        grad_key = grad_key + scale * jnp.einsum(
            "hqk,qhd->khd", grad_scores, query, preferred_element_type=jnp.float32
        )
        grad_value = grad_value + jnp.einsum(
            "hqk,qhd->khd", weights_low, grad_mixed, preferred_element_type=jnp.float32
        )
        grad_key, grad_value = (
            shifted(grad_key.astype(jnp.bfloat16), "ctx", 1).astype(grad_key.dtype),
            shifted(grad_value.astype(jnp.bfloat16), "ctx", 1).astype(grad_value.dtype),
        )
        key_block, value_block = shifted((key_block, value_block), "ctx", 1)
        return (key_block, value_block, grad_key, grad_value, grad_query)

    cycle_start = (
        keys,
        values,
        jnp.zeros((rows, HEADS, query_width), jnp.float32),
        jnp.zeros((rows, HEADS, VDIM), jnp.float32),
        jnp.zeros((rows, HEADS, query_width), jnp.float32),
    )
    cycle_end = lax.fori_loop(0, devices, rotation_loop_step, cycle_start)
    grad_key = cycle_end[2]
    grad_value = cycle_end[3]
    grad_query = cycle_end[4]
    grad_key_rotary = jnp.sum(grad_key[..., NOPE:], 1)
    grad_expanded_latent = jnp.concatenate([grad_key[..., :NOPE], grad_value], -1)
    grad_expanded_latent = grad_expanded_latent.reshape(rows, HEADS * (NOPE + VDIM)).astype(
        jnp.bfloat16
    )
    grad_latent = contract_last(grad_expanded_latent, expand_full)
    grad_expand_w = leading_contraction(latent, grad_expanded_latent)
    grad_comp_latent, grad_gain_latent = latent_pull(grad_latent)
    grad_comp_rope = key_pull(grad_key_rotary)[0]
    grad_compressed = jnp.concatenate([grad_comp_latent, grad_comp_rope], -1).astype(jnp.bfloat16)
    grad_query_rope = query_pull(grad_query[..., NOPE:])[0]
    grad_query_raw = jnp.concatenate([grad_query[..., :NOPE], grad_query_rope], -1)
    grad_query_raw = grad_query_raw.reshape(rows, HEADS * query_width).astype(jnp.bfloat16)
    grad_normed = contract_last(grad_query_raw, query_full) + contract_last(
        grad_compressed, compress_full
    )
    grad_query_w = leading_contraction(normed, grad_query_raw)
    grad_compress_w = leading_contraction(normed, grad_compressed)
    grad_hidden_norm, grad_gain_first = norm_pull(grad_normed)
    grad_input = grad_residual + grad_hidden_norm
    dense_parts = (
        lax.psum_scatter(grad_gain_first, ("ctx", "fsdp"), scatter_dimension=0, tiled=True),
        lax.psum_scatter(grad_gain_latent, ("ctx", "fsdp"), scatter_dimension=0, tiled=True),
        lax.psum_scatter(grad_query_w, ("ctx", "fsdp"), scatter_dimension=0, tiled=True),
        lax.psum_scatter(grad_compress_w, ("ctx", "fsdp"), scatter_dimension=0, tiled=True),
        lax.psum_scatter(grad_expand_w, ("ctx", "fsdp"), scatter_dimension=0, tiled=True),
        lax.psum_scatter(grad_output_w, ("ctx", "fsdp"), scatter_dimension=0, tiled=True),
        lax.psum_scatter(grad_gain_second, ("ctx", "fsdp"), scatter_dimension=0, tiled=True),
        lax.psum_scatter(grad_router, ("ctx", "fsdp"), scatter_dimension=0, tiled=True),
        lax.psum_scatter(grad_sgate, ("ctx", "fsdp"), scatter_dimension=0, tiled=True),
        lax.psum_scatter(grad_sup, ("ctx", "fsdp"), scatter_dimension=0, tiled=True),
        lax.psum_scatter(grad_sdown, ("ctx", "fsdp"), scatter_dimension=0, tiled=True),
    )
    return (
        output[None],
        grad_input[None],
        dense_parts[0],
        dense_parts[1],
        dense_parts[2],
        dense_parts[3],
        dense_parts[4],
        dense_parts[5],
        dense_parts[6],
        dense_parts[7],
        dense_parts[8],
        dense_parts[9],
        dense_parts[10],
        expert_parts[0],
        expert_parts[1],
        expert_parts[2],
    )


def solution(mesh):
    token_spec = P("fsdp", "ctx", None)
    vector = P(("ctx", "fsdp"))
    matrix = P(("ctx", "fsdp"), None)
    expert = P("ctx", "fsdp", None)
    weights = (vector, vector, matrix, matrix, matrix, matrix, vector, matrix, matrix, matrix, matrix)
    weights = weights + (expert,) * 3
    return jax.shard_map(
        local if mesh.shape["ctx"] == HEADS else local_gathered,
        mesh=mesh,
        in_specs=(token_spec, token_spec, P("fsdp", None), P("fsdp", None), token_spec) + weights,
        out_specs=(token_spec, token_spec) + weights,
        check_vma=False,
    )
```
